128 devices in a mesh: dp: 32 (over y, x, core), mp: 4 (over z).
Axes of the slice: x: 4, y: 4, z: 4, core: 2. Of those that a mesh axis runs over, the one named last changes fastest.
Arguments:
- sparse_ids: int32 [65536, 26], P(('dp', 'mp')), may hold values from 0 to 524287, as said below
- dense_feats: float32 [65536, 13], P(('dp', 'mp')), may hold values from -6 to 6
- labels: int32 [65536, 2], P(('dp', 'mp')), may hold values 0 or 1
- tables: float32 [26, 524288, 16], P(None, ('dp', 'mp')), may hold values from -6 to 6
- dense_w: float32 [13, 96], replicated, may hold values from -1.75 to 1.75
- dense_b: float32 [96], replicated, may hold values from -3 to 3
- w_in: bfloat16 [8, 512, 256], P(None, None, 'mp'), may hold values from -0.25 to 0.25
- b_in: bfloat16 [8, 256], P(None, 'mp'), may hold values from -3 to 3
- w_out: bfloat16 [8, 256, 128], P(None, 'mp'), may hold values from -0.375 to 0.375
- b_out: float32 [8, 128], replicated, may hold values from -3 to 3
- gate_w: float32 [2, 512, 8], replicated, may hold values from -0.125 to 0.125
- gate_b: float32 [2, 8], replicated, may hold values from -0.6 to 0.6
- tower_w1: float32 [2, 128, 64], replicated, may hold values from -0.5 to 0.5
- tower_b1: float32 [2, 64], replicated, may hold values from -3 to 3
- tower_w2: float32 [2, 64], replicated, may hold values from -0.75 to 0.75
- tower_b2: float32 [2], replicated, may hold values from -3 to 3
Outputs:
- grad_tables: float32 [26, 524288, 16], P(None, ('dp', 'mp'))
- grad_dense_w: float32 [13, 96], replicated
- grad_dense_b: float32 [96], replicated
- grad_w_in: float32 [8, 512, 256], P(None, None, 'mp')
- grad_b_in: float32 [8, 256], P(None, 'mp')
- grad_w_out: float32 [8, 256, 128], P(None, 'mp')
- grad_b_out: float32 [8, 128], replicated
- grad_gate_w: float32 [2, 512, 8], replicated
- grad_gate_b: float32 [2, 8], replicated
- grad_tower_w1: float32 [2, 128, 64], replicated
- grad_tower_b1: float32 [2, 64], replicated
- grad_tower_w2: float32 [2, 64], replicated
- grad_tower_b2: float32 [2], replicated
- grad_dense: float32 [65536, 13], P(('dp', 'mp'))
The draws below stay inside these ranges and needn't reach their ends.
Inputs may be any that keep to these rules, and one draw needn't show every extreme that they name: `sparse_ids`: consider the 512 examples of one device (blocks of rows in the order of dp, then mp) and the table rows of one device (ids in [j * 4096, (j + 1) * 4096)). At most 208 of a device's 13312 ids, over all features, fall in one device's rows; each device sends exactly 208 ids to each of 16 devices and splits the rest as evenly as possible over the others.
All inputs are finite; a program needn't handle non-finite values. No bound on the sum of `labels` on one device may be relied on, other than what follows from the above.
Results may differ from the reference program's by a relative error of at most 0.02.
Values may be sent and summed in bfloat16 or wider, within the bound.
A program may use at most 192 MiB of HBM per device.

```python
import jax
import jax.numpy as jnp
from jax import lax

FIELDS = 26
EMB = 16
VOCAB = 524288
DENSE = 13
DPROJ = 96
EXPERTS = 8
HID = 256
EOUT = 128
TASKS = 2
THID = 64
OWNERS = 128
BATCH = 65536
ROWS_DEV = 4096
LOOKUPS = 13312
CAP = 208
HOT = 16
DIN = 512


def draw_sparse_ids(key, part):
    key = jax.random.fold_in(key, 7)
    base_key, source_key = jax.random.split(key)
    listing = jax.random.permutation(base_key, OWNERS).astype(jnp.int32)
    slot_ids = jnp.arange(LOOKUPS, dtype=jnp.int32)

    def per_source(source):
        source_rng = jax.random.fold_in(source_key, source)
        offset_key, order_key, bound_key, row_key = jax.random.split(source_rng, 4)
        offset = jax.random.randint(offset_key, (), OWNERS - HOT + 1, OWNERS + 1)
        ranked = listing[(jnp.arange(OWNERS, dtype=jnp.int32) + offset) % OWNERS]
        hot_owner = ranked[jnp.minimum(slot_ids // CAP, HOT - 1)]
        cold_owner = ranked[HOT + (slot_ids - HOT * CAP) % (OWNERS - HOT)]
        owner_of = jnp.where(slot_ids < HOT * CAP, hot_owner, cold_owner)
        owner_of = jax.random.permutation(order_key, owner_of)
        row_limit = jax.random.randint(bound_key, (LOOKUPS,), 1, ROWS_DEV + 1)
        row_ids = jax.random.randint(row_key, (LOOKUPS,), 0, row_limit)
        return owner_of * ROWS_DEV + row_ids
    drawn_ids = jax.vmap(per_source)(jnp.arange(OWNERS, dtype=jnp.int32))
    return drawn_ids.reshape(BATCH, FIELDS).astype(jnp.int32)


def with_ends(result, own_key, smallest, top_value):
    index_at = [jax.random.randint(jax.random.fold_in(own_key, axis), (), 0, length) for axis, length in enumerate(result.shape)]
    main_axis = result.shape.index(max(result.shape))
    beside = index_at[:main_axis] + [(index_at[main_axis] + 1) % result.shape[main_axis]] + index_at[main_axis + 1:]
    return result.at[tuple(index_at)].set(smallest).at[tuple(beside)].set(top_value)


def steps_of(stream_key, extent, cuts, least, high):
    level, own = 1.0, jax.random.fold_in(stream_key, 6)
    for axis_at, parts in cuts:
        draws = jnp.exp(jax.random.uniform(jax.random.fold_in(own, axis_at), (parts,), jnp.float32, least / len(cuts), high / len(cuts)))
        level = level * jnp.repeat(draws, extent[axis_at] // parts).reshape([-1 if axis == axis_at else 1 for axis in range(len(extent))])
    return level


def gaussian(rng, shape, deviation, bound, cuts=(), kind=jnp.bfloat16):
    gain = steps_of(rng, shape, cuts, -0.22, 0.18) if cuts else 1.0
    values = jax.random.normal(rng, shape, jnp.float32) * deviation * gain
    return jnp.minimum(jnp.maximum(values, -bound), bound).astype(kind)


def setup_inputs(seed: int = 0) -> dict:
    key_of = jax.random.split(jax.random.key(seed), 17)
    sparse_ids = draw_sparse_ids(jax.random.fold_in(key_of[16], 71), 0)
    dense_feats = gaussian(key_of[1], (BATCH, DENSE), 1.0, 6.0, ((0, 128),), jnp.float32)
    labels = with_ends((jax.random.randint(key_of[2], (BATCH, TASKS), 0, 2) < 1).astype(jnp.int32), jax.random.fold_in(key_of[2], 1), 0, 1)
    tables = gaussian(key_of[3], (FIELDS, VOCAB, EMB), 1.0, 6.0, ((1, 128),), jnp.float32)
    dense_w = gaussian(key_of[4], (DENSE, DPROJ), DENSE ** -0.5, 1.75, (), jnp.float32)
    dense_b = gaussian(key_of[5], (DPROJ,), 0.5, 3.0, (), jnp.float32)
    w_in = gaussian(key_of[6], (EXPERTS, DIN, HID), DIN ** -0.5, 0.25, ((2, 4),))
    b_in = gaussian(key_of[7], (EXPERTS, HID), 0.5, 3.0, ((1, 4),))
    w_out = gaussian(key_of[8], (EXPERTS, HID, EOUT), HID ** -0.5, 0.375, ((1, 4),))
    b_out = gaussian(key_of[9], (EXPERTS, EOUT), 0.5, 3.0, (), jnp.float32)
    gate_w = gaussian(key_of[10], (TASKS, DIN, EXPERTS), (4 * DIN) ** -0.5, 0.125, (), jnp.float32)
    gate_b = gaussian(key_of[11], (TASKS, EXPERTS), 0.1, 0.6, (), jnp.float32)
    tower_w1 = gaussian(key_of[12], (TASKS, EOUT, THID), EOUT ** -0.5, 0.5, (), jnp.float32)
    tower_b1 = gaussian(key_of[13], (TASKS, THID), 0.5, 3.0, (), jnp.float32)
    tower_w2 = gaussian(key_of[14], (TASKS, THID), THID ** -0.5, 0.75, (), jnp.float32)
    tower_b2 = gaussian(key_of[15], (TASKS,), 0.5, 3.0, (), jnp.float32)
    return {"sparse_ids": sparse_ids, "dense_feats": dense_feats, "labels": labels, "tables": tables, "dense_w": dense_w, "dense_b": dense_b, "w_in": w_in, "b_in": b_in, "w_out": w_out, "b_out": b_out, "gate_w": gate_w, "gate_b": gate_b, "tower_w1": tower_w1, "tower_b1": tower_b1, "tower_w2": tower_w2, "tower_b2": tower_b2}


exact_prec = lax.Precision.HIGHEST

@jax.custom_vjp
def low(v):
    return lax.optimization_barrier(v.astype(jnp.bfloat16)).astype(jnp.float32)

@jax.custom_vjp
def low_back(v):
    return v

def low_keep(v):
    return (low(v), None)

def low_pass(kept, grad):
    return (grad,)

def back_keep(v):
    return (v, None)

def back_low(kept, grad):
    return (low(grad),)
low.defvjp(low_keep, low_pass)
low_back.defvjp(back_keep, back_low)

def smooth(value):
    return jax.nn.gelu(value, approximate=True)

def head_loss(inputs, expert_raw, gate_w, gate_b, b_out, tower_w1, tower_b1, tower_w2, tower_b2, label_block):
    row_count = inputs.shape[0]
    logits = jnp.einsum('rd,tdk->rtk', inputs, gate_w, precision=exact_prec) + gate_b[None]
    gate_probs = jax.nn.softmax(logits, axis=-1)
    outputs = expert_raw.reshape(row_count, EXPERTS, EOUT) + b_out[None]
    mixture = jnp.einsum('rtk,rko->rto', gate_probs, outputs, precision=exact_prec)
    tower_mid = smooth(jnp.einsum('rto,toh->rth', mixture, tower_w1, precision=exact_prec) + tower_b1[None])
    task_logit = jnp.einsum('rth,th->rt', tower_mid, tower_w2, precision=exact_prec) + tower_b2[None]
    return jnp.sum(jax.nn.softplus(task_logit) - label_block.astype(jnp.float32) * task_logit)

def forward(tables, dense_w, dense_b, w_in, b_in, w_out, b_out, gate_w, gate_b, tower_w1, tower_b1, tower_w2, tower_b2, dense_feats, sparse_ids, labels):
    picked = tables[jnp.arange(FIELDS, dtype=jnp.int32)[None, :], sparse_ids]
    embedded = picked.reshape(BATCH, FIELDS * EMB)
    projected = jnp.dot(dense_feats, dense_w, precision=exact_prec) + dense_b[None]
    inputs = jnp.concatenate([embedded, projected], axis=1)
    block_rows = min(4096, BATCH)
    block_count = BATCH // block_rows
    weight_in = w_in.transpose(1, 0, 2).reshape(DIN, EXPERTS * HID)
    bias_in = b_in.reshape(-1)

    def block_loss(pieces):
        row_block, label_block = pieces
        low_rows = low(row_block)
        pre_act = low_back(jnp.dot(low_rows, weight_in, precision=exact_prec) + bias_in[None])
        hidden = low(smooth(pre_act))
        product = jnp.einsum('rkh,kho->rko', hidden.reshape(block_rows, EXPERTS, HID), w_out, precision=exact_prec)
        expert_raw = low_back(product.reshape(block_rows, EXPERTS * EOUT))
        return head_loss(low_rows, expert_raw, gate_w, gate_b, b_out, tower_w1, tower_b1, tower_w2, tower_b2, label_block)
    checked = jax.checkpoint(block_loss)

    def step_block(running, pieces):
        return (running + checked(pieces), None)
    running, unused = lax.scan(step_block, jnp.zeros((), jnp.float32), (inputs.reshape(block_count, block_rows, DIN), labels.reshape(block_count, block_rows, TASKS)))
    return running

def reference(sparse_ids, dense_feats, labels, tables, dense_w, dense_b, w_in, b_in, w_out, b_out, gate_w, gate_b, tower_w1, tower_b1, tower_w2, tower_b2):
    params = (tables, dense_w, dense_b, w_in.astype(jnp.float32), b_in.astype(jnp.float32), w_out.astype(jnp.float32), b_out, gate_w, gate_b, tower_w1, tower_b1, tower_w2, tower_b2, dense_feats)

    def loss_of(*param_list):
        return forward(*param_list, sparse_ids, labels)
    loss_value, pullback = jax.vjp(loss_of, *params)
    gradients = pullback(jnp.ones_like(loss_value))
    return (gradients[0], gradients[1], gradients[2], gradients[3], gradients[4], gradients[5], gradients[6], gradients[7], gradients[8], gradients[9], gradients[10], gradients[11], gradients[12], gradients[13])
```

```python
import functools

import jax
import jax.numpy as jnp
from jax import lax
from jax.experimental import pallas as pl
from jax.experimental.pallas import tpu as pltpu
from jax.sharding import PartitionSpec as P

ALL = ("dp", "mp")
EXACT = lax.Precision.HIGHEST
F32 = jnp.float32
BF16 = jnp.bfloat16

OWNERS = 128
FIELDS = 26
EMB = 16
ROWS_LOC = 512
ROWS_DEV = 4096
LOOKUPS = ROWS_LOC * FIELDS
PACKED = FIELDS * ROWS_DEV // 8
CAP = 208
COLD = 96
HOT = 16
SLOTS = 256
GROUPS = SLOTS // 8
EXPERTS = 8
HID = 256
EOUT = 128
TASKS = 2
THID = 64
DIN = 512
DENSE = 13
DPROJ = 96
SMALL = 256
CHUNK = 80

VM = pl.BlockSpec(memory_space=pltpu.VMEM)
SM = pl.BlockSpec(memory_space=pltpu.SMEM)


def params(mib):
    return pltpu.CompilerParams(vmem_limit_bytes=mib * 1024 * 1024)


def shape(dims, dtype):
    return jax.ShapeDtypeStruct(dims, dtype)


def lane_group(rows):
    return lax.broadcasted_iota(jnp.int32, (rows, 128), 1) // EMB


def dot_nt(a, b, precision=None):
    return lax.dot_general(
        a, b, (((1,), (1,)), ((), ())), precision=precision, preferred_element_type=F32
    )


def dot_tn(a, b, precision=None):
    return lax.dot_general(
        a, b, (((0,), (0,)), ((), ())), precision=precision, preferred_element_type=F32
    )


def dot_nn(a, b, precision=None):
    return lax.dot_general(
        a, b, (((1,), (0,)), ((), ())), precision=precision, preferred_element_type=F32
    )


def split3(value):
    high = value.astype(BF16)
    rest = value - high.astype(F32)
    mid = rest.astype(BF16)
    low = (rest - mid.astype(F32)).astype(BF16)
    return high, mid, low


def route_kernel(key_ref, pay_ref, req_ref, src_ref, hot_ref, keys, pays, starts_v, starts, sem):
    keys[pl.ds(0, 104), :] = key_ref[...]
    keys[pl.ds(104, 8), :] = jnp.full((8, 128), 1 << 30, jnp.int32)
    pays[pl.ds(0, 104), :] = pay_ref[...]
    pays[pl.ds(104, 8), :] = jnp.zeros((8, 128), jnp.int32)
    owner_at = lax.broadcasted_iota(jnp.int32, (128, 128), 0)

    def count(step, total):
        rows = keys[pl.ds(pl.multiple_of(step * 8, 8), 8), :] >> 14
        for at in range(8):
            total = total + (rows[at : at + 1, :] < owner_at).astype(jnp.int32)
        return total

    below = lax.fori_loop(0, 13, count, jnp.zeros((128, 128), jnp.int32))
    first = jnp.sum(below.astype(F32).T, axis=0, keepdims=True).astype(jnp.int32)
    starts_v[...] = jnp.broadcast_to(first, (8, 128))
    copy = pltpu.make_async_copy(starts_v, starts, sem)
    copy.start()
    copy.wait()
    for at in range(HOT):
        hot_ref[at] = 0
    lane = lax.broadcasted_iota(jnp.int32, (1, 128), 1)
    turn = (lane % 8) * EMB

    def per_owner(owner, hot_count):
        start = starts[0, owner]
        end = jnp.where(owner == OWNERS - 1, LOOKUPS, starts[0, jnp.minimum(owner + 1, 127)])
        row = start >> 7
        off = start & 127
        back = (128 - off) & 127
        key = [pltpu.roll(keys[pl.ds(row + at, 1), :], back, 1) for at in range(3)]
        pay = [pltpu.roll(pays[pl.ds(row + at, 1), :], back, 1) for at in range(3)]
        for half in range(2):
            here = lane < 128 - off
            seg = jnp.where(here, key[half], key[half + 1])
            load = jnp.where(here, pay[half], pay[half + 1])
            valid = (seg >> 14) == owner
            if half:
                valid = valid & (lane < CAP - 128)
            source = jnp.where(valid, seg & 16383, LOOKUPS)
            wanted = jnp.where(valid, load >> 7, PACKED) * 128 + ((turn - load) & 127)
            src_ref[pl.ds(2 * owner + half, 1), :] = source
            req_ref[pl.ds(2 * owner + half, 1), :] = wanted
        is_hot = (end - start > COLD) & (hot_count < HOT)

        @pl.when(is_hot)
        def _():
            hot_ref[hot_count] = owner

        return hot_count + is_hot.astype(jnp.int32)

    lax.fori_loop(0, OWNERS, per_owner, 0)


def route(keys, pays):
    return pl.pallas_call(
        route_kernel,
        in_specs=[VM, VM],
        out_specs=[VM, VM, SM],
        out_shape=[
            shape((2 * OWNERS, 128), jnp.int32),
            shape((2 * OWNERS, 128), jnp.int32),
            shape((HOT,), jnp.int32),
        ],
        scratch_shapes=[
            pltpu.VMEM((112, 128), jnp.int32),
            pltpu.VMEM((112, 128), jnp.int32),
            pltpu.VMEM((8, 128), jnp.int32),
            pltpu.SMEM((8, 128), jnp.int32),
            pltpu.SemaphoreType.DMA,
        ],
        compiler_params=params(32),
        name="route",
    )(keys, pays)


def pack_kernel(table_ref, out_ref):
    for part in range(4):
        block = jnp.concatenate(
            [table_ref[0, :, pl.ds(part * 1024 + k * 128, 128)] for k in range(8)], axis=0
        )
        out_ref[pl.ds(part * 128, 128), :] = block.T


def pack_tables(tables_t):
    return pl.pallas_call(
        pack_kernel,
        grid=(FIELDS,),
        in_specs=[pl.BlockSpec((1, EMB, ROWS_DEV), lambda f: (f, 0, 0))],
        out_specs=pl.BlockSpec((512, 128), lambda f: (f, 0)),
        out_shape=shape((PACKED + 8, 128), F32),
        compiler_params=params(32),
        name="pack_tables",
    )(tables_t)


def look_up_kernel(ids_ref, table_ref, out_ref, found):
    group = lane_group(1)

    def per_source(source, carry):
        for q in range(CAP // 8):
            total = None
            for g in range(8):
                wanted = ids_ref[source * SLOTS + q * 8 + g]
                row = table_ref[pl.ds(lax.shift_right_logical(wanted, 7), 1), :]
                row = pltpu.roll(row, wanted & 127, 1)
                total = jnp.where(group == g, row, total) if g else row
            found[pl.ds(source * GROUPS + q, 1), :] = total
        return carry

    lax.fori_loop(0, OWNERS, per_source, 0)

    def narrow(step, carry):
        at = pl.ds(pl.multiple_of(step * 512, 512), 512)
        out_ref[at, :] = found[at, :].astype(BF16)
        return carry

    lax.fori_loop(0, OWNERS * GROUPS // 512, narrow, 0)


def look_up(ids, table):
    return pl.pallas_call(
        look_up_kernel,
        in_specs=[SM, VM],
        out_specs=VM,
        out_shape=shape((OWNERS * GROUPS, 128), BF16),
        scratch_shapes=[pltpu.VMEM((OWNERS * GROUPS, 128), F32)],
        compiler_params=params(48),
        name="look_up",
    )(ids, table)


def embed_kernel(src_ref, hot_ref, answer_ref, feats_ref, dw_ref, db_ref, out_ref, wide, rows):
    def widen(step, carry):
        at = pl.ds(pl.multiple_of(step * 512, 512), 512)
        wide[at, :] = answer_ref[at, :].astype(F32)
        return carry

    lax.fori_loop(0, OWNERS * GROUPS // 512, widen, 0)

    def place(owner, first, last):
        for q in range(first, last):
            row = wide[pl.ds(owner * GROUPS + q, 1), :]
            for g in range(8):
                at = src_ref[owner * SLOTS + q * 8 + g]
                rows[pl.ds(at, 1), :] = pltpu.roll(row, 128 - EMB * g, 1) if g else row

    def per_owner(owner, carry):
        place(owner, 0, COLD // 8)
        return carry

    def per_hot(at, carry):
        place(hot_ref[at], COLD // 8, CAP // 8)
        return carry

    lax.fori_loop(0, OWNERS, per_owner, 0)
    lax.fori_loop(0, HOT, per_hot, 0)
    group = lane_group(ROWS_LOC)
    for tile in range(4):
        total = None
        for u in range(min(8, FIELDS - tile * 8)):
            block = rows[pl.ds((tile * 8 + u) * ROWS_LOC, ROWS_LOC), :]
            if u:
                block = pltpu.roll(block, EMB * u, 1)
            total = jnp.where(group == u, block, total) if u else block
        if tile == 3:
            projected = dot_tn(feats_ref[...], dw_ref[...], EXACT) + db_ref[...]
            total = jnp.where(group < 2, total, projected)
        out_ref[:, pl.ds(tile * 128, 128)] = total.astype(BF16)


def embed(src, hot, answer, feats_t, dense_w, dense_b):
    return pl.pallas_call(
        embed_kernel,
        in_specs=[SM, SM, VM, VM, VM, VM],
        out_specs=VM,
        out_shape=shape((ROWS_LOC, DIN), BF16),
        scratch_shapes=[
            pltpu.VMEM((OWNERS * GROUPS, 128), F32),
            pltpu.VMEM((LOOKUPS + 8, 128), F32),
        ],
        compiler_params=params(48),
        name="embed",
    )(src, hot, answer, feats_t, dense_w, dense_b)


C0 = 0.7978845608
C1 = 0.7978845608 * 0.044715


def gelu_both(value):
    square = value * value
    bend = jnp.tanh(value * (C0 + C1 * square))
    half = 0.5 * (1.0 + bend)
    slope = half + 0.5 * value * (1.0 - bend * bend) * (C0 + 3.0 * C1 * square)
    return value * half, slope


def model_kernel(
    x_ref,
    labels_ref,
    feats_ref,
    dw_ref,
    w_in_ref,
    b_in_ref,
    w_out_ref,
    b_out_ref,
    gate_w_ref,
    gate_b_ref,
    w1_ref,
    b1_ref,
    w2_ref,
    b2_ref,
    grads_ref,
    small_ref,
    d_in_ref,
    grad_dense_ref,
    hidden,
    slope,
    outs,
    probs,
    d_raw,
    prod_hi,
    prod_lo,
    mix,
    stage,
):
    x = x_ref[...]
    phase = pl.program_id(0)

    def forward(k, carry):
        pre = dot_nt(x, w_in_ref[k]) + b_in_ref[k].astype(F32)
        act, grad = gelu_both(pre)
        act = act.astype(BF16)
        hidden[k] = act
        slope[k] = grad
        outs[k] = dot_nn(act, w_out_ref[k]) + b_out_ref[k]
        return carry

    def head():
        gate_parts = jnp.concatenate(split3(gate_w_ref[...]), axis=0)
        stage[...] = dot_nt(gate_parts, x)
        logits = stage[0:16] + stage[16:32] + stage[32:48] + gate_b_ref[...]
        logits = logits.reshape(TASKS, EXPERTS, ROWS_LOC)
        gates = jnp.exp(logits - jnp.max(logits, axis=1, keepdims=True))
        gates = gates / jnp.sum(gates, axis=1, keepdims=True)
        gates_t = gates.reshape(TASKS * EXPERTS, ROWS_LOC)
        gate_stack = jnp.concatenate(split3(gates_t), axis=0)
        row_at = lax.broadcasted_iota(jnp.int32, (48, 128), 0) % 16

        def spread(k, carry):
            ones = (row_at == k).astype(F32).astype(BF16)
            probs[k] = dot_tn(gate_stack, ones)
            return carry

        lax.fori_loop(0, TASKS * EXPERTS, spread, 0)

        for t in range(TASKS):
            def add(k, total):
                return total + probs[t * EXPERTS + k] * outs[k]

            mix[:, pl.ds(t * EOUT, EOUT)] = lax.fori_loop(
                1, EXPERTS, add, probs[t * EXPERTS] * outs[0]
            )
        mixture = mix[...]
        zero = jnp.zeros((THID, EOUT), F32)
        w1_bd = jnp.concatenate(
            [
                jnp.concatenate([w1_ref[0], zero], axis=1),
                jnp.concatenate([zero, w1_ref[1]], axis=1),
            ],
            axis=0,
        )
        upper, upper_slope = gelu_both(dot_nt(mixture, w1_bd, EXACT) + b1_ref[...])
        w2_bd = w2_ref[...]
        logit = dot_nt(w2_bd, upper, EXACT) + b2_ref[...]
        d_logit = jax.nn.sigmoid(logit) - labels_ref[...].astype(F32)
        d_pre1 = dot_tn(d_logit, w2_bd, EXACT) * upper_slope
        grad_w2 = dot_nn(d_logit, upper, EXACT)
        grad_b1 = jnp.sum(d_pre1, axis=0, keepdims=True)
        grad_w1 = dot_tn(d_pre1, mixture, EXACT)
        d_mix = dot_nn(d_pre1, w1_bd, EXACT)
        mix[...] = d_mix

        def back_raw(k, carry):
            d_one = mix[:, pl.ds(0, EOUT)]
            d_two = mix[:, pl.ds(EOUT, EOUT)]
            grad = probs[k] * d_one + probs[EXPERTS + k] * d_two
            small_ref[pl.ds(128 + k, 1), :] = jnp.sum(grad, axis=0, keepdims=True)
            d_raw[k] = grad.astype(BF16)
            value = outs[k]
            for t, d_task in enumerate((d_one, d_two)):
                product = value * d_task
                high = product.astype(BF16)
                at = pl.ds(pl.multiple_of((t * EXPERTS + k) * EOUT, EOUT), EOUT)
                prod_hi[:, at] = high
                prod_lo[:, at] = (product - high.astype(F32)).astype(BF16)
            return carry

        lax.fori_loop(0, EXPERTS, back_raw, 0)

        wide = TASKS * EXPERTS * EOUT
        column_gate = lax.broadcasted_iota(jnp.int32, (16, wide), 1) // EOUT
        own_gate = lax.broadcasted_iota(jnp.int32, (16, wide), 0)
        ones = (column_gate == own_gate).astype(F32).astype(BF16)
        stage[0:16] = dot_nt(ones, prod_hi[...])
        stage[16:32] = dot_nt(ones, prod_lo[...])
        d_gates = stage[0:16] + stage[16:32]
        d_gates = d_gates.reshape(TASKS, EXPERTS, ROWS_LOC)
        mean = jnp.sum(d_gates * gates, axis=1, keepdims=True)
        d_logits = (gates * (d_gates - mean)).reshape(16, ROWS_LOC)
        d_parts = jnp.concatenate(split3(d_logits), axis=0)
        stage[...] = dot_nn(d_parts, x)
        grad_gate = stage[0:16] + stage[16:32] + stage[32:48]
        d_in_ref[...] = dot_tn(d_logits, gate_w_ref[...], EXACT)
        small_ref[pl.ds(0, THID), :] = grad_w1[0:THID, 0:EOUT]
        small_ref[pl.ds(THID, THID), :] = grad_w1[THID : 2 * THID, EOUT : 2 * EOUT]
        for tile in range(4):
            small_ref[pl.ds(136 + 16 * tile, 16), :] = grad_gate[:, tile * 128 : tile * 128 + 128]
        small_ref[pl.ds(217, 1), :] = grad_b1
        lane = lax.broadcasted_iota(jnp.int32, (1, 128), 1)
        small_ref[pl.ds(218, 1), :] = jnp.where(lane < THID, grad_w2[0:1], grad_w2[1:2])
        small_ref[pl.ds(219, 1), :] = jnp.zeros((1, 128), F32)
        small_ref[pl.ds(220, 2), :] = jnp.broadcast_to(
            jnp.sum(d_logit, axis=1, keepdims=True), (2, 128)
        )
        small_ref[pl.ds(222, 2), :] = jnp.zeros((2, 128), F32)
        small_ref[pl.ds(224, 16), :] = jnp.broadcast_to(
            jnp.sum(d_logits, axis=1, keepdims=True), (16, 128)
        )

    def backward(k, carry):
        d_out = d_raw[k]
        grad_out = dot_tn(hidden[k], d_out).astype(BF16)
        d_pre = (dot_nt(d_out, w_out_ref[k]) * slope[k]).astype(BF16)
        bias = jnp.sum(d_pre.astype(F32), axis=0, keepdims=True)
        small_ref[pl.ds(240 + 2 * k, 1), :] = bias[:, 0:128]
        small_ref[pl.ds(241 + 2 * k, 1), :] = bias[:, 128:256]
        grad_in = dot_tn(d_pre, x).astype(BF16)
        for part in range(4):
            for block in range(5):
                for piece in range(4):
                    at = block * 64 + piece * 16
                    rows = slice(part * 64 + piece * 16, part * 64 + piece * 16 + 16)
                    if block < 4:
                        value = grad_in[rows, block * 128 : block * 128 + 128]
                    else:
                        value = grad_out[rows, :]
                    grads_ref[4 * k + at // CHUNK, part, pl.ds(at % CHUNK, 16), :] = value
        d_in_ref[...] += dot_nn(d_pre, w_in_ref[k])
        return carry

    def tail():
        d_last = d_in_ref[:, pl.ds(384, 128)]
        small_ref[pl.ds(200, 16), :] = jnp.zeros((16, 128), F32)
        small_ref[pl.ds(200, DENSE), :] = dot_nn(feats_ref[...], d_last, EXACT)
        small_ref[pl.ds(216, 1), :] = jnp.sum(d_last, axis=0, keepdims=True)
        grad_dense_ref[...] = dot_nt(dw_ref[...], d_last, EXACT)

    @pl.when(phase == 0)
    def _():
        lax.fori_loop(0, EXPERTS, forward, 0)

    @pl.when(phase == 1)
    def _():
        head()

    @pl.when(phase == 2)
    def _():
        lax.fori_loop(0, EXPERTS, backward, 0)
        tail()


def model(*operands):
    return pl.pallas_call(
        model_kernel,
        grid=(3,),
        in_specs=[VM] * 14,
        out_specs=[VM] * 4,
        out_shape=[
            shape((32, 4, CHUNK, 128), BF16),
            shape((SMALL, 128), F32),
            shape((ROWS_LOC, DIN), F32),
            shape((DENSE, ROWS_LOC), F32),
        ],
        scratch_shapes=[
            pltpu.VMEM((EXPERTS, ROWS_LOC, HID), BF16),
            pltpu.VMEM((EXPERTS, ROWS_LOC, HID), F32),
            pltpu.VMEM((EXPERTS, ROWS_LOC, EOUT), F32),
            pltpu.VMEM((TASKS * EXPERTS, ROWS_LOC, EOUT), F32),
            pltpu.VMEM((EXPERTS, ROWS_LOC, EOUT), BF16),
            pltpu.VMEM((ROWS_LOC, TASKS * EXPERTS * EOUT), BF16),
            pltpu.VMEM((ROWS_LOC, TASKS * EXPERTS * EOUT), BF16),
            pltpu.VMEM((ROWS_LOC, TASKS * EOUT), F32),
            pltpu.VMEM((48, DIN), F32),
        ],
        compiler_params=params(56),
        name="model",
    )(*operands)


def spread_kernel(src_ref, hot_ref, d_ref, out_ref, wide, rows):
    for field in range(FIELDS):
        block = d_ref[:, pl.ds((field // 8) * 128, 128)]
        if field % 8:
            block = pltpu.roll(block, 128 - EMB * (field % 8), 1)
        rows[pl.ds(field * ROWS_LOC, ROWS_LOC), :] = block
    rows[pl.ds(LOOKUPS, 8), :] = jnp.zeros((8, 128), F32)
    group = lane_group(1)

    def collect(owner, first, last):
        for q in range(first, last):
            total = None
            for g in range(8):
                at = src_ref[owner * SLOTS + q * 8 + g]
                row = rows[pl.ds(at, 1), :]
                total = jnp.where(group == g, pltpu.roll(row, EMB * g, 1), total) if g else row
            wide[pl.ds(owner * GROUPS + q, 1), :] = total

    def per_owner(owner, carry):
        collect(owner, 0, COLD // 8)
        return carry

    def per_hot(at, carry):
        collect(hot_ref[at], COLD // 8, CAP // 8)
        return carry

    lax.fori_loop(0, OWNERS, per_owner, 0)
    lax.fori_loop(0, HOT, per_hot, 0)

    def narrow(step, carry):
        at = pl.ds(pl.multiple_of(step * 512, 512), 512)
        out_ref[at, :] = wide[at, :].astype(BF16)
        return carry

    lax.fori_loop(0, OWNERS * GROUPS // 512, narrow, 0)


def spread_grads(src, hot, d_inputs):
    return pl.pallas_call(
        spread_kernel,
        in_specs=[SM, SM, VM],
        out_specs=VM,
        out_shape=shape((OWNERS * GROUPS, 128), BF16),
        scratch_shapes=[
            pltpu.VMEM((OWNERS * GROUPS, 128), F32),
            pltpu.VMEM((LOOKUPS + 8, 128), F32),
        ],
        compiler_params=params(48),
        name="spread_grads",
    )(src, hot, d_inputs)


PARTS = 4


def scatter_kernel(ids_ref, grads_ref, out_ref, wide, *sums):
    def widen(step, carry):
        at = pl.ds(pl.multiple_of(step * 512, 512), 512)
        wide[at, :] = grads_ref[at, :].astype(F32)
        return carry

    lax.fori_loop(0, OWNERS * GROUPS // 512, widen, 0)

    def clear(step, carry):
        at = pl.ds(pl.multiple_of(step * 512, 512), 512)
        for total in sums:
            total[at, :] = jnp.zeros((512, 128), F32)
        return carry

    lax.fori_loop(0, PACKED // 512, clear, 0)
    group = lane_group(1)

    def per_source(source, carry):
        for q in range(CAP // 8):
            row = wide[pl.ds(source * GROUPS + q, 1), :]
            for g in range(8):
                wanted = ids_ref[source * SLOTS + q * 8 + g]
                part = jnp.where(group == g, row, 0.0)
                part = pltpu.roll(part, (128 - wanted) & 127, 1)
                at = pl.ds(lax.shift_right_logical(wanted, 7), 1)
                total = sums[g % PARTS]
                total[at, :] = total[at, :] + part
        return carry

    lax.fori_loop(0, OWNERS, per_source, 0)

    def write(field, carry):
        for part in range(4):
            at = pl.ds(pl.multiple_of(field * 512 + part * 128, 128), 128)
            block = sums[0][at, :]
            for total in sums[1:]:
                block = block + total[at, :]
            block = block.T
            for k in range(8):
                out_ref[field, :, pl.ds(part * 1024 + k * 128, 128)] = block[16 * k : 16 * k + 16]
        return carry

    lax.fori_loop(0, FIELDS, write, 0)


def scatter_add(ids, grads):
    return pl.pallas_call(
        scatter_kernel,
        in_specs=[SM, VM],
        out_specs=VM,
        out_shape=shape((FIELDS, EMB, ROWS_DEV), F32),
        scratch_shapes=[pltpu.VMEM((OWNERS * GROUPS, 128), F32)]
        + [pltpu.VMEM((PACKED + 8, 128), F32)] * PARTS,
        compiler_params=params(56),
        name="scatter_add",
    )(ids, grads)


def sum_kernel(parts_ref, out_ref):
    total = parts_ref[0].astype(F32)

    def add(at, total):
        return total + parts_ref[at].astype(F32)

    total = lax.fori_loop(1, OWNERS, add, total)
    for at in range(out_ref.shape[0]):
        out_ref[at] = total.astype(out_ref.dtype)


def sum_parts(parts, copies, name):
    return pl.pallas_call(
        sum_kernel,
        in_specs=[VM],
        out_specs=VM,
        out_shape=shape((copies,) + parts.shape[1:], parts.dtype),
        compiler_params=params(32),
        name=name,
    )(parts)


def exchange(value, axes):
    return lax.all_to_all(value, axes, split_axis=0, concat_axis=0, tiled=True)


def body(
    sparse_ids,
    dense_feats,
    labels,
    tables,
    dense_w,
    dense_b,
    w_in,
    b_in,
    w_out,
    b_out,
    gate_w,
    gate_b,
    tower_w1,
    tower_b1,
    tower_w2,
    tower_b2,
):
    part = lax.axis_index("mp")
    w_in_all = lax.all_gather(w_in.transpose(0, 2, 1), "mp", axis=1, tiled=True)
    w_out_all = lax.all_gather(w_out, "mp", axis=1, tiled=True)
    b_in_all = lax.all_gather(b_in, "mp", axis=1, tiled=True)

    ids = sparse_ids.T
    field = lax.broadcasted_iota(jnp.int32, (FIELDS, ROWS_LOC), 0)
    example = lax.broadcasted_iota(jnp.int32, (FIELDS, ROWS_LOC), 1)
    row = ids & (ROWS_DEV - 1)
    packed = field * 512 + (row >> 10) * 128 + (row & 127)
    key = ((ids >> 12) << 14) | (field * ROWS_LOC + example)
    load = (packed << 7) | (((row >> 7) & 7) * EMB)
    keys, loads = lax.sort((key.reshape(-1), load.reshape(-1)), num_keys=1, is_stable=False)
    requests, sources, hot = route(keys.reshape(-1, 128), loads.reshape(-1, 128))
    asked = exchange(requests, ALL).reshape(-1)
    sources = sources.reshape(-1)
    table = pack_tables(tables.transpose(0, 2, 1))
    answer = exchange(look_up(asked, table), ALL)
    feats_t = dense_feats.T
    dense_pad = jnp.pad(dense_w, ((0, 0), (128 - DPROJ, 0)))
    bias_pad = jnp.pad(dense_b, (128 - DPROJ, 0)).reshape(1, 128)
    inputs = embed(sources, hot, answer, feats_t, dense_pad, bias_pad)
    task_at = lax.broadcasted_iota(jnp.int32, (TASKS, TASKS * THID), 1) // THID
    task_row = lax.broadcasted_iota(jnp.int32, (TASKS, TASKS * THID), 0)
    w2_bd = jnp.where(task_at == task_row, tower_w2.reshape(1, -1), 0.0)
    grads, small, d_inputs, grad_dense = model(
        inputs,
        labels.T,
        feats_t,
        dense_pad,
        w_in_all,
        b_in_all.reshape(EXPERTS, 1, HID),
        w_out_all,
        b_out.reshape(EXPERTS, 1, EOUT),
        gate_w.transpose(0, 2, 1).reshape(TASKS * EXPERTS, DIN),
        gate_b.reshape(TASKS * EXPERTS, 1),
        tower_w1.transpose(0, 2, 1),
        tower_b1.reshape(1, TASKS * THID),
        w2_bd,
        tower_b2.reshape(TASKS, 1),
    )
    grads = exchange(grads.reshape(OWNERS, CHUNK, 128), ALL)
    small = exchange(small.reshape(OWNERS, 2, 128), ALL)
    incoming = exchange(spread_grads(sources, hot, d_inputs), ALL)
    grads = exchange(sum_parts(grads, 32, "sum_grads"), "dp")
    small = exchange(sum_parts(small, OWNERS, "sum_small"), ALL).reshape(SMALL, 128)
    grad_tables = scatter_add(asked, incoming).transpose(0, 2, 1)

    grads = grads.reshape(EXPERTS, 5, 64, 128).astype(F32)
    grad_w_in = grads[:, :4].transpose(0, 1, 3, 2).reshape(EXPERTS, DIN, 64)
    grad_w_out = grads[:, 4]
    grad_w1 = small[0:128].reshape(TASKS, THID, EOUT).transpose(0, 2, 1)
    grad_b_out = small[128:136]
    grad_gate_w = small[136:200].reshape(4, TASKS, EXPERTS, 128)
    grad_gate_w = grad_gate_w.transpose(1, 0, 3, 2).reshape(TASKS, DIN, EXPERTS)
    grad_dense_w = small[200 : 200 + DENSE, 128 - DPROJ :]
    grad_dense_b = small[216, 128 - DPROJ :]
    grad_b1 = small[217].reshape(TASKS, THID)
    grad_w2 = small[218].reshape(TASKS, THID)
    grad_b2 = small[220:222, 0]
    grad_gate_b = small[224:240, 0].reshape(TASKS, EXPERTS)
    grad_b_in = small[240:256].reshape(EXPERTS, HID)
    grad_b_in = lax.dynamic_slice(grad_b_in, (0, part * 64), (EXPERTS, 64))
    return (
        grad_tables,
        grad_dense_w,
        grad_dense_b,
        grad_w_in,
        grad_b_in,
        grad_w_out,
        grad_b_out,
        grad_gate_w,
        grad_gate_b,
        grad_w1,
        grad_b1,
        grad_w2,
        grad_b2,
        grad_dense.T,
    )


def solution(mesh):
    return jax.shard_map(
        body,
        mesh=mesh,
        in_specs=(
            P(ALL, None),
            P(ALL, None),
            P(ALL, None),
            P(None, ALL, None),
            P(),
            P(),
            P(None, None, "mp"),
            P(None, "mp"),
            P(None, "mp", None),
            P(),
            P(),
            P(),
            P(),
            P(),
            P(),
            P(),
        ),
        out_specs=(
            P(None, ALL, None),
            P(),
            P(),
            P(None, None, "mp"),
            P(None, "mp"),
            P(None, "mp", None),
            P(),
            P(),
            P(),
            P(),
            P(),
            P(),
            P(),
            P(ALL, None),
        ),
        check_vma=False,
    )
```

```python
import functools

import jax
import jax.numpy as jnp
from jax import lax
from jax.experimental import pallas as pl
from jax.experimental.pallas import tpu as pltpu
from jax.sharding import PartitionSpec as P

ALL = ("dp", "mp")
EXACT = lax.Precision.HIGHEST
F32 = jnp.float32
BF16 = jnp.bfloat16

OWNERS = 128
FIELDS = 26
EMB = 16
ROWS_LOC = 512
ROWS_DEV = 4096
LOOKUPS = ROWS_LOC * FIELDS
PACKED = FIELDS * ROWS_DEV // 8
CAP = 208
COLD = 96
HOT = 16
SLOTS = 256
GROUPS = SLOTS // 8
EXPERTS = 8
HID = 256
EOUT = 128
TASKS = 2
THID = 64
DIN = 512
DENSE = 13
DPROJ = 96
CHUNK = 80
TILES = 32
SENT = CHUNK + 16
PART = 64
SUMS = 6

VM = pl.BlockSpec(memory_space=pltpu.VMEM)
SM = pl.BlockSpec(memory_space=pltpu.SMEM)


def params(mib):
    return pltpu.CompilerParams(vmem_limit_bytes=mib * 1024 * 1024)


def shape(dims, dtype):
    return jax.ShapeDtypeStruct(dims, dtype)


def lane_group(rows):
    return lax.broadcasted_iota(jnp.int32, (rows, 128), 1) // EMB


def sublane_group():
    return lax.broadcasted_iota(jnp.int32, (128, 128), 0) // EMB


def eight(index, unit=8):
    return pl.multiple_of(index, unit)


def dot_nt(a, b, precision=None):
    return lax.dot_general(
        a, b, (((1,), (1,)), ((), ())), precision=precision, preferred_element_type=F32
    )


def dot_tn(a, b, precision=None):
    return lax.dot_general(
        a, b, (((0,), (0,)), ((), ())), precision=precision, preferred_element_type=F32
    )


def dot_nn(a, b, precision=None):
    return lax.dot_general(
        a, b, (((1,), (0,)), ((), ())), precision=precision, preferred_element_type=F32
    )


def split3(value):
    high = value.astype(BF16)
    rest = value - high.astype(F32)
    mid = rest.astype(BF16)
    low = (rest - mid.astype(F32)).astype(BF16)
    return high, mid, low


def route_kernel(key_ref, load_ref, req_ref, src_ref, hot_ref, both, cut, starts_v, starts, sem):
    own = (key_ref[...] & 16383) << 17
    both[pl.ds(0, 104), :] = own | load_ref[...]
    both[pl.ds(104, 8), :] = jnp.zeros((8, 128), jnp.int32)
    owner_at = lax.broadcasted_iota(jnp.int32, (128, 128), 0)

    def count(step, total):
        rows = key_ref[pl.ds(eight(step * 8), 8), :] >> 14
        for at in range(8):
            total = total + (rows[at : at + 1, :] < owner_at).astype(jnp.int32)
        return total

    below = lax.fori_loop(0, 13, count, jnp.zeros((128, 128), jnp.int32))
    first = jnp.sum(below.astype(F32).T, axis=0, keepdims=True).astype(jnp.int32)
    starts_v[...] = jnp.broadcast_to(first, (8, 128))
    copy = pltpu.make_async_copy(starts_v, starts, sem)
    copy.start()
    copy.wait()
    for at in range(2 * HOT):
        hot_ref[at] = 0
    lane = lax.broadcasted_iota(jnp.int32, (1, 128), 1)
    unused = (LOOKUPS << 17) | (PACKED * 8)

    def per_owner(owner, hot_count):
        start = starts[0, owner]
        end = jnp.where(owner == OWNERS - 1, LOOKUPS, starts[0, jnp.minimum(owner + 1, 127)])
        row = start >> 7
        off = start & 127
        pieces = [both[pl.ds(row + at, 1), :] for at in range(3)]
        for half in range(2):
            piece = jnp.where(lane >= off, pieces[half], pieces[half + 1])
            piece = pltpu.roll(piece, (128 - off) & 127, 1)
            cut[pl.ds(2 * owner + half, 1), :] = jnp.where(
                lane < end - start - 128 * half, piece, unused
            )
        hot_ref[hot_count] = owner
        return jnp.minimum(hot_count + (end - start > COLD).astype(jnp.int32), 2 * HOT - 1)

    lax.fori_loop(0, OWNERS, per_owner, 0, unroll=8)
    src_ref[...] = cut[...] >> 17
    req_ref[...] = cut[...] & ((1 << 17) - 1)


def route(keys, loads):
    return pl.pallas_call(
        route_kernel,
        in_specs=[VM, VM],
        out_specs=[VM, VM, SM],
        out_shape=[
            shape((2 * OWNERS, 128), jnp.int32),
            shape((2 * OWNERS, 128), jnp.int32),
            shape((2 * HOT,), jnp.int32),
        ],
        scratch_shapes=[
            pltpu.VMEM((112, 128), jnp.int32),
            pltpu.VMEM((2 * OWNERS, 128), jnp.int32),
            pltpu.VMEM((8, 128), jnp.int32),
            pltpu.SMEM((8, 128), jnp.int32),
            pltpu.SemaphoreType.DMA,
        ],
        compiler_params=params(32),
        name="route",
    )(keys, loads)


def pack_kernel(table_ref, out_ref):
    for part in range(4):
        block = jnp.concatenate(
            [table_ref[0, :, pl.ds(part * 1024 + k * 128, 128)] for k in range(8)], axis=0
        )
        out_ref[pl.ds(part * 128, 128), :] = block.T


def pack_tables(tables_t):
    return pl.pallas_call(
        pack_kernel,
        grid=(FIELDS,),
        in_specs=[pl.BlockSpec((1, EMB, ROWS_DEV), lambda f: (f, 0, 0))],
        out_specs=pl.BlockSpec((512, 128), lambda f: (f, 0)),
        out_shape=shape((PACKED + 8, 128), F32),
        compiler_params=params(32),
        name="pack_tables",
    )(tables_t)


def split_wanted(asked_ref, rows_v, groups, rows, sem):
    rows_v[...] = asked_ref[...] >> 3
    copy = pltpu.make_async_copy(rows_v, rows, sem)
    copy.start()
    groups[...] = asked_ref[...] & 7
    copy.wait()


def split_scratch():
    return [
        pltpu.VMEM((2 * OWNERS, 128), jnp.int32),
        pltpu.VMEM((2 * OWNERS, 128), jnp.int32),
        pltpu.SMEM((2 * OWNERS, 128), jnp.int32),
        pltpu.SemaphoreType.DMA,
    ]


def look_up_kernel(asked_ref, table_ref, out_ref, rows_v, groups, rows, sem, even, odd):
    split_wanted(asked_ref, rows_v, groups, rows, sem)
    at_group = sublane_group()

    def gather(source, found):
        for n in range(CAP):
            at = rows[2 * source + n // 128, n % 128]
            found[pl.ds(n, 1), :] = table_ref[pl.ds(at, 1), :]

    def pick(source, found):
        for half in range(2):
            block = found[pl.ds(half * 128, 128), :].T
            block = jnp.where(at_group == groups[pl.ds(2 * source + half, 1), :], block, 0.0)
            block = jnp.sum(block.reshape(8, EMB, 128), axis=0)
            out_ref[pl.ds(eight(source * GROUPS + EMB * half, EMB), EMB), :] = block.astype(BF16)

    even[...] = jnp.zeros_like(even)
    odd[...] = jnp.zeros_like(odd)
    gather(0, even)

    def two_sources(step, carry):
        source = 2 * step
        gather(source + 1, odd)
        pick(source, even)
        gather(jnp.minimum(source + 2, OWNERS - 1), even)
        pick(source + 1, odd)
        return carry

    lax.fori_loop(0, OWNERS // 2, two_sources, 0)


def look_up(asked, table):
    return pl.pallas_call(
        look_up_kernel,
        in_specs=[VM, VM],
        out_specs=VM,
        out_shape=shape((OWNERS * GROUPS, 128), BF16),
        scratch_shapes=split_scratch() + [pltpu.VMEM((SLOTS, 128), F32)] * 2,
        compiler_params=params(48),
        name="look_up",
    )(asked, table)


def embed_kernel(
    src_ref, hot_ref, ids_ref, answer_ref, feats_ref, dw_ref, db_ref, out_ref, slots, rows, x_t
):
    for block in range(32):
        owner, half = block // 2 * 8, block % 2
        parts = [
            answer_ref[pl.ds((owner + u) * GROUPS + EMB * half, EMB), :] for u in range(8)
        ]
        slots[pl.ds(block * 128, 128), :] = jnp.concatenate(parts, axis=0).astype(F32).T

    def cold(step, carry):
        base = step // 6 * SLOTS + step % 6 * 16
        source = step // 6 * (8 * SLOTS) + step % 6 * 16
        for n in range(16):
            row = slots[pl.ds(base + n, 1), :]
            for u in range(8):
                rows[pl.ds(src_ref[source + u * SLOTS + n], 1), :] = row
        return carry

    def hot(at, carry):
        owner = hot_ref[at]
        base = (owner >> 3) * SLOTS
        for n in range(COLD, CAP):
            rows[pl.ds(src_ref[owner * SLOTS + n], 1), :] = slots[pl.ds(base + n, 1), :]
        return carry

    lax.fori_loop(0, OWNERS // 8 * 6, cold, 0)
    lax.fori_loop(0, HOT, hot, 0)
    at_group = sublane_group()

    def field(f, carry):
        group = (ids_ref[pl.ds(f, 1), :] >> 12) & 7
        for part in range(4):
            block = rows[pl.ds(eight(f * ROWS_LOC + part * 128, 128), 128), :].T
            block = jnp.where(at_group == group[:, part * 128 : part * 128 + 128], block, 0.0)
            block = jnp.sum(block.reshape(8, EMB, 128), axis=0)
            x_t[pl.ds(eight(f * EMB, EMB), EMB), pl.ds(part * 128, 128)] = block
        return carry

    lax.fori_loop(0, FIELDS, field, 0)
    x_t[pl.ds(FIELDS * EMB, DPROJ), :] = dot_tn(dw_ref[...], feats_ref[...], EXACT) + db_ref[...]
    out_ref[...] = x_t[...].T.astype(BF16)


def embed(src, hot, ids, answer, feats_t, dense_w, dense_b):
    return pl.pallas_call(
        embed_kernel,
        in_specs=[SM, SM, VM, VM, VM, VM, VM],
        out_specs=VM,
        out_shape=shape((ROWS_LOC, DIN), BF16),
        scratch_shapes=[
            pltpu.VMEM((OWNERS * GROUPS, 128), F32),
            pltpu.VMEM((LOOKUPS + 8, 128), F32),
            pltpu.VMEM((DIN, ROWS_LOC), F32),
        ],
        compiler_params=params(48),
        name="embed",
    )(src, hot, ids, answer, feats_t, dense_w, dense_b)


C0 = 0.7978845608
C1 = 0.7978845608 * 0.044715


def gelu_both(value):
    square = value * value
    bend = jnp.tanh(value * (C0 + C1 * square))
    half = 0.5 * (1.0 + bend)
    slope = half + 0.5 * value * (1.0 - bend * bend) * (C0 + 3.0 * C1 * square)
    return value * half, slope


def two_parts(value):
    high = value.astype(BF16).astype(F32)
    return jnp.concatenate([high, value - high], axis=0).astype(BF16)


def one_of(parts):
    wide = parts.astype(F32)
    return wide[0:8] + wide[8:16]


def model_kernel(
    x_ref,
    labels_ref,
    feats_ref,
    dw_ref,
    weights_ref,
    b_out_ref,
    gate_w_ref,
    gate_b_ref,
    w1_ref,
    b1_ref,
    w2_ref,
    b2_ref,
    grads_ref,
    d_low_ref,
    grad_dense_ref,
    small_ref,
    small_b,
    d_in_ref,
    hidden,
    slope,
    outs,
    probs,
    d_raw,
    prod_hi,
    prod_lo,
    mix,
    stage,
):
    x = x_ref[...]
    phase = pl.program_id(0)

    def weights_in(k):
        return jnp.concatenate(
            [weights_ref[p, k, pl.ds(0, PART), pl.ds(0, DIN)] for p in range(4)], axis=0
        )

    def weights_out(k):
        return jnp.concatenate(
            [weights_ref[p, k, pl.ds(0, PART), pl.ds(DIN, EOUT)] for p in range(4)], axis=0
        )

    def forward(k, carry):
        bias = [
            weights_ref[p, k, pl.ds(PART, 16), pl.ds(0, 128)].astype(F32)[0:1, 0:PART]
            for p in range(4)
        ]
        pre = dot_nt(x, weights_in(k)) + jnp.concatenate(bias, axis=1)
        act, grad = gelu_both(pre)
        act = act.astype(BF16)
        hidden[k] = act
        slope[k] = grad
        outs[k] = dot_nn(act, weights_out(k)) + b_out_ref[k]
        return carry

    def head():
        gate_parts = jnp.concatenate(split3(gate_w_ref[...]), axis=0)
        stage[...] = dot_nt(gate_parts, x)
        logits = stage[0:16] + stage[16:32] + stage[32:48] + gate_b_ref[...]
        logits = logits.reshape(TASKS, EXPERTS, ROWS_LOC)
        gates = jnp.exp(logits - jnp.max(logits, axis=1, keepdims=True))
        gates = gates / jnp.sum(gates, axis=1, keepdims=True)
        gates_t = gates.reshape(TASKS * EXPERTS, ROWS_LOC)
        gate_stack = jnp.concatenate(split3(gates_t), axis=0)
        row_at = lax.broadcasted_iota(jnp.int32, (48, 128), 0) % 16

        def spread(k, carry):
            ones = (row_at == k).astype(F32).astype(BF16)
            probs[k] = dot_tn(gate_stack, ones)
            return carry

        lax.fori_loop(0, TASKS * EXPERTS, spread, 0)

        for t in range(TASKS):
            def add(k, total):
                return total + probs[t * EXPERTS + k] * outs[k]

            mix[:, pl.ds(t * EOUT, EOUT)] = lax.fori_loop(
                1, EXPERTS, add, probs[t * EXPERTS] * outs[0]
            )
        mixture = mix[...]
        zero = jnp.zeros((THID, EOUT), F32)
        w1_bd = jnp.concatenate(
            [
                jnp.concatenate([w1_ref[0], zero], axis=1),
                jnp.concatenate([zero, w1_ref[1]], axis=1),
            ],
            axis=0,
        )
        upper, upper_slope = gelu_both(dot_nt(mixture, w1_bd, EXACT) + b1_ref[...])
        w2_bd = w2_ref[...]
        logit = dot_nt(w2_bd, upper, EXACT) + b2_ref[...]
        d_logit = jax.nn.sigmoid(logit) - labels_ref[...].astype(F32)
        d_pre1 = dot_tn(d_logit, w2_bd, EXACT) * upper_slope
        grad_w2 = dot_nn(d_logit, upper, EXACT)
        grad_b1 = jnp.sum(d_pre1, axis=0, keepdims=True)
        grad_w1 = dot_tn(d_pre1, mixture, EXACT)
        d_mix = dot_nn(d_pre1, w1_bd, EXACT)
        mix[...] = d_mix

        def back_raw(k, carry):
            d_one = mix[:, pl.ds(0, EOUT)]
            d_two = mix[:, pl.ds(EOUT, EOUT)]
            grad = probs[k] * d_one + probs[EXPERTS + k] * d_two
            small_ref[pl.ds(128 + k, 1), :] = jnp.sum(grad, axis=0, keepdims=True)
            d_raw[k] = grad.astype(BF16)
            value = outs[k]
            for t, d_task in enumerate((d_one, d_two)):
                product = value * d_task
                high = product.astype(BF16)
                at = pl.ds(pl.multiple_of((t * EXPERTS + k) * EOUT, EOUT), EOUT)
                prod_hi[:, at] = high
                prod_lo[:, at] = (product - high.astype(F32)).astype(BF16)
            return carry

        lax.fori_loop(0, EXPERTS, back_raw, 0)

        wide = TASKS * EXPERTS * EOUT
        column_gate = lax.broadcasted_iota(jnp.int32, (16, wide), 1) // EOUT
        own_gate = lax.broadcasted_iota(jnp.int32, (16, wide), 0)
        ones = (column_gate == own_gate).astype(F32).astype(BF16)
        stage[0:16] = dot_nt(ones, prod_hi[...])
        stage[16:32] = dot_nt(ones, prod_lo[...])
        d_gates = stage[0:16] + stage[16:32]
        d_gates = d_gates.reshape(TASKS, EXPERTS, ROWS_LOC)
        mean = jnp.sum(d_gates * gates, axis=1, keepdims=True)
        d_logits = (gates * (d_gates - mean)).reshape(16, ROWS_LOC)
        d_parts = jnp.concatenate(split3(d_logits), axis=0)
        stage[...] = dot_nn(d_parts, x)
        grad_gate = stage[0:16] + stage[16:32] + stage[32:48]
        d_in_ref[...] = dot_tn(d_logits, gate_w_ref[...], EXACT)
        small_ref[pl.ds(0, THID), :] = grad_w1[0:THID, 0:EOUT]
        small_ref[pl.ds(THID, THID), :] = grad_w1[THID : 2 * THID, EOUT : 2 * EOUT]
        for tile in range(4):
            small_ref[pl.ds(136 + 16 * tile, 16), :] = grad_gate[:, tile * 128 : tile * 128 + 128]
        small_ref[pl.ds(217, 1), :] = grad_b1
        lane = lax.broadcasted_iota(jnp.int32, (1, 128), 1)
        small_ref[pl.ds(218, 1), :] = jnp.where(lane < THID, grad_w2[0:1], grad_w2[1:2])
        small_ref[pl.ds(219, 1), :] = jnp.zeros((1, 128), F32)
        small_b[...] = jnp.zeros_like(small_b)
        small_ref[pl.ds(220, 2), :] = jnp.broadcast_to(
            jnp.sum(d_logit, axis=1, keepdims=True), (2, 128)
        )
        small_ref[pl.ds(222, 2), :] = jnp.zeros((2, 128), F32)
        small_ref[pl.ds(224, 16), :] = jnp.broadcast_to(
            jnp.sum(d_logits, axis=1, keepdims=True), (16, 128)
        )

    def backward(k, carry):
        d_out = d_raw[k]
        grad_out = dot_tn(hidden[k], d_out).astype(BF16)
        d_pre = (dot_nt(d_out, weights_out(k)) * slope[k]).astype(BF16)
        bias = jnp.sum(d_pre.astype(F32), axis=0, keepdims=True)
        for p in range(4):
            small_b[p, pl.ds(k, 1), pl.ds(0, PART)] = bias[:, PART * p : PART * p + PART]
        grad_in = dot_tn(d_pre, x).astype(BF16)
        for part in range(4):
            for block in range(5):
                for piece in range(4):
                    at = block * 64 + piece * 16
                    rows = slice(part * 64 + piece * 16, part * 64 + piece * 16 + 16)
                    if block < 4:
                        value = grad_in[rows, block * 128 : block * 128 + 128]
                    else:
                        value = grad_out[rows, :]
                    grads_ref[4 * k + at // CHUNK, part, pl.ds(at % CHUNK, 16), :] = value
        d_in_ref[...] += dot_nn(d_pre, weights_in(k))
        return carry

    def tail():
        d_last = d_in_ref[:, pl.ds(DIN - DPROJ, DPROJ)]
        small_ref[pl.ds(200, 16), :] = jnp.zeros((16, 128), F32)
        small_ref[pl.ds(200, DENSE), pl.ds(0, DPROJ)] = dot_nn(feats_ref[...], d_last, EXACT)
        small_ref[pl.ds(216, 1), :] = jnp.zeros((1, 128), F32)
        small_ref[pl.ds(216, 1), pl.ds(0, DPROJ)] = jnp.sum(d_last, axis=0, keepdims=True)
        grad_dense_ref[...] = dot_nt(dw_ref[...], d_last, EXACT)
        d_low_ref[...] = d_in_ref[...].astype(BF16)
        for tile in range(TILES - 2):
            value = small_ref[pl.ds(8 * tile, 8), :]
            both = two_parts(value)
            for p in range(4):
                grads_ref[tile, p, pl.ds(CHUNK, 16), :] = both
        for p in range(4):
            grads_ref[TILES - 2, p, pl.ds(CHUNK, 16), :] = two_parts(small_b[p])
            grads_ref[TILES - 1, p, pl.ds(CHUNK, 16), :] = jnp.zeros((16, 128), BF16)

    @pl.when(phase == 0)
    def _():
        lax.fori_loop(0, EXPERTS, forward, 0)

    @pl.when(phase == 1)
    def _():
        head()

    @pl.when(phase == 2)
    def _():
        lax.fori_loop(0, EXPERTS, backward, 0)
        tail()


def model(*operands):
    return pl.pallas_call(
        model_kernel,
        grid=(3,),
        in_specs=[VM] * len(operands),
        out_specs=[VM] * 3,
        out_shape=[
            shape((TILES, 4, SENT, 128), BF16),
            shape((ROWS_LOC, DIN), BF16),
            shape((DENSE, ROWS_LOC), F32),
        ],
        scratch_shapes=[
            pltpu.VMEM((8 * (TILES - 2), 128), F32),
            pltpu.VMEM((4, 8, 128), F32),
            pltpu.VMEM((ROWS_LOC, DIN), F32),
            pltpu.VMEM((EXPERTS, ROWS_LOC, HID), BF16),
            pltpu.VMEM((EXPERTS, ROWS_LOC, HID), F32),
            pltpu.VMEM((EXPERTS, ROWS_LOC, EOUT), F32),
            pltpu.VMEM((TASKS * EXPERTS, ROWS_LOC, EOUT), F32),
            pltpu.VMEM((EXPERTS, ROWS_LOC, EOUT), BF16),
            pltpu.VMEM((ROWS_LOC, TASKS * EXPERTS * EOUT), BF16),
            pltpu.VMEM((ROWS_LOC, TASKS * EXPERTS * EOUT), BF16),
            pltpu.VMEM((ROWS_LOC, TASKS * EOUT), F32),
            pltpu.VMEM((48, DIN), F32),
        ],
        compiler_params=params(56),
        name="model",
    )(*operands)


def spread_kernel(src_ref, hot_ref, d_ref, out_ref, slots, rows, hot_rows):
    lane_from = lax.broadcasted_iota(jnp.int32, (128, 128), 0)
    lane_to = lax.broadcasted_iota(jnp.int32, (128, 128), 1)
    for field in range(FIELDS):
        take = lane_from == EMB * (field % 8) + lane_to % EMB
        copies = dot_nn(d_ref[:, pl.ds(field // 8 * 128, 128)], take.astype(F32).astype(BF16))
        rows[pl.ds(field * ROWS_LOC, ROWS_LOC), :] = copies
    rows[pl.ds(LOOKUPS, 8), :] = jnp.zeros((8, 128), F32)
    group = lane_group(1)

    def clear(step, carry):
        slots[pl.ds(eight(step * SLOTS + COLD), SLOTS - COLD), :] = jnp.zeros(
            (SLOTS - COLD, 128), F32
        )
        return carry

    lax.fori_loop(0, OWNERS // 8, clear, 0)

    def cold(step, carry):
        base = step // 6 * SLOTS + step % 6 * 16
        source = step // 6 * (8 * SLOTS) + step % 6 * 16
        for n in range(16):
            total = rows[pl.ds(src_ref[source + n], 1), :]
            for u in range(1, 8):
                row = rows[pl.ds(src_ref[source + u * SLOTS + n], 1), :]
                total = jnp.where(group == u, row, total)
            slots[pl.ds(base + n, 1), :] = total
        return carry

    def hot(at, carry):
        owner = hot_ref[at]
        for n in range(COLD, CAP):
            row = rows[pl.ds(src_ref[owner * SLOTS + n], 1), :]
            hot_rows[pl.ds(at * (CAP - COLD) + n - COLD, 1), :] = row
        return carry

    lax.fori_loop(0, OWNERS // 8 * 6, cold, 0)
    lax.fori_loop(0, HOT, hot, 0)
    wide_group = lane_group(CAP - COLD)

    def merge(at, carry):
        owner = hot_ref[at]
        place = pl.ds(eight((owner >> 3) * SLOTS + COLD), CAP - COLD)
        new = hot_rows[pl.ds(eight(at * (CAP - COLD)), CAP - COLD), :]
        slots[place, :] = jnp.where(wide_group == (owner & 7), new, slots[place, :])
        return carry

    lax.fori_loop(0, HOT, merge, 0)
    for block in range(32):
        owner, half = block // 2 * 8, block % 2
        turned = slots[pl.ds(block * 128, 128), :].T.astype(BF16)
        for u in range(8):
            out_ref[pl.ds((owner + u) * GROUPS + EMB * half, EMB), :] = turned[
                EMB * u : EMB * u + EMB
            ]


def spread_grads(src, hot, d_inputs):
    return pl.pallas_call(
        spread_kernel,
        in_specs=[SM, SM, VM],
        out_specs=VM,
        out_shape=shape((OWNERS * GROUPS, 128), BF16),
        scratch_shapes=[
            pltpu.VMEM((OWNERS * GROUPS, 128), F32),
            pltpu.VMEM((LOOKUPS + 8, 128), F32),
            pltpu.VMEM((HOT * (CAP - COLD), 128), F32),
        ],
        compiler_params=params(48),
        name="spread_grads",
    )(src, hot, d_inputs)


def scatter_kernel(
    asked_ref, grads_ref, out_ref, rows_v, groups, rows, sem, even, odd, *sums
):
    split_wanted(asked_ref, rows_v, groups, rows, sem)
    at_group = sublane_group()

    def clear(step, carry):
        for total in sums:
            total[pl.ds(eight(step * 512), 512), :] = jnp.zeros((512, 128), F32)
        return carry

    lax.fori_loop(0, PACKED // 512, clear, 0)

    def place(source, found):
        for half in range(2):
            block = grads_ref[pl.ds(eight(source * GROUPS + EMB * half, EMB), EMB), :].astype(F32)
            block = jnp.broadcast_to(block[None], (8, EMB, 128)).reshape(128, 128)
            block = jnp.where(at_group == groups[pl.ds(2 * source + half, 1), :], block, 0.0)
            found[pl.ds(half * 128, 128), :] = block.T

    def add(source, found):
        for n in range(CAP):
            at = pl.ds(rows[2 * source + n // 128, n % 128], 1)
            total = sums[n % SUMS]
            total[at, :] = total[at, :] + found[pl.ds(n, 1), :]

    place(0, even)

    def two_sources(step, carry):
        source = 2 * step
        place(source + 1, odd)
        add(source, even)
        place(jnp.minimum(source + 2, OWNERS - 1), even)
        add(source + 1, odd)
        return carry

    lax.fori_loop(0, OWNERS // 2, two_sources, 0)

    def write(field, carry):
        for part in range(4):
            at = pl.ds(eight(field * 512 + part * 128, 128), 128)
            block = sums[0][at, :]
            for total in sums[1:]:
                block = block + total[at, :]
            block = block.T
            for k in range(8):
                out_ref[field, :, pl.ds(part * 1024 + k * 128, 128)] = block[16 * k : 16 * k + 16]
        return carry

    lax.fori_loop(0, FIELDS, write, 0)


def scatter_add(asked, grads):
    return pl.pallas_call(
        scatter_kernel,
        in_specs=[VM, VM],
        out_specs=VM,
        out_shape=shape((FIELDS, EMB, ROWS_DEV), F32),
        scratch_shapes=split_scratch()
        + [pltpu.VMEM((SLOTS, 128), F32)] * 2
        + [pltpu.VMEM((PACKED + 8, 128), F32)] * SUMS,
        compiler_params=params(58),
        name="scatter_add",
    )(asked, grads)


def sum_kernel(parts_ref, out_ref):
    def add(at, total):
        return total + parts_ref[at].astype(F32)

    total = lax.fori_loop(1, OWNERS, add, parts_ref[0].astype(F32))
    small = two_parts(total[CHUNK : CHUNK + 8] + total[CHUNK + 8 : SENT])
    low = total[0:CHUNK].astype(BF16)
    for at in range(TILES):
        out_ref[at, pl.ds(0, CHUNK), :] = low
        out_ref[at, pl.ds(CHUNK, 16), :] = small


def sum_parts(parts):
    return pl.pallas_call(
        sum_kernel,
        in_specs=[VM],
        out_specs=VM,
        out_shape=shape((TILES, SENT, 128), BF16),
        compiler_params=params(32),
        name="sum_parts",
    )(parts)


def unpack_kernel(
    sums_ref,
    w_in_ref,
    w_out_ref,
    w1_ref,
    b_out_ref,
    gate_ref,
    dense_w_ref,
    dense_b_ref,
    b1_ref,
    w2_ref,
    b2_ref,
    gate_b_ref,
    b_in_ref,
):
    def expert(k, carry):
        rows = [sums_ref[4 * k + at, pl.ds(0, CHUNK), :] for at in range(4)]
        rows = jnp.concatenate(rows, axis=0).astype(F32)
        for block in range(4):
            w_in_ref[k, :, pl.ds(block * 128, 128)] = rows[PART * block : PART * block + PART]
        w_out_ref[k] = rows[4 * PART : 5 * PART]
        return carry

    lax.fori_loop(0, EXPERTS, expert, 0)

    def tile(at):
        return one_of(sums_ref[at, pl.ds(CHUNK, 16), :])

    for at in range(16):
        w1_ref[at // 8, pl.ds(at % 8 * 8, 8), :] = tile(at)
    b_out_ref[...] = tile(16)
    for at in range(8):
        gate_ref[pl.ds(at % 2 * 8, 8), pl.ds(at // 2 * 128, 128)] = tile(17 + at)
    dense_w_ref[pl.ds(0, 8), :] = tile(25)[:, 0:DPROJ]
    dense_w_ref[pl.ds(8, DENSE - 8), :] = tile(26)[0 : DENSE - 8, 0:DPROJ]
    rest = tile(27)
    dense_b_ref[...] = rest[0:1, 0:DPROJ]
    for t in range(TASKS):
        b1_ref[pl.ds(t, 1), :] = rest[1:2, t * THID : t * THID + THID]
        w2_ref[pl.ds(t, 1), :] = rest[2:3, t * THID : t * THID + THID]
    lane = lax.broadcasted_iota(jnp.int32, (1, 128), 1)
    b2_ref[...] = jnp.where(lane == 0, rest[4:5], rest[5:6])[:, 0:TASKS]
    own = lax.broadcasted_iota(jnp.int32, (8, 128), 0) == lax.broadcasted_iota(
        jnp.int32, (8, 128), 1
    )
    for t in range(TASKS):
        value = jnp.sum(jnp.where(own, tile(28 + t), 0.0), axis=0, keepdims=True)
        gate_b_ref[pl.ds(t, 1), :] = value[:, 0:EXPERTS]
    b_in_ref[...] = tile(30)[:, 0:PART]


def unpack(sums):
    return pl.pallas_call(
        unpack_kernel,
        in_specs=[VM],
        out_specs=[VM] * 12,
        out_shape=[
            shape((EXPERTS, PART, DIN), F32),
            shape((EXPERTS, PART, EOUT), F32),
            shape((TASKS, THID, EOUT), F32),
            shape((EXPERTS, EOUT), F32),
            shape((TASKS * EXPERTS, DIN), F32),
            shape((DENSE, DPROJ), F32),
            shape((1, DPROJ), F32),
            shape((TASKS, THID), F32),
            shape((TASKS, THID), F32),
            shape((1, TASKS), F32),
            shape((TASKS, EXPERTS), F32),
            shape((EXPERTS, PART), F32),
        ],
        compiler_params=params(32),
        name="unpack",
    )(sums)


def exchange(value, axes):
    return lax.all_to_all(value, axes, split_axis=0, concat_axis=0, tiled=True)


def body(
    sparse_ids,
    dense_feats,
    labels,
    tables,
    dense_w,
    dense_b,
    w_in,
    b_in,
    w_out,
    b_out,
    gate_w,
    gate_b,
    tower_w1,
    tower_b1,
    tower_w2,
    tower_b2,
):
    weights = jnp.concatenate([w_in.transpose(0, 2, 1), w_out], axis=2)
    bias = jnp.pad(b_in[:, None, :], ((0, 0), (0, 15), (0, DIN + EOUT - PART)))
    weights = lax.all_gather(jnp.concatenate([weights, bias], axis=1), "mp", axis=0)

    ids = sparse_ids.T
    field = lax.broadcasted_iota(jnp.int32, (FIELDS, ROWS_LOC), 0)
    example = lax.broadcasted_iota(jnp.int32, (FIELDS, ROWS_LOC), 1)
    row = ids & (ROWS_DEV - 1)
    packed = field * 512 + (row >> 10) * 128 + (row & 127)
    key = ((ids >> 12) << 14) | (field * ROWS_LOC + example)
    load = (packed << 3) | ((row >> 7) & 7)
    keys, loads = lax.sort((key.reshape(-1), load.reshape(-1)), num_keys=1, is_stable=False)
    requests, sources, hot = route(keys.reshape(-1, 128), loads.reshape(-1, 128))
    asked = exchange(requests, ALL)
    sources = sources.reshape(-1)
    table = pack_tables(tables.transpose(0, 2, 1))
    answer = exchange(look_up(asked, table), ALL)
    feats_t = dense_feats.T
    inputs = embed(sources, hot, ids, answer, feats_t, dense_w, dense_b.reshape(DPROJ, 1))
    task_at = lax.broadcasted_iota(jnp.int32, (TASKS, TASKS * THID), 1) // THID
    task_row = lax.broadcasted_iota(jnp.int32, (TASKS, TASKS * THID), 0)
    w2_bd = jnp.where(task_at == task_row, tower_w2.reshape(1, -1), 0.0)
    grads, d_inputs, grad_dense = model(
        inputs,
        labels.T,
        feats_t,
        dense_w,
        weights,
        b_out.reshape(EXPERTS, 1, EOUT),
        gate_w.transpose(0, 2, 1).reshape(TASKS * EXPERTS, DIN),
        gate_b.reshape(TASKS * EXPERTS, 1),
        tower_w1.transpose(0, 2, 1),
        tower_b1.reshape(1, TASKS * THID),
        w2_bd,
        tower_b2.reshape(TASKS, 1),
    )
    grads = exchange(grads.reshape(OWNERS, SENT, 128), ALL)
    incoming = exchange(spread_grads(sources, hot, d_inputs), ALL)
    sums = exchange(sum_parts(grads), "dp")
    grad_tables = scatter_add(asked, incoming).transpose(0, 2, 1)
    (
        grad_w_in,
        grad_w_out,
        grad_w1,
        grad_b_out,
        grad_gate_w,
        grad_dense_w,
        grad_dense_b,
        grad_b1,
        grad_w2,
        grad_b2,
        grad_gate_b,
        grad_b_in,
    ) = unpack(sums)
    return (
        grad_tables,
        grad_dense_w,
        grad_dense_b.reshape(DPROJ),
        grad_w_in.transpose(0, 2, 1),
        grad_b_in,
        grad_w_out,
        grad_b_out,
        grad_gate_w.reshape(TASKS, EXPERTS, DIN).transpose(0, 2, 1),
        grad_gate_b,
        grad_w1.transpose(0, 2, 1),
        grad_b1,
        grad_w2,
        grad_b2.reshape(TASKS),
        grad_dense.T,
    )


def solution(mesh):
    return jax.shard_map(
        body,
        mesh=mesh,
        in_specs=(
            P(ALL, None),
            P(ALL, None),
            P(ALL, None),
            P(None, ALL, None),
            P(),
            P(),
            P(None, None, "mp"),
            P(None, "mp"),
            P(None, "mp", None),
            P(),
            P(),
            P(),
            P(),
            P(),
            P(),
            P(),
        ),
        out_specs=(
            P(None, ALL, None),
            P(),
            P(),
            P(None, None, "mp"),
            P(None, "mp"),
            P(None, "mp", None),
            P(),
            P(),
            P(),
            P(),
            P(),
            P(),
            P(),
            P(ALL, None),
        ),
        check_vma=False,
    )
```

```python
import functools

import jax
import jax.numpy as jnp
from jax import lax
from jax.experimental import pallas as pl
from jax.experimental.pallas import tpu as pltpu
from jax.sharding import PartitionSpec as P

ALL = ("dp", "mp")
EXACT = lax.Precision.HIGHEST
F32 = jnp.float32
BF16 = jnp.bfloat16

OWNERS = 128
FIELDS = 26
EMB = 16
ROWS_LOC = 512
ROWS_DEV = 4096
LOOKUPS = ROWS_LOC * FIELDS
PACKED = FIELDS * ROWS_DEV // 8
CAP = 208
COLD = 96
HOT = 16
SLOTS = 256
GROUPS = SLOTS // 8
EXPERTS = 8
HID = 256
EOUT = 128
TASKS = 2
THID = 64
DIN = 512
DENSE = 13
DPROJ = 96
CHUNK = 80
TILES = 32
SENT = CHUNK + 16
PART = 64
SUMS = 6

VM = pl.BlockSpec(memory_space=pltpu.VMEM)
SM = pl.BlockSpec(memory_space=pltpu.SMEM)


def params(mib):
    return pltpu.CompilerParams(vmem_limit_bytes=mib * 1024 * 1024)


def shape(dims, dtype):
    return jax.ShapeDtypeStruct(dims, dtype)


def lane_group(rows):
    return lax.broadcasted_iota(jnp.int32, (rows, 128), 1) // EMB


def sublane_group():
    return lax.broadcasted_iota(jnp.int32, (128, 128), 0) // EMB


def eight(index, unit=8):
    return pl.multiple_of(index, unit)


def dot_nt(a, b, precision=None):
    return lax.dot_general(
        a, b, (((1,), (1,)), ((), ())), precision=precision, preferred_element_type=F32
    )


def dot_tn(a, b, precision=None):
    return lax.dot_general(
        a, b, (((0,), (0,)), ((), ())), precision=precision, preferred_element_type=F32
    )


def dot_nn(a, b, precision=None):
    return lax.dot_general(
        a, b, (((1,), (0,)), ((), ())), precision=precision, preferred_element_type=F32
    )


def split3(value):
    high = value.astype(BF16)
    rest = value - high.astype(F32)
    mid = rest.astype(BF16)
    low = (rest - mid.astype(F32)).astype(BF16)
    return high, mid, low


def route_kernel(key_ref, load_ref, req_ref, src_ref, hot_ref, both, cut, starts_v, starts, sem):
    own = (key_ref[...] & 16383) << 17
    both[pl.ds(0, 104), :] = own | load_ref[...]
    both[pl.ds(104, 8), :] = jnp.zeros((8, 128), jnp.int32)
    owner_at = lax.broadcasted_iota(jnp.int32, (128, 128), 0)

    def count(step, total):
        rows = key_ref[pl.ds(eight(step * 8), 8), :] >> 14
        for at in range(8):
            total = total + (rows[at : at + 1, :] < owner_at).astype(jnp.int32)
        return total

    below = lax.fori_loop(0, 13, count, jnp.zeros((128, 128), jnp.int32))
    first = jnp.sum(below.astype(F32).T, axis=0, keepdims=True).astype(jnp.int32)
    starts_v[...] = jnp.broadcast_to(first, (8, 128))
    copy = pltpu.make_async_copy(starts_v, starts, sem)
    copy.start()
    copy.wait()
    for at in range(2 * HOT):
        hot_ref[at] = 0
    lane = lax.broadcasted_iota(jnp.int32, (1, 128), 1)
    unused = (LOOKUPS << 17) | (PACKED * 8)

    def per_owner(owner, hot_count):
        start = starts[0, owner]
        end = jnp.where(owner == OWNERS - 1, LOOKUPS, starts[0, jnp.minimum(owner + 1, 127)])
        row = start >> 7
        off = start & 127
        pieces = [both[pl.ds(row + at, 1), :] for at in range(3)]
        for half in range(2):
            piece = jnp.where(lane >= off, pieces[half], pieces[half + 1])
            piece = pltpu.roll(piece, (128 - off) & 127, 1)
            cut[pl.ds(2 * owner + half, 1), :] = jnp.where(
                lane < end - start - 128 * half, piece, unused
            )
        hot_ref[hot_count] = owner
        return jnp.minimum(hot_count + (end - start > COLD).astype(jnp.int32), 2 * HOT - 1)

    lax.fori_loop(0, OWNERS, per_owner, 0, unroll=8)
    src_ref[...] = cut[...] >> 17
    req_ref[...] = cut[...] & ((1 << 17) - 1)


def route(keys, loads):
    return pl.pallas_call(
        route_kernel,
        in_specs=[VM, VM],
        out_specs=[VM, VM, SM],
        out_shape=[
            shape((2 * OWNERS, 128), jnp.int32),
            shape((2 * OWNERS, 128), jnp.int32),
            shape((2 * HOT,), jnp.int32),
        ],
        scratch_shapes=[
            pltpu.VMEM((112, 128), jnp.int32),
            pltpu.VMEM((2 * OWNERS, 128), jnp.int32),
            pltpu.VMEM((8, 128), jnp.int32),
            pltpu.SMEM((8, 128), jnp.int32),
            pltpu.SemaphoreType.DMA,
        ],
        compiler_params=params(32),
        name="route",
    )(keys, loads)


def pack_kernel(table_ref, out_ref):
    for part in range(4):
        block = jnp.concatenate(
            [table_ref[0, :, pl.ds(part * 1024 + k * 128, 128)] for k in range(8)], axis=0
        )
        out_ref[pl.ds(part * 128, 128), :] = block.T


def pack_tables(tables_t):
    return pl.pallas_call(
        pack_kernel,
        grid=(FIELDS,),
        in_specs=[pl.BlockSpec((1, EMB, ROWS_DEV), lambda f: (f, 0, 0))],
        out_specs=pl.BlockSpec((512, 128), lambda f: (f, 0)),
        out_shape=shape((PACKED + 8, 128), F32),
        compiler_params=params(32),
        name="pack_tables",
    )(tables_t)


def split_wanted(asked_ref, rows_v, groups, rows, sem):
    rows_v[...] = asked_ref[...] >> 3
    copy = pltpu.make_async_copy(rows_v, rows, sem)
    copy.start()
    groups[...] = asked_ref[...] & 7
    copy.wait()


def split_scratch():
    return [
        pltpu.VMEM((2 * OWNERS, 128), jnp.int32),
        pltpu.VMEM((2 * OWNERS, 128), jnp.int32),
        pltpu.SMEM((2 * OWNERS, 128), jnp.int32),
        pltpu.SemaphoreType.DMA,
    ]


def my_index():
    return lax.axis_index("dp") * lax.axis_size("mp") + lax.axis_index("mp")


def place_of(index):
    return (index // 4, index % 4)


def greet_all(me):
    barrier = pltpu.get_barrier_semaphore()

    def greet(step, carry):
        pl.semaphore_signal(
            barrier,
            inc=1,
            device_id=place_of((me + step) % OWNERS),
            device_id_type=pl.DeviceIdType.MESH,
        )
        return carry

    lax.fori_loop(1, OWNERS, greet, 0)
    return barrier


def look_up_kernel(
    asked_ref,
    table_ref,
    out_ref,
    rows_v,
    groups,
    rows,
    sem,
    even,
    odd,
    ready,
    send_sem,
    recv_sem,
    own_sem,
):
    me = my_index()
    barrier = greet_all(me)
    split_wanted(asked_ref, rows_v, groups, rows, sem)
    at_group = sublane_group()

    def gather(source, found):
        for n in range(CAP):
            at = rows[2 * source + n // 128, n % 128]
            found[pl.ds(n, 1), :] = table_ref[pl.ds(at, 1), :]

    def pick(source, found):
        for half in range(2):
            block = found[pl.ds(half * 128, 128), :].T
            block = jnp.where(at_group == groups[pl.ds(2 * source + half, 1), :], block, 0.0)
            block = jnp.sum(block.reshape(8, EMB, 128), axis=0)
            ready[pl.ds(eight(source * GROUPS + EMB * half, EMB), EMB), :] = block.astype(BF16)

    def block_of(ref, index):
        return ref.at[pl.ds(eight(index * GROUPS, GROUPS), GROUPS), :]

    def send(source):
        pltpu.make_async_remote_copy(
            src_ref=block_of(ready, source),
            dst_ref=block_of(out_ref, me),
            send_sem=send_sem,
            recv_sem=recv_sem,
            device_id=place_of(source),
            device_id_type=pl.DeviceIdType.MESH,
        ).start()

    even[...] = jnp.zeros_like(even)
    odd[...] = jnp.zeros_like(odd)
    gather(me, even)
    gather((me + 1) % OWNERS, odd)
    pick(me, even)
    own = pltpu.make_async_copy(block_of(ready, me), block_of(out_ref, me), own_sem)
    own.start()
    pl.semaphore_wait(barrier, OWNERS - 1)

    def two_sources(step, carry):
        first = (me + 2 * step + 1) % OWNERS
        second = (me + 2 * step + 2) % OWNERS
        third = (me + 2 * step + 3) % OWNERS
        gather(second, even)
        pick(first, odd)
        send(first)
        gather(third, odd)
        pick(second, even)
        send(second)
        return carry

    lax.fori_loop(0, OWNERS // 2 - 1, two_sources, 0)
    last = (me + OWNERS - 1) % OWNERS
    pick(last, odd)
    send(last)
    own.wait()
    every = pl.ds(0, (OWNERS - 1) * GROUPS)
    pltpu.make_async_copy(ready.at[every, :], ready.at[every, :], send_sem).wait()
    pltpu.make_async_copy(out_ref.at[every, :], out_ref.at[every, :], recv_sem).wait()


def look_up(asked, table):
    return pl.pallas_call(
        look_up_kernel,
        in_specs=[VM, VM],
        out_specs=VM,
        out_shape=shape((OWNERS * GROUPS, 128), BF16),
        scratch_shapes=split_scratch()
        + [pltpu.VMEM((SLOTS, 128), F32)] * 2
        + [pltpu.VMEM((OWNERS * GROUPS, 128), BF16)]
        + [pltpu.SemaphoreType.DMA] * 3,
        compiler_params=pltpu.CompilerParams(
            vmem_limit_bytes=48 * 1024 * 1024, collective_id=0, has_side_effects=True
        ),
        name="look_up",
    )(asked, table)


def embed_kernel(
    src_ref, hot_ref, ids_ref, answer_ref, feats_ref, dw_ref, db_ref, out_ref, slots, rows, x_t
):
    for block in range(32):
        owner, half = block // 2 * 8, block % 2
        parts = [
            answer_ref[pl.ds((owner + u) * GROUPS + EMB * half, EMB), :] for u in range(8)
        ]
        slots[pl.ds(block * 128, 128), :] = jnp.concatenate(parts, axis=0).astype(F32).T

    def cold(step, carry):
        base = step // 6 * SLOTS + step % 6 * 16
        source = step // 6 * (8 * SLOTS) + step % 6 * 16
        for n in range(16):
            row = slots[pl.ds(base + n, 1), :]
            for u in range(8):
                rows[pl.ds(src_ref[source + u * SLOTS + n], 1), :] = row
        return carry

    def hot(at, carry):
        owner = hot_ref[at]
        base = (owner >> 3) * SLOTS
        for n in range(COLD, CAP):
            rows[pl.ds(src_ref[owner * SLOTS + n], 1), :] = slots[pl.ds(base + n, 1), :]
        return carry

    lax.fori_loop(0, OWNERS // 8 * 6, cold, 0)
    lax.fori_loop(0, HOT, hot, 0)
    at_group = sublane_group()

    def field(f, carry):
        group = (ids_ref[pl.ds(f, 1), :] >> 12) & 7
        for part in range(4):
            block = rows[pl.ds(eight(f * ROWS_LOC + part * 128, 128), 128), :].T
            block = jnp.where(at_group == group[:, part * 128 : part * 128 + 128], block, 0.0)
            block = jnp.sum(block.reshape(8, EMB, 128), axis=0)
            x_t[pl.ds(eight(f * EMB, EMB), EMB), pl.ds(part * 128, 128)] = block
        return carry

    lax.fori_loop(0, FIELDS, field, 0)
    x_t[pl.ds(FIELDS * EMB, DPROJ), :] = dot_tn(dw_ref[...], feats_ref[...], EXACT) + db_ref[...]
    out_ref[...] = x_t[...].T.astype(BF16)


def embed(src, hot, ids, answer, feats_t, dense_w, dense_b):
    return pl.pallas_call(
        embed_kernel,
        in_specs=[SM, SM, VM, VM, VM, VM, VM],
        out_specs=VM,
        out_shape=shape((ROWS_LOC, DIN), BF16),
        scratch_shapes=[
            pltpu.VMEM((OWNERS * GROUPS, 128), F32),
            pltpu.VMEM((LOOKUPS + 8, 128), F32),
            pltpu.VMEM((DIN, ROWS_LOC), F32),
        ],
        compiler_params=params(48),
        name="embed",
    )(src, hot, ids, answer, feats_t, dense_w, dense_b)


C0 = 0.7978845608
C1 = 0.7978845608 * 0.044715


def gelu_both(value):
    square = value * value
    bend = jnp.tanh(value * (C0 + C1 * square))
    half = 0.5 * (1.0 + bend)
    slope = half + 0.5 * value * (1.0 - bend * bend) * (C0 + 3.0 * C1 * square)
    return value * half, slope


def two_parts(value):
    high = value.astype(BF16).astype(F32)
    return jnp.concatenate([high, value - high], axis=0).astype(BF16)


def one_of(parts):
    wide = parts.astype(F32)
    return wide[0:8] + wide[8:16]


def model_kernel(
    x_ref,
    labels_ref,
    feats_ref,
    dw_ref,
    weights_ref,
    b_out_ref,
    gate_w_ref,
    gate_b_ref,
    w1_ref,
    b1_ref,
    w2_ref,
    b2_ref,
    grads_ref,
    d_low_ref,
    grad_dense_ref,
    small_ref,
    small_b,
    d_in_ref,
    hidden,
    slope,
    outs,
    probs,
    d_raw,
    prod_hi,
    prod_lo,
    mix,
    stage,
):
    x = x_ref[...]
    phase = pl.program_id(0)

    def weights_in(k):
        return jnp.concatenate(
            [weights_ref[p, k, pl.ds(0, PART), pl.ds(0, DIN)] for p in range(4)], axis=0
        )

    def weights_out(k):
        return jnp.concatenate(
            [weights_ref[p, k, pl.ds(0, PART), pl.ds(DIN, EOUT)] for p in range(4)], axis=0
        )

    def forward(k, carry):
        bias = [
            weights_ref[p, k, pl.ds(PART, 16), pl.ds(0, 128)].astype(F32)[0:1, 0:PART]
            for p in range(4)
        ]
        pre = dot_nt(x, weights_in(k)) + jnp.concatenate(bias, axis=1)
        act, grad = gelu_both(pre)
        act = act.astype(BF16)
        hidden[k] = act
        slope[k] = grad
        outs[k] = dot_nn(act, weights_out(k)) + b_out_ref[k]
        return carry

    def head():
        gate_parts = jnp.concatenate(split3(gate_w_ref[...]), axis=0)
        stage[...] = dot_nt(gate_parts, x)
        logits = stage[0:16] + stage[16:32] + stage[32:48] + gate_b_ref[...]
        logits = logits.reshape(TASKS, EXPERTS, ROWS_LOC)
        gates = jnp.exp(logits - jnp.max(logits, axis=1, keepdims=True))
        gates = gates / jnp.sum(gates, axis=1, keepdims=True)
        gates_t = gates.reshape(TASKS * EXPERTS, ROWS_LOC)
        gate_stack = jnp.concatenate(split3(gates_t), axis=0)
        row_at = lax.broadcasted_iota(jnp.int32, (48, 128), 0) % 16

        def spread(k, carry):
            ones = (row_at == k).astype(F32).astype(BF16)
            probs[k] = dot_tn(gate_stack, ones)
            return carry

        lax.fori_loop(0, TASKS * EXPERTS, spread, 0)

        for t in range(TASKS):
            def add(k, total):
                return total + probs[t * EXPERTS + k] * outs[k]

            mix[:, pl.ds(t * EOUT, EOUT)] = lax.fori_loop(
                1, EXPERTS, add, probs[t * EXPERTS] * outs[0]
            )
        mixture = mix[...]
        zero = jnp.zeros((THID, EOUT), F32)
        w1_bd = jnp.concatenate(
            [
                jnp.concatenate([w1_ref[0], zero], axis=1),
                jnp.concatenate([zero, w1_ref[1]], axis=1),
            ],
            axis=0,
        )
        upper, upper_slope = gelu_both(dot_nt(mixture, w1_bd, EXACT) + b1_ref[...])
        w2_bd = w2_ref[...]
        logit = dot_nt(w2_bd, upper, EXACT) + b2_ref[...]
        d_logit = jax.nn.sigmoid(logit) - labels_ref[...].astype(F32)
        d_pre1 = dot_tn(d_logit, w2_bd, EXACT) * upper_slope
        grad_w2 = dot_nn(d_logit, upper, EXACT)
        grad_b1 = jnp.sum(d_pre1, axis=0, keepdims=True)
        grad_w1 = dot_tn(d_pre1, mixture, EXACT)
        d_mix = dot_nn(d_pre1, w1_bd, EXACT)
        mix[...] = d_mix

        def back_raw(k, carry):
            d_one = mix[:, pl.ds(0, EOUT)]
            d_two = mix[:, pl.ds(EOUT, EOUT)]
            grad = probs[k] * d_one + probs[EXPERTS + k] * d_two
            small_ref[pl.ds(128 + k, 1), :] = jnp.sum(grad, axis=0, keepdims=True)
            d_raw[k] = grad.astype(BF16)
            value = outs[k]
            for t, d_task in enumerate((d_one, d_two)):
                product = value * d_task
                high = product.astype(BF16)
                at = pl.ds(pl.multiple_of((t * EXPERTS + k) * EOUT, EOUT), EOUT)
                prod_hi[:, at] = high
                prod_lo[:, at] = (product - high.astype(F32)).astype(BF16)
            return carry

        lax.fori_loop(0, EXPERTS, back_raw, 0)

        wide = TASKS * EXPERTS * EOUT
        column_gate = lax.broadcasted_iota(jnp.int32, (16, wide), 1) // EOUT
        own_gate = lax.broadcasted_iota(jnp.int32, (16, wide), 0)
        ones = (column_gate == own_gate).astype(F32).astype(BF16)
        stage[0:16] = dot_nt(ones, prod_hi[...])
        stage[16:32] = dot_nt(ones, prod_lo[...])
        d_gates = stage[0:16] + stage[16:32]
        d_gates = d_gates.reshape(TASKS, EXPERTS, ROWS_LOC)
        mean = jnp.sum(d_gates * gates, axis=1, keepdims=True)
        d_logits = (gates * (d_gates - mean)).reshape(16, ROWS_LOC)
        d_parts = jnp.concatenate(split3(d_logits), axis=0)
        stage[...] = dot_nn(d_parts, x)
        grad_gate = stage[0:16] + stage[16:32] + stage[32:48]
        d_in_ref[...] = dot_tn(d_logits, gate_w_ref[...], EXACT)
        small_ref[pl.ds(0, THID), :] = grad_w1[0:THID, 0:EOUT]
        small_ref[pl.ds(THID, THID), :] = grad_w1[THID : 2 * THID, EOUT : 2 * EOUT]
        for tile in range(4):
            small_ref[pl.ds(136 + 16 * tile, 16), :] = grad_gate[:, tile * 128 : tile * 128 + 128]
        small_ref[pl.ds(217, 1), :] = grad_b1
        lane = lax.broadcasted_iota(jnp.int32, (1, 128), 1)
        small_ref[pl.ds(218, 1), :] = jnp.where(lane < THID, grad_w2[0:1], grad_w2[1:2])
        small_ref[pl.ds(219, 1), :] = jnp.zeros((1, 128), F32)
        small_b[...] = jnp.zeros_like(small_b)
        small_ref[pl.ds(220, 2), :] = jnp.broadcast_to(
            jnp.sum(d_logit, axis=1, keepdims=True), (2, 128)
        )
        small_ref[pl.ds(222, 2), :] = jnp.zeros((2, 128), F32)
        small_ref[pl.ds(224, 16), :] = jnp.broadcast_to(
            jnp.sum(d_logits, axis=1, keepdims=True), (16, 128)
        )

    def backward(k, carry):
        d_out = d_raw[k]
        grad_out = dot_tn(hidden[k], d_out).astype(BF16)
        d_pre = (dot_nt(d_out, weights_out(k)) * slope[k]).astype(BF16)
        bias = jnp.sum(d_pre.astype(F32), axis=0, keepdims=True)
        for p in range(4):
            small_b[p, pl.ds(k, 1), pl.ds(0, PART)] = bias[:, PART * p : PART * p + PART]
        grad_in = dot_tn(d_pre, x).astype(BF16)
        for part in range(4):
            for block in range(5):
                for piece in range(4):
                    at = block * 64 + piece * 16
                    rows = slice(part * 64 + piece * 16, part * 64 + piece * 16 + 16)
                    if block < 4:
                        value = grad_in[rows, block * 128 : block * 128 + 128]
                    else:
                        value = grad_out[rows, :]
                    grads_ref[4 * k + at // CHUNK, part, pl.ds(at % CHUNK, 16), :] = value
        d_in_ref[...] += dot_nn(d_pre, weights_in(k))
        return carry

    def tail():
        d_last = d_in_ref[:, pl.ds(DIN - DPROJ, DPROJ)]
        small_ref[pl.ds(200, 16), :] = jnp.zeros((16, 128), F32)
        small_ref[pl.ds(200, DENSE), pl.ds(0, DPROJ)] = dot_nn(feats_ref[...], d_last, EXACT)
        small_ref[pl.ds(216, 1), :] = jnp.zeros((1, 128), F32)
        small_ref[pl.ds(216, 1), pl.ds(0, DPROJ)] = jnp.sum(d_last, axis=0, keepdims=True)
        grad_dense_ref[...] = dot_nt(dw_ref[...], d_last, EXACT)
        d_low_ref[...] = d_in_ref[...].astype(BF16)
        for tile in range(TILES - 2):
            value = small_ref[pl.ds(8 * tile, 8), :]
            both = two_parts(value)
            for p in range(4):
                grads_ref[tile, p, pl.ds(CHUNK, 16), :] = both
        for p in range(4):
            grads_ref[TILES - 2, p, pl.ds(CHUNK, 16), :] = two_parts(small_b[p])
            grads_ref[TILES - 1, p, pl.ds(CHUNK, 16), :] = jnp.zeros((16, 128), BF16)

    @pl.when(phase == 0)
    def _():
        lax.fori_loop(0, EXPERTS, forward, 0)

    @pl.when(phase == 1)
    def _():
        head()

    @pl.when(phase == 2)
    def _():
        lax.fori_loop(0, EXPERTS, backward, 0)
        tail()


def model(*operands):
    return pl.pallas_call(
        model_kernel,
        grid=(3,),
        in_specs=[VM] * len(operands),
        out_specs=[VM] * 3,
        out_shape=[
            shape((TILES, 4, SENT, 128), BF16),
            shape((ROWS_LOC, DIN), BF16),
            shape((DENSE, ROWS_LOC), F32),
        ],
        scratch_shapes=[
            pltpu.VMEM((8 * (TILES - 2), 128), F32),
            pltpu.VMEM((4, 8, 128), F32),
            pltpu.VMEM((ROWS_LOC, DIN), F32),
            pltpu.VMEM((EXPERTS, ROWS_LOC, HID), BF16),
            pltpu.VMEM((EXPERTS, ROWS_LOC, HID), F32),
            pltpu.VMEM((EXPERTS, ROWS_LOC, EOUT), F32),
            pltpu.VMEM((TASKS * EXPERTS, ROWS_LOC, EOUT), F32),
            pltpu.VMEM((EXPERTS, ROWS_LOC, EOUT), BF16),
            pltpu.VMEM((ROWS_LOC, TASKS * EXPERTS * EOUT), BF16),
            pltpu.VMEM((ROWS_LOC, TASKS * EXPERTS * EOUT), BF16),
            pltpu.VMEM((ROWS_LOC, TASKS * EOUT), F32),
            pltpu.VMEM((48, DIN), F32),
        ],
        compiler_params=params(56),
        name="model",
    )(*operands)


def spread_kernel(src_ref, hot_ref, d_ref, out_ref, slots, rows, hot_rows):
    lane_from = lax.broadcasted_iota(jnp.int32, (128, 128), 0)
    lane_to = lax.broadcasted_iota(jnp.int32, (128, 128), 1)
    for field in range(FIELDS):
        take = lane_from == EMB * (field % 8) + lane_to % EMB
        copies = dot_nn(d_ref[:, pl.ds(field // 8 * 128, 128)], take.astype(F32).astype(BF16))
        rows[pl.ds(field * ROWS_LOC, ROWS_LOC), :] = copies
    rows[pl.ds(LOOKUPS, 8), :] = jnp.zeros((8, 128), F32)
    group = lane_group(1)

    def clear(step, carry):
        slots[pl.ds(eight(step * SLOTS + COLD), SLOTS - COLD), :] = jnp.zeros(
            (SLOTS - COLD, 128), F32
        )
        return carry

    lax.fori_loop(0, OWNERS // 8, clear, 0)

    def cold(step, carry):
        base = step // 6 * SLOTS + step % 6 * 16
        source = step // 6 * (8 * SLOTS) + step % 6 * 16
        for n in range(16):
            total = rows[pl.ds(src_ref[source + n], 1), :]
            for u in range(1, 8):
                row = rows[pl.ds(src_ref[source + u * SLOTS + n], 1), :]
                total = jnp.where(group == u, row, total)
            slots[pl.ds(base + n, 1), :] = total
        return carry

    def hot(at, carry):
        owner = hot_ref[at]
        for n in range(COLD, CAP):
            row = rows[pl.ds(src_ref[owner * SLOTS + n], 1), :]
            hot_rows[pl.ds(at * (CAP - COLD) + n - COLD, 1), :] = row
        return carry

    lax.fori_loop(0, OWNERS // 8 * 6, cold, 0)
    lax.fori_loop(0, HOT, hot, 0)
    wide_group = lane_group(CAP - COLD)

    def merge(at, carry):
        owner = hot_ref[at]
        place = pl.ds(eight((owner >> 3) * SLOTS + COLD), CAP - COLD)
        new = hot_rows[pl.ds(eight(at * (CAP - COLD)), CAP - COLD), :]
        slots[place, :] = jnp.where(wide_group == (owner & 7), new, slots[place, :])
        return carry

    lax.fori_loop(0, HOT, merge, 0)
    for block in range(32):
        owner, half = block // 2 * 8, block % 2
        turned = slots[pl.ds(block * 128, 128), :].T.astype(BF16)
        for u in range(8):
            out_ref[pl.ds((owner + u) * GROUPS + EMB * half, EMB), :] = turned[
                EMB * u : EMB * u + EMB
            ]


def spread_grads(src, hot, d_inputs):
    return pl.pallas_call(
        spread_kernel,
        in_specs=[SM, SM, VM],
        out_specs=VM,
        out_shape=shape((OWNERS * GROUPS, 128), BF16),
        scratch_shapes=[
            pltpu.VMEM((OWNERS * GROUPS, 128), F32),
            pltpu.VMEM((LOOKUPS + 8, 128), F32),
            pltpu.VMEM((HOT * (CAP - COLD), 128), F32),
        ],
        compiler_params=params(48),
        name="spread_grads",
    )(src, hot, d_inputs)


def scatter_kernel(
    asked_ref, grads_ref, out_ref, rows_v, groups, rows, sem, even, odd, *sums
):
    split_wanted(asked_ref, rows_v, groups, rows, sem)
    at_group = sublane_group()

    def clear(step, carry):
        for total in sums:
            total[pl.ds(eight(step * 512), 512), :] = jnp.zeros((512, 128), F32)
        return carry

    lax.fori_loop(0, PACKED // 512, clear, 0)

    def place(source, found):
        for half in range(2):
            block = grads_ref[pl.ds(eight(source * GROUPS + EMB * half, EMB), EMB), :].astype(F32)
            block = jnp.broadcast_to(block[None], (8, EMB, 128)).reshape(128, 128)
            block = jnp.where(at_group == groups[pl.ds(2 * source + half, 1), :], block, 0.0)
            found[pl.ds(half * 128, 128), :] = block.T

    def add(source, found):
        for n in range(CAP):
            at = pl.ds(rows[2 * source + n // 128, n % 128], 1)
            total = sums[n % SUMS]
            total[at, :] = total[at, :] + found[pl.ds(n, 1), :]

    place(0, even)

    def two_sources(step, carry):
        source = 2 * step
        place(source + 1, odd)
        add(source, even)
        place(jnp.minimum(source + 2, OWNERS - 1), even)
        add(source + 1, odd)
        return carry

    lax.fori_loop(0, OWNERS // 2, two_sources, 0)

    def write(field, carry):
        for part in range(4):
            at = pl.ds(eight(field * 512 + part * 128, 128), 128)
            block = sums[0][at, :]
            for total in sums[1:]:
                block = block + total[at, :]
            block = block.T
            for k in range(8):
                out_ref[field, :, pl.ds(part * 1024 + k * 128, 128)] = block[16 * k : 16 * k + 16]
        return carry

    lax.fori_loop(0, FIELDS, write, 0)


def scatter_add(asked, grads):
    return pl.pallas_call(
        scatter_kernel,
        in_specs=[VM, VM],
        out_specs=VM,
        out_shape=shape((FIELDS, EMB, ROWS_DEV), F32),
        scratch_shapes=split_scratch()
        + [pltpu.VMEM((SLOTS, 128), F32)] * 2
        + [pltpu.VMEM((PACKED + 8, 128), F32)] * SUMS,
        compiler_params=params(58),
        name="scatter_add",
    )(asked, grads)


def sum_kernel(parts_ref, out_ref):
    def add(at, total):
        return total + parts_ref[at].astype(F32)

    total = lax.fori_loop(1, OWNERS, add, parts_ref[0].astype(F32))
    small = two_parts(total[CHUNK : CHUNK + 8] + total[CHUNK + 8 : SENT])
    low = total[0:CHUNK].astype(BF16)
    for at in range(TILES):
        out_ref[at, pl.ds(0, CHUNK), :] = low
        out_ref[at, pl.ds(CHUNK, 16), :] = small


def sum_parts(parts):
    return pl.pallas_call(
        sum_kernel,
        in_specs=[VM],
        out_specs=VM,
        out_shape=shape((TILES, SENT, 128), BF16),
        compiler_params=params(32),
        name="sum_parts",
    )(parts)


def unpack_kernel(
    sums_ref,
    w_in_ref,
    w_out_ref,
    w1_ref,
    b_out_ref,
    gate_ref,
    dense_w_ref,
    dense_b_ref,
    b1_ref,
    w2_ref,
    b2_ref,
    gate_b_ref,
    b_in_ref,
):
    def expert(k, carry):
        rows = [sums_ref[4 * k + at, pl.ds(0, CHUNK), :] for at in range(4)]
        rows = jnp.concatenate(rows, axis=0).astype(F32)
        for block in range(4):
            w_in_ref[k, :, pl.ds(block * 128, 128)] = rows[PART * block : PART * block + PART]
        w_out_ref[k] = rows[4 * PART : 5 * PART]
        return carry

    lax.fori_loop(0, EXPERTS, expert, 0)

    def tile(at):
        return one_of(sums_ref[at, pl.ds(CHUNK, 16), :])

    for at in range(16):
        w1_ref[at // 8, pl.ds(at % 8 * 8, 8), :] = tile(at)
    b_out_ref[...] = tile(16)
    for at in range(8):
        gate_ref[pl.ds(at % 2 * 8, 8), pl.ds(at // 2 * 128, 128)] = tile(17 + at)
    dense_w_ref[pl.ds(0, 8), :] = tile(25)[:, 0:DPROJ]
    dense_w_ref[pl.ds(8, DENSE - 8), :] = tile(26)[0 : DENSE - 8, 0:DPROJ]
    rest = tile(27)
    dense_b_ref[...] = rest[0:1, 0:DPROJ]
    for t in range(TASKS):
        b1_ref[pl.ds(t, 1), :] = rest[1:2, t * THID : t * THID + THID]
        w2_ref[pl.ds(t, 1), :] = rest[2:3, t * THID : t * THID + THID]
    lane = lax.broadcasted_iota(jnp.int32, (1, 128), 1)
    b2_ref[...] = jnp.where(lane == 0, rest[4:5], rest[5:6])[:, 0:TASKS]
    own = lax.broadcasted_iota(jnp.int32, (8, 128), 0) == lax.broadcasted_iota(
        jnp.int32, (8, 128), 1
    )
    for t in range(TASKS):
        value = jnp.sum(jnp.where(own, tile(28 + t), 0.0), axis=0, keepdims=True)
        gate_b_ref[pl.ds(t, 1), :] = value[:, 0:EXPERTS]
    b_in_ref[...] = tile(30)[:, 0:PART]


def unpack(sums):
    return pl.pallas_call(
        unpack_kernel,
        in_specs=[VM],
        out_specs=[VM] * 12,
        out_shape=[
            shape((EXPERTS, PART, DIN), F32),
            shape((EXPERTS, PART, EOUT), F32),
            shape((TASKS, THID, EOUT), F32),
            shape((EXPERTS, EOUT), F32),
            shape((TASKS * EXPERTS, DIN), F32),
            shape((DENSE, DPROJ), F32),
            shape((1, DPROJ), F32),
            shape((TASKS, THID), F32),
            shape((TASKS, THID), F32),
            shape((1, TASKS), F32),
            shape((TASKS, EXPERTS), F32),
            shape((EXPERTS, PART), F32),
        ],
        compiler_params=params(32),
        name="unpack",
    )(sums)


def exchange(value, axes):
    return lax.all_to_all(value, axes, split_axis=0, concat_axis=0, tiled=True)


def body(
    sparse_ids,
    dense_feats,
    labels,
    tables,
    dense_w,
    dense_b,
    w_in,
    b_in,
    w_out,
    b_out,
    gate_w,
    gate_b,
    tower_w1,
    tower_b1,
    tower_w2,
    tower_b2,
):
    weights = jnp.concatenate([w_in.transpose(0, 2, 1), w_out], axis=2)
    bias = jnp.pad(b_in[:, None, :], ((0, 0), (0, 15), (0, DIN + EOUT - PART)))
    weights = lax.all_gather(jnp.concatenate([weights, bias], axis=1), "mp", axis=0)

    ids = sparse_ids.T
    field = lax.broadcasted_iota(jnp.int32, (FIELDS, ROWS_LOC), 0)
    example = lax.broadcasted_iota(jnp.int32, (FIELDS, ROWS_LOC), 1)
    row = ids & (ROWS_DEV - 1)
    packed = field * 512 + (row >> 10) * 128 + (row & 127)
    key = ((ids >> 12) << 14) | (field * ROWS_LOC + example)
    load = (packed << 3) | ((row >> 7) & 7)
    keys, loads = lax.sort((key.reshape(-1), load.reshape(-1)), num_keys=1, is_stable=False)
    requests, sources, hot = route(keys.reshape(-1, 128), loads.reshape(-1, 128))
    asked = exchange(requests, ALL)
    sources = sources.reshape(-1)
    table = pack_tables(tables.transpose(0, 2, 1))
    answer = look_up(asked, table)
    feats_t = dense_feats.T
    inputs = embed(sources, hot, ids, answer, feats_t, dense_w, dense_b.reshape(DPROJ, 1))
    task_at = lax.broadcasted_iota(jnp.int32, (TASKS, TASKS * THID), 1) // THID
    task_row = lax.broadcasted_iota(jnp.int32, (TASKS, TASKS * THID), 0)
    w2_bd = jnp.where(task_at == task_row, tower_w2.reshape(1, -1), 0.0)
    grads, d_inputs, grad_dense = model(
        inputs,
        labels.T,
        feats_t,
        dense_w,
        weights,
        b_out.reshape(EXPERTS, 1, EOUT),
        gate_w.transpose(0, 2, 1).reshape(TASKS * EXPERTS, DIN),
        gate_b.reshape(TASKS * EXPERTS, 1),
        tower_w1.transpose(0, 2, 1),
        tower_b1.reshape(1, TASKS * THID),
        w2_bd,
        tower_b2.reshape(TASKS, 1),
    )
    grads = exchange(grads.reshape(OWNERS, SENT, 128), ALL)
    incoming = exchange(spread_grads(sources, hot, d_inputs), ALL)
    sums = exchange(sum_parts(grads), "dp")
    grad_tables = scatter_add(asked, incoming).transpose(0, 2, 1)
    (
        grad_w_in,
        grad_w_out,
        grad_w1,
        grad_b_out,
        grad_gate_w,
        grad_dense_w,
        grad_dense_b,
        grad_b1,
        grad_w2,
        grad_b2,
        grad_gate_b,
        grad_b_in,
    ) = unpack(sums)
    return (
        grad_tables,
        grad_dense_w,
        grad_dense_b.reshape(DPROJ),
        grad_w_in.transpose(0, 2, 1),
        grad_b_in,
        grad_w_out,
        grad_b_out,
        grad_gate_w.reshape(TASKS, EXPERTS, DIN).transpose(0, 2, 1),
        grad_gate_b,
        grad_w1.transpose(0, 2, 1),
        grad_b1,
        grad_w2,
        grad_b2.reshape(TASKS),
        grad_dense.T,
    )


def solution(mesh):
    return jax.shard_map(
        body,
        mesh=mesh,
        in_specs=(
            P(ALL, None),
            P(ALL, None),
            P(ALL, None),
            P(None, ALL, None),
            P(),
            P(),
            P(None, None, "mp"),
            P(None, "mp"),
            P(None, "mp", None),
            P(),
            P(),
            P(),
            P(),
            P(),
            P(),
            P(),
        ),
        out_specs=(
            P(None, ALL, None),
            P(),
            P(),
            P(None, None, "mp"),
            P(None, "mp"),
            P(None, "mp", None),
            P(),
            P(),
            P(),
            P(),
            P(),
            P(),
            P(),
            P(ALL, None),
        ),
        check_vma=False,
    )
```

```python
import functools

import jax
import jax.numpy as jnp
from jax import lax
from jax.experimental import pallas as pl
from jax.experimental.pallas import tpu as pltpu
from jax.sharding import PartitionSpec as P

ALL = ("dp", "mp")
EXACT = lax.Precision.HIGHEST
F32 = jnp.float32
BF16 = jnp.bfloat16

OWNERS = 128
FIELDS = 26
EMB = 16
ROWS_LOC = 512
ROWS_DEV = 4096
LOOKUPS = ROWS_LOC * FIELDS
PACKED = FIELDS * ROWS_DEV // 8
CAP = 208
COLD = 96
HOT = 16
SLOTS = 256
GROUPS = SLOTS // 8
EXPERTS = 8
HID = 256
EOUT = 128
TASKS = 2
THID = 64
DIN = 512
DENSE = 13
DPROJ = 96
CHUNK = 80
TILES = 32
CHIPS = OWNERS // 2
PART = 64
SUMS = 6

VM = pl.BlockSpec(memory_space=pltpu.VMEM)
SM = pl.BlockSpec(memory_space=pltpu.SMEM)


def params(mib):
    return pltpu.CompilerParams(vmem_limit_bytes=mib * 1024 * 1024)


def shape(dims, dtype):
    return jax.ShapeDtypeStruct(dims, dtype)


def lane_group(rows):
    return lax.broadcasted_iota(jnp.int32, (rows, 128), 1) // EMB


def sublane_group():
    return lax.broadcasted_iota(jnp.int32, (128, 128), 0) // EMB


def eight(index, unit=8):
    return pl.multiple_of(index, unit)


def dot_nt(a, b, precision=None):
    return lax.dot_general(
        a, b, (((1,), (1,)), ((), ())), precision=precision, preferred_element_type=F32
    )


def dot_tn(a, b, precision=None):
    return lax.dot_general(
        a, b, (((0,), (0,)), ((), ())), precision=precision, preferred_element_type=F32
    )


def dot_nn(a, b, precision=None):
    return lax.dot_general(
        a, b, (((1,), (0,)), ((), ())), precision=precision, preferred_element_type=F32
    )


def split3(value):
    high = value.astype(BF16)
    rest = value - high.astype(F32)
    mid = rest.astype(BF16)
    low = (rest - mid.astype(F32)).astype(BF16)
    return high, mid, low


def my_index():
    return lax.axis_index("dp") * lax.axis_size("mp") + lax.axis_index("mp")


def place_of(index):
    return (index // 4, index % 4)


def greet_all(me):
    barrier = pltpu.get_barrier_semaphore()

    def greet(step, carry):
        pl.semaphore_signal(
            barrier,
            inc=1,
            device_id=place_of((me + step) % OWNERS),
            device_id_type=pl.DeviceIdType.MESH,
        )
        return carry

    lax.fori_loop(1, OWNERS, greet, 0)
    return barrier


def block_of(ref, index):
    return ref.at[pl.ds(eight(index * GROUPS, GROUPS), GROUPS), :]


def send_block(ready, landing, me, dest, send_sem, recv_sem):
    pltpu.make_async_remote_copy(
        src_ref=block_of(ready, dest),
        dst_ref=block_of(landing, me),
        send_sem=send_sem,
        recv_sem=recv_sem,
        device_id=place_of(dest),
        device_id_type=pl.DeviceIdType.MESH,
    ).start()


def wait_blocks(ready, landing, send_sem, recv_sem):
    every = pl.ds(0, (OWNERS - 1) * GROUPS)
    pltpu.make_async_copy(ready.at[every, :], ready.at[every, :], send_sem).wait()
    pltpu.make_async_copy(landing.at[every, :], landing.at[every, :], recv_sem).wait()


def remote_params(mib, identity):
    return pltpu.CompilerParams(
        vmem_limit_bytes=mib * 1024 * 1024, collective_id=identity, has_side_effects=True
    )


def route_kernel(
    key_ref,
    load_ref,
    req_ref,
    src_ref,
    hot_src_ref,
    hot_ref,
    hot_at_ref,
    both,
    cut,
    starts_v,
    starts,
    sem,
):
    own = (key_ref[...] & 16383) << 17
    both[pl.ds(0, 104), :] = own | load_ref[...]
    both[pl.ds(104, 8), :] = jnp.zeros((8, 128), jnp.int32)
    owner_at = lax.broadcasted_iota(jnp.int32, (128, 128), 0)

    def count(step, total):
        rows = key_ref[pl.ds(eight(step * 8), 8), :] >> 14
        for at in range(8):
            total = total + (rows[at : at + 1, :] < owner_at).astype(jnp.int32)
        return total

    below = lax.fori_loop(0, 13, count, jnp.zeros((128, 128), jnp.int32))
    first = jnp.sum(below.astype(F32).T, axis=0, keepdims=True).astype(jnp.int32)
    starts_v[...] = jnp.broadcast_to(first, (8, 128))
    copy = pltpu.make_async_copy(starts_v, starts, sem)
    copy.start()
    copy.wait()
    for at in range(2 * HOT):
        hot_ref[at] = 0
    lane = lax.broadcasted_iota(jnp.int32, (1, 128), 1)
    unused = (LOOKUPS << 17) | (PACKED * 8)

    def per_owner(owner, hot_count):
        start = starts[0, owner]
        end = jnp.where(owner == OWNERS - 1, LOOKUPS, starts[0, jnp.minimum(owner + 1, 127)])
        row = start >> 7
        off = start & 127
        pieces = [both[pl.ds(row + at, 1), :] for at in range(3)]
        for half in range(2):
            piece = jnp.where(lane >= off, pieces[half], pieces[half + 1])
            piece = pltpu.roll(piece, (128 - off) & 127, 1)
            piece = jnp.where(lane < end - start - 128 * half, piece, unused)
            cut[pl.ds(2 * owner + half, 1), :] = piece
            hot_src_ref[pl.ds(2 * hot_count + half, 1), :] = piece >> 17
        is_hot = end - start > COLD
        hot_ref[hot_count] = owner
        hot_at_ref[owner] = jnp.where(is_hot & (hot_count < HOT), hot_count, HOT)
        return jnp.minimum(hot_count + is_hot.astype(jnp.int32), 2 * HOT - 1)

    lax.fori_loop(0, OWNERS, per_owner, 0, unroll=8)
    src_ref[...] = cut[...] >> 17
    req_ref[...] = (cut[...] & ((1 << 17) - 1)).reshape(OWNERS, 2, 128)


def route(keys, loads):
    return pl.pallas_call(
        route_kernel,
        in_specs=[VM, VM],
        out_specs=[VM, VM, VM, SM, SM],
        out_shape=[
            shape((OWNERS, 2, 128), jnp.int32),
            shape((2 * OWNERS, 128), jnp.int32),
            shape((4 * HOT, 128), jnp.int32),
            shape((2 * HOT,), jnp.int32),
            shape((OWNERS,), jnp.int32),
        ],
        scratch_shapes=[
            pltpu.VMEM((112, 128), jnp.int32),
            pltpu.VMEM((2 * OWNERS, 128), jnp.int32),
            pltpu.VMEM((8, 128), jnp.int32),
            pltpu.SMEM((8, 128), jnp.int32),
            pltpu.SemaphoreType.DMA,
        ],
        compiler_params=params(32),
        name="route",
    )(keys, loads)


def split_wanted(asked_ref, rows_v, groups, rows, sem):
    rows_v[...] = asked_ref[...] >> 3
    copy = pltpu.make_async_copy(rows_v, rows, sem)
    copy.start()
    groups[...] = asked_ref[...] & 7
    copy.wait()


def split_scratch():
    return [
        pltpu.VMEM((OWNERS, 2, 128), jnp.int32),
        pltpu.VMEM((OWNERS, 2, 128), jnp.int32),
        pltpu.SMEM((OWNERS, 2, 128), jnp.int32),
        pltpu.SemaphoreType.DMA,
    ]


def look_up_kernel(
    wanted_ref,
    tables_ref,
    out_ref,
    asked_ref,
    fields,
    table,
    rows_v,
    groups,
    rows,
    sem,
    even,
    odd,
    ready,
    field_sem,
    ask_send,
    ask_recv,
    send_sem,
    recv_sem,
    own_sem,
):
    me = my_index()

    def field_copy(field):
        return pltpu.make_async_copy(
            tables_ref.at[field], fields.at[field], field_sem.at[field]
        )

    def start_field(field, carry):
        field_copy(field).start()
        return carry

    lax.fori_loop(0, FIELDS, start_field, 0)
    barrier = greet_all(me)

    def pack(field, carry):
        field_copy(field).wait()
        for part in range(4):
            block = jnp.concatenate(
                [fields[field, :, pl.ds(part * 1024 + k * 128, 128)] for k in range(8)], axis=0
            )
            table[pl.ds(eight(field * 512 + part * 128, 128), 128), :] = block.T
        return carry

    lax.fori_loop(0, 8, pack, 0)
    table[pl.ds(PACKED, 8), :] = jnp.zeros((8, 128), F32)
    asked_ref[me] = wanted_ref[me]
    pl.semaphore_wait(barrier, OWNERS - 1)

    def ask(step, carry):
        owner = (me + step) % OWNERS
        pltpu.make_async_remote_copy(
            src_ref=wanted_ref.at[owner],
            dst_ref=asked_ref.at[me],
            send_sem=ask_send,
            recv_sem=ask_recv,
            device_id=place_of(owner),
            device_id_type=pl.DeviceIdType.MESH,
        ).start()
        return carry

    lax.fori_loop(1, OWNERS, ask, 0)
    lax.fori_loop(8, FIELDS, pack, 0)
    others = pl.ds(0, OWNERS - 1)
    pltpu.make_async_copy(asked_ref.at[others], asked_ref.at[others], ask_recv).wait()
    split_wanted(asked_ref, rows_v, groups, rows, sem)
    at_group = sublane_group()

    def gather(source, found):
        for n in range(CAP):
            at = rows[source, n // 128, n % 128]
            found[pl.ds(n, 1), :] = table[pl.ds(at, 1), :]

    def pick(source, found):
        for half in range(2):
            block = found[pl.ds(half * 128, 128), :].T
            block = jnp.where(at_group == groups[source, pl.ds(half, 1), :], block, 0.0)
            block = jnp.sum(block.reshape(8, EMB, 128), axis=0)
            ready[pl.ds(eight(source * GROUPS + EMB * half, EMB), EMB), :] = block.astype(BF16)

    def send(source):
        send_block(ready, out_ref, me, source, send_sem, recv_sem)

    even[...] = jnp.zeros_like(even)
    odd[...] = jnp.zeros_like(odd)
    gather(me, even)
    gather((me + 1) % OWNERS, odd)
    pick(me, even)
    own = pltpu.make_async_copy(block_of(ready, me), block_of(out_ref, me), own_sem)
    own.start()

    def two_sources(step, carry):
        first = (me + 2 * step + 1) % OWNERS
        second = (me + 2 * step + 2) % OWNERS
        third = (me + 2 * step + 3) % OWNERS
        gather(second, even)
        pick(first, odd)
        send(first)
        gather(third, odd)
        pick(second, even)
        send(second)
        return carry

    lax.fori_loop(0, OWNERS // 2 - 1, two_sources, 0)
    last = (me + OWNERS - 1) % OWNERS
    pick(last, odd)
    send(last)
    own.wait()
    pltpu.make_async_copy(wanted_ref.at[others], wanted_ref.at[others], ask_send).wait()
    wait_blocks(ready, out_ref, send_sem, recv_sem)


def look_up(wanted, tables_t):
    return pl.pallas_call(
        look_up_kernel,
        in_specs=[VM, pl.BlockSpec(memory_space=pl.ANY)],
        out_specs=[VM, VM],
        out_shape=[
            shape((OWNERS * GROUPS, 128), BF16),
            shape((OWNERS, 2, 128), jnp.int32),
        ],
        scratch_shapes=[
            pltpu.VMEM((FIELDS, EMB, ROWS_DEV), F32),
            pltpu.VMEM((PACKED + 8, 128), F32),
        ]
        + split_scratch()
        + [pltpu.VMEM((SLOTS, 128), F32)] * 2
        + [pltpu.VMEM((OWNERS * GROUPS, 128), BF16)]
        + [pltpu.SemaphoreType.DMA((FIELDS,))]
        + [pltpu.SemaphoreType.DMA] * 5,
        compiler_params=remote_params(48, 0),
        name="look_up",
    )(wanted, tables_t)


def embed_kernel(
    src_ref, hot_ref, ids_ref, answer_ref, feats_ref, dw_ref, db_ref, out_ref, slots, rows, x_t
):
    for block in range(32):
        owner, half = block // 2 * 8, block % 2
        parts = [
            answer_ref[pl.ds((owner + u) * GROUPS + EMB * half, EMB), :] for u in range(8)
        ]
        slots[pl.ds(block * 128, 128), :] = jnp.concatenate(parts, axis=0).astype(F32).T

    def cold(step, carry):
        base = step // 6 * SLOTS + step % 6 * 16
        source = step // 6 * (8 * SLOTS) + step % 6 * 16
        for n in range(16):
            row = slots[pl.ds(base + n, 1), :]
            for u in range(8):
                rows[pl.ds(src_ref[source + u * SLOTS + n], 1), :] = row
        return carry

    def hot(at, carry):
        owner = hot_ref[at]
        base = (owner >> 3) * SLOTS
        for n in range(COLD, CAP):
            rows[pl.ds(src_ref[owner * SLOTS + n], 1), :] = slots[pl.ds(base + n, 1), :]
        return carry

    lax.fori_loop(0, OWNERS // 8 * 6, cold, 0)
    lax.fori_loop(0, HOT, hot, 0)
    at_group = sublane_group()

    def field(f, carry):
        group = (ids_ref[pl.ds(f, 1), :] >> 12) & 7
        for part in range(4):
            block = rows[pl.ds(eight(f * ROWS_LOC + part * 128, 128), 128), :].T
            block = jnp.where(at_group == group[:, part * 128 : part * 128 + 128], block, 0.0)
            block = jnp.sum(block.reshape(8, EMB, 128), axis=0)
            x_t[pl.ds(eight(f * EMB, EMB), EMB), pl.ds(part * 128, 128)] = block
        return carry

    lax.fori_loop(0, FIELDS, field, 0)
    x_t[pl.ds(FIELDS * EMB, DPROJ), :] = dot_tn(dw_ref[...], feats_ref[...], EXACT) + db_ref[...]
    out_ref[...] = x_t[...].T.astype(BF16)


def embed(src, hot, ids, answer, feats_t, dense_w, dense_b):
    return pl.pallas_call(
        embed_kernel,
        in_specs=[SM, SM, VM, VM, VM, VM, VM],
        out_specs=VM,
        out_shape=shape((ROWS_LOC, DIN), BF16),
        scratch_shapes=[
            pltpu.VMEM((OWNERS * GROUPS, 128), F32),
            pltpu.VMEM((LOOKUPS + 8, 128), F32),
            pltpu.VMEM((DIN, ROWS_LOC), F32),
        ],
        compiler_params=params(48),
        name="embed",
    )(src, hot, ids, answer, feats_t, dense_w, dense_b)


C0 = 0.7978845608
C1 = 0.7978845608 * 0.044715


def gelu_both(value):
    square = value * value
    bend = jnp.tanh(value * (C0 + C1 * square))
    half = 0.5 * (1.0 + bend)
    slope = half + 0.5 * value * (1.0 - bend * bend) * (C0 + 3.0 * C1 * square)
    return value * half, slope


def model_kernel(
    x_ref,
    labels_ref,
    feats_ref,
    dw_ref,
    weights_ref,
    b_out_ref,
    gate_w_ref,
    gate_b_ref,
    w1_ref,
    b1_ref,
    w2_ref,
    b2_ref,
    src_ref,
    hot_src_ref,
    hot_at_ref,
    rows_out_ref,
    experts_out_ref,
    small_out_ref,
    grad_dense_ref,
    small_ref,
    small_two,
    d_in_ref,
    hidden,
    slope,
    outs,
    probs,
    d_raw,
    prod_hi,
    prod_lo,
    mix,
    stage,
    own_grad,
    pair_send,
    pair_recv,
    share_send,
    share_recv,
    small_recv,
    experts_own,
    experts_all,
    small_own,
    small_all,
    rows,
    hot_rows,
    even,
    odd,
    ready,
    landing,
    pair_sems,
    sems,
):
    x = x_ref[...]
    phase = pl.program_id(0)
    line = lax.axis_index("dp")
    part = lax.axis_index("mp")
    core = line % 2
    chip = line // 2 * 4 + part
    me = my_index()

    def weights_in(k):
        return jnp.concatenate(
            [weights_ref[p, k, pl.ds(0, PART), pl.ds(0, DIN)] for p in range(4)], axis=0
        )

    def weights_out(k):
        return jnp.concatenate(
            [weights_ref[p, k, pl.ds(0, PART), pl.ds(DIN, EOUT)] for p in range(4)], axis=0
        )

    def forward(k, carry):
        bias = [
            weights_ref[p, k, pl.ds(PART, 16), pl.ds(0, 128)].astype(F32)[0:1, 0:PART]
            for p in range(4)
        ]
        pre = dot_nt(x, weights_in(k)) + jnp.concatenate(bias, axis=1)
        act, grad = gelu_both(pre)
        act = act.astype(BF16)
        hidden[k] = act
        slope[k] = grad
        outs[k] = dot_nn(act, weights_out(k)) + b_out_ref[k]
        return carry

    def head():
        gate_parts = jnp.concatenate(split3(gate_w_ref[...]), axis=0)
        stage[...] = dot_nt(gate_parts, x)
        logits = stage[0:16] + stage[16:32] + stage[32:48] + gate_b_ref[...]
        logits = logits.reshape(TASKS, EXPERTS, ROWS_LOC)
        gates = jnp.exp(logits - jnp.max(logits, axis=1, keepdims=True))
        gates = gates / jnp.sum(gates, axis=1, keepdims=True)
        gates_t = gates.reshape(TASKS * EXPERTS, ROWS_LOC)
        gate_stack = jnp.concatenate(split3(gates_t), axis=0)
        row_at = lax.broadcasted_iota(jnp.int32, (48, 128), 0) % 16

        def spread(k, carry):
            ones = (row_at == k).astype(F32).astype(BF16)
            probs[k] = dot_tn(gate_stack, ones)
            return carry

        lax.fori_loop(0, TASKS * EXPERTS, spread, 0)

        for t in range(TASKS):
            def add(k, total):
                return total + probs[t * EXPERTS + k] * outs[k]

            mix[:, pl.ds(t * EOUT, EOUT)] = lax.fori_loop(
                1, EXPERTS, add, probs[t * EXPERTS] * outs[0]
            )
        mixture = mix[...]
        zero = jnp.zeros((THID, EOUT), F32)
        w1_bd = jnp.concatenate(
            [
                jnp.concatenate([w1_ref[0], zero], axis=1),
                jnp.concatenate([zero, w1_ref[1]], axis=1),
            ],
            axis=0,
        )
        upper, upper_slope = gelu_both(dot_nt(mixture, w1_bd, EXACT) + b1_ref[...])
        w2_bd = w2_ref[...]
        logit = dot_nt(w2_bd, upper, EXACT) + b2_ref[...]
        d_logit = jax.nn.sigmoid(logit) - labels_ref[...].astype(F32)
        d_pre1 = dot_tn(d_logit, w2_bd, EXACT) * upper_slope
        grad_w2 = dot_nn(d_logit, upper, EXACT)
        grad_b1 = jnp.sum(d_pre1, axis=0, keepdims=True)
        grad_w1 = dot_tn(d_pre1, mixture, EXACT)
        d_mix = dot_nn(d_pre1, w1_bd, EXACT)
        mix[...] = d_mix

        def back_raw(k, carry):
            d_one = mix[:, pl.ds(0, EOUT)]
            d_two = mix[:, pl.ds(EOUT, EOUT)]
            grad = probs[k] * d_one + probs[EXPERTS + k] * d_two
            small_ref[pl.ds(128 + k, 1), :] = jnp.sum(grad, axis=0, keepdims=True)
            d_raw[k] = grad.astype(BF16)
            value = outs[k]
            for t, d_task in enumerate((d_one, d_two)):
                product = value * d_task
                high = product.astype(BF16)
                at = pl.ds(pl.multiple_of((t * EXPERTS + k) * EOUT, EOUT), EOUT)
                prod_hi[:, at] = high
                prod_lo[:, at] = (product - high.astype(F32)).astype(BF16)
            return carry

        lax.fori_loop(0, EXPERTS, back_raw, 0)

        wide = TASKS * EXPERTS * EOUT
        column_gate = lax.broadcasted_iota(jnp.int32, (16, wide), 1) // EOUT
        own_gate = lax.broadcasted_iota(jnp.int32, (16, wide), 0)
        ones = (column_gate == own_gate).astype(F32).astype(BF16)
        stage[0:16] = dot_nt(ones, prod_hi[...])
        stage[16:32] = dot_nt(ones, prod_lo[...])
        d_gates = stage[0:16] + stage[16:32]
        d_gates = d_gates.reshape(TASKS, EXPERTS, ROWS_LOC)
        mean = jnp.sum(d_gates * gates, axis=1, keepdims=True)
        d_logits = (gates * (d_gates - mean)).reshape(16, ROWS_LOC)
        d_parts = jnp.concatenate(split3(d_logits), axis=0)
        stage[...] = dot_nn(d_parts, x)
        grad_gate = stage[0:16] + stage[16:32] + stage[32:48]
        d_in_ref[...] = dot_tn(d_logits, gate_w_ref[...], EXACT)
        small_ref[pl.ds(0, THID), :] = grad_w1[0:THID, 0:EOUT]
        small_ref[pl.ds(THID, THID), :] = grad_w1[THID : 2 * THID, EOUT : 2 * EOUT]
        for tile in range(4):
            small_ref[pl.ds(136 + 16 * tile, 16), :] = grad_gate[:, tile * 128 : tile * 128 + 128]
        small_ref[pl.ds(217, 1), :] = grad_b1
        lane = lax.broadcasted_iota(jnp.int32, (1, 128), 1)
        small_ref[pl.ds(218, 1), :] = jnp.where(lane < THID, grad_w2[0:1], grad_w2[1:2])
        small_ref[pl.ds(219, 1), :] = jnp.zeros((1, 128), F32)
        small_ref[pl.ds(240, 16 + 32), :] = jnp.zeros((48, 128), F32)
        small_ref[pl.ds(220, 2), :] = jnp.broadcast_to(
            jnp.sum(d_logit, axis=1, keepdims=True), (2, 128)
        )
        small_ref[pl.ds(222, 2), :] = jnp.zeros((2, 128), F32)
        small_ref[pl.ds(224, 16), :] = jnp.broadcast_to(
            jnp.sum(d_logits, axis=1, keepdims=True), (16, 128)
        )

    def backward(k, store):
        d_out = d_raw[k]
        grad_out = dot_tn(hidden[k], d_out)
        d_pre = (dot_nt(d_out, weights_out(k)) * slope[k]).astype(BF16)
        bias = jnp.sum(d_pre.astype(F32), axis=0, keepdims=True)
        for p in range(4):
            small_ref[pl.ds(8 * (TILES + p) + k, 1), pl.ds(0, PART)] = bias[
                :, PART * p : PART * p + PART
            ]
        grad_in = dot_tn(d_pre, x)
        for p in range(4):
            at = slice(PART * p, PART * p + PART)
            for block in range(4):
                store(p, block, grad_in[at, block * 128 : block * 128 + 128])
            store(p, 4, grad_out[at, :])
        d_in_ref[...] += dot_nn(d_pre, weights_in(k))

    def remote(source, target, sem, place):
        return pltpu.make_async_remote_copy(
            src_ref=source,
            dst_ref=target,
            send_sem=sems.at[sem],
            recv_sem=sems.at[sem + 1],
            device_id=place,
            device_id_type=pl.DeviceIdType.MESH,
        )

    def wait_all(ref, sem):
        pltpu.make_async_copy(ref, ref, sem).wait()

    def experts(step, carry):
        q = (step + line // 2 + part) % 4

        def for_pair(p, block, value):
            pair_send[q, p, pl.ds(PART * block, PART), :] = value.astype(BF16)

        def for_own(p, block, value):
            own_grad[p, pl.ds(PART * block, PART), :] = value

        backward(2 * q + 1 - core, for_pair)
        pair = pltpu.make_async_remote_copy(
            src_ref=pair_send.at[q],
            dst_ref=pair_recv.at[q],
            send_sem=sems.at[0],
            recv_sem=pair_sems.at[q],
            device_id=(line + 1 - 2 * core, part),
            device_id_type=pl.DeviceIdType.MESH,
        )
        pair.start()
        backward(2 * q + core, for_own)
        pair.wait_recv()
        for p in range(4):
            total = own_grad[p] + pair_recv[q, p].astype(F32)
            share_send[q, p] = total.astype(BF16).reshape(4, CHUNK, 128)
        for r in range(4):
            for p in range(4):
                target = 2 * (4 * q + r) + core
                mine = (target == line) & (part == p)

                @pl.when(mine)
                def _():
                    share_recv[chip] = share_send[q, p, r]

                @pl.when(jnp.logical_not(mine))
                def _():
                    remote(
                        share_send.at[q, p, r], share_recv.at[chip], 1, (target, p)
                    ).start()

        return carry

    def tail():
        d_last = d_in_ref[:, pl.ds(DIN - DPROJ, DPROJ)]
        small_ref[pl.ds(200, 16), :] = jnp.zeros((16, 128), F32)
        small_ref[pl.ds(200, DENSE), pl.ds(0, DPROJ)] = dot_nn(feats_ref[...], d_last, EXACT)
        small_ref[pl.ds(216, 1), :] = jnp.zeros((1, 128), F32)
        small_ref[pl.ds(216, 1), pl.ds(0, DPROJ)] = jnp.sum(d_last, axis=0, keepdims=True)
        grad_dense_ref[...] = dot_nt(dw_ref[...], d_last, EXACT)

    def small_pair():
        return pltpu.make_async_remote_copy(
            src_ref=small_ref,
            dst_ref=small_two,
            send_sem=sems.at[9],
            recv_sem=sems.at[10],
            device_id=(line + 1 - 2 * core, part),
            device_id_type=pl.DeviceIdType.MESH,
        )

    def share_small():
        small_pair().wait()
        small_two[...] = small_two[...] + small_ref[...]
        for a in range(16):
            for p in range(4):
                target = 2 * a + core
                at = 8 * target
                if a == 15:
                    at = 8 * (TILES + p) - core * (8 + 8 * p)
                source = small_two.at[pl.ds(eight(at), 8), :]
                mine = (target == line) & (part == p)

                @pl.when(mine)
                def _():
                    small_recv[chip] = small_two[pl.ds(eight(at), 8), :]

                @pl.when(jnp.logical_not(mine))
                def _():
                    remote(source, small_recv.at[chip], 3, (target, p)).start()

    def add_up():
        others = pl.ds(0, CHIPS - 1)
        wait_all(share_recv.at[others], sems.at[2])
        wait_all(small_recv.at[others], sems.at[4])

        def add(at, totals):
            total, small = totals
            return total + share_recv[at].astype(F32), small + small_recv[at]

        total, small = lax.fori_loop(
            1, CHIPS, add, (share_recv[0].astype(F32), small_recv[0])
        )
        experts_own[...] = total.astype(BF16)
        small_own[...] = small
        experts_all[line] = total.astype(BF16)
        small_all[line] = small

        def give(step, carry):
            place = ((line + step) % TILES, part)
            remote(experts_own, experts_all.at[line], 5, place).start()
            remote(small_own, small_all.at[line], 7, place).start()
            return carry

        lax.fori_loop(1, TILES, give, 0)

    def drain():
        others = pl.ds(0, CHIPS - 1)
        wait_all(pair_send, sems.at[0])
        wait_all(share_recv.at[others], sems.at[1])
        wait_all(small_recv.at[others], sems.at[3])
        others = pl.ds(0, TILES - 1)
        for sem in (5, 6):
            wait_all(experts_all.at[others], sems.at[sem])
        for sem in (7, 8):
            wait_all(small_all.at[others], sems.at[sem])
        experts_out_ref[...] = experts_all[...]
        small_out_ref[...] = small_all[...]

    def spread():
        lane_from = lax.broadcasted_iota(jnp.int32, (128, 128), 0)
        lane_to = lax.broadcasted_iota(jnp.int32, (128, 128), 1)
        for field in range(FIELDS):
            take = lane_from == EMB * (field % 8) + lane_to % EMB
            copies = dot_nn(d_in_ref[:, pl.ds(field // 8 * 128, 128)].astype(BF16), take.astype(F32).astype(BF16))
            rows[pl.ds(field * ROWS_LOC, ROWS_LOC), :] = copies
        rows[pl.ds(LOOKUPS, 8), :] = jnp.zeros((8, 128), F32)
        group = lane_group(1)
        wide_group = lane_group(CAP - COLD)

        def hot(at, carry):
            for n in range(COLD, CAP):
                row = rows[pl.ds(hot_src_ref[at * SLOTS + n], 1), :]
                hot_rows[at, pl.ds(n - COLD, 1), :] = row
            return carry

        lax.fori_loop(0, HOT, hot, 0)
        hot_rows[HOT] = jnp.zeros((CAP - COLD, 128), F32)

        def collect(step, slots):
            source = (me // 8 + step) % 16 * (8 * SLOTS)
            for n in range(COLD):
                total = rows[pl.ds(src_ref[source + n], 1), :]
                for u in range(1, 8):
                    row = rows[pl.ds(src_ref[source + u * SLOTS + n], 1), :]
                    total = jnp.where(group == u, row, total)
                slots[pl.ds(n, 1), :] = total

        def finish(step, slots):
            first = (me // 8 + step) % 16 * 8
            total = jnp.zeros((CAP - COLD, 128), F32)
            for u in range(8):
                total = jnp.where(wide_group == u, hot_rows[hot_at_ref[first + u]], total)
            slots[pl.ds(COLD, CAP - COLD), :] = total
            for half in range(2):
                turned = slots[pl.ds(half * 128, 128), :].T.astype(BF16)
                for u in range(8):
                    at = eight((first + u) * GROUPS + EMB * half, EMB)
                    ready[pl.ds(at, EMB), :] = turned[EMB * u : EMB * u + EMB]

        def send(step):
            first = (me // 8 + step) % 16 * 8
            for u in range(8):
                dest = first + (me + u) % 8

                @pl.when(dest != me)
                def _():
                    send_block(ready, landing, me, dest, sems.at[11], sems.at[12])

        for slots in (even, odd):
            slots[pl.ds(CAP, SLOTS - CAP), :] = jnp.zeros((SLOTS - CAP, 128), F32)
        collect(0, even)
        share_small()

        def two_groups(pair, carry):
            step = 2 * pair
            collect(step + 1, odd)
            finish(step, even)
            send(step)
            collect(jnp.minimum(step + 2, 15), even)
            finish(step + 1, odd)
            send(step + 1)
            return carry

        lax.fori_loop(0, 6, two_groups, 0)
        add_up()
        lax.fori_loop(6, 8, two_groups, 0)
        wait_blocks(ready, landing, sems.at[11], sems.at[12])
        rows_out_ref[...] = landing[...]
        mine = pl.ds(eight(me * GROUPS, GROUPS), GROUPS)
        rows_out_ref[mine, :] = ready[mine, :]
        drain()

    @pl.when(phase == 0)
    def _():
        greet_all(me)
        lax.fori_loop(0, EXPERTS, forward, 0)

    @pl.when(phase == 1)
    def _():
        head()

    @pl.when(phase == 2)
    def _():
        pl.semaphore_wait(pltpu.get_barrier_semaphore(), OWNERS - 1)
        lax.fori_loop(0, 4, experts, 0)
        tail()
        small_pair().start()
        spread()


def model(*operands):
    return pl.pallas_call(
        model_kernel,
        grid=(3,),
        in_specs=[VM] * (len(operands) - 3) + [SM] * 3,
        out_specs=[VM] * 4,
        out_shape=[
            shape((OWNERS * GROUPS, 128), BF16),
            shape((TILES, CHUNK, 128), BF16),
            shape((TILES, 8, 128), F32),
            shape((DENSE, ROWS_LOC), F32),
        ],
        scratch_shapes=[
            pltpu.VMEM((8 * (TILES + 4), 128), F32),
            pltpu.VMEM((8 * (TILES + 4), 128), F32),
            pltpu.VMEM((ROWS_LOC, DIN), F32),
            pltpu.VMEM((EXPERTS, ROWS_LOC, HID), BF16),
            pltpu.VMEM((EXPERTS, ROWS_LOC, HID), F32),
            pltpu.VMEM((EXPERTS, ROWS_LOC, EOUT), F32),
            pltpu.VMEM((TASKS * EXPERTS, ROWS_LOC, EOUT), F32),
            pltpu.VMEM((EXPERTS, ROWS_LOC, EOUT), BF16),
            pltpu.VMEM((ROWS_LOC, TASKS * EXPERTS * EOUT), BF16),
            pltpu.VMEM((ROWS_LOC, TASKS * EXPERTS * EOUT), BF16),
            pltpu.VMEM((ROWS_LOC, TASKS * EOUT), F32),
            pltpu.VMEM((48, DIN), F32),
            pltpu.VMEM((4, 4 * CHUNK, 128), F32),
            pltpu.VMEM((4, 4, 4 * CHUNK, 128), BF16),
            pltpu.VMEM((4, 4, 4 * CHUNK, 128), BF16),
            pltpu.VMEM((4, 4, 4, CHUNK, 128), BF16),
            pltpu.VMEM((CHIPS, CHUNK, 128), BF16),
            pltpu.VMEM((CHIPS, 8, 128), F32),
            pltpu.VMEM((CHUNK, 128), BF16),
            pltpu.VMEM((TILES, CHUNK, 128), BF16),
            pltpu.VMEM((8, 128), F32),
            pltpu.VMEM((TILES, 8, 128), F32),
            pltpu.VMEM((LOOKUPS + 8, 128), F32),
            pltpu.VMEM((HOT + 1, CAP - COLD, 128), F32),
            pltpu.VMEM((SLOTS, 128), F32),
            pltpu.VMEM((SLOTS, 128), F32),
            pltpu.VMEM((OWNERS * GROUPS, 128), BF16),
            pltpu.VMEM((OWNERS * GROUPS, 128), BF16),
            pltpu.SemaphoreType.DMA((4,)),
            pltpu.SemaphoreType.DMA((13,)),
        ],
        compiler_params=remote_params(58, 1),
        name="model",
    )(*operands)


def scatter_kernel(
    asked_ref, grads_ref, out_ref, rows_v, groups, rows, sem, even, odd, *sums
):
    split_wanted(asked_ref, rows_v, groups, rows, sem)
    at_group = sublane_group()

    def clear(step, carry):
        for total in sums:
            total[pl.ds(eight(step * 512), 512), :] = jnp.zeros((512, 128), F32)
        return carry

    lax.fori_loop(0, PACKED // 512, clear, 0)

    def place(source, found):
        for half in range(2):
            block = grads_ref[pl.ds(eight(source * GROUPS + EMB * half, EMB), EMB), :].astype(F32)
            block = jnp.broadcast_to(block[None], (8, EMB, 128)).reshape(128, 128)
            block = jnp.where(at_group == groups[source, pl.ds(half, 1), :], block, 0.0)
            found[pl.ds(half * 128, 128), :] = block.T

    def add(source, found):
        for n in range(CAP):
            at = pl.ds(rows[source, n // 128, n % 128], 1)
            total = sums[n % SUMS]
            total[at, :] = total[at, :] + found[pl.ds(n, 1), :]

    place(0, even)

    def two_sources(step, carry):
        source = 2 * step
        place(source + 1, odd)
        add(source, even)
        place(jnp.minimum(source + 2, OWNERS - 1), even)
        add(source + 1, odd)
        return carry

    lax.fori_loop(0, OWNERS // 2, two_sources, 0)

    def write(field, carry):
        for part in range(4):
            at = pl.ds(eight(field * 512 + part * 128, 128), 128)
            block = sums[0][at, :]
            for total in sums[1:]:
                block = block + total[at, :]
            block = block.T
            for k in range(8):
                out_ref[field, :, pl.ds(part * 1024 + k * 128, 128)] = block[16 * k : 16 * k + 16]
        return carry

    lax.fori_loop(0, FIELDS, write, 0)


def scatter_add(asked, grads):
    return pl.pallas_call(
        scatter_kernel,
        in_specs=[VM, VM],
        out_specs=VM,
        out_shape=shape((FIELDS, EMB, ROWS_DEV), F32),
        scratch_shapes=split_scratch()
        + [pltpu.VMEM((SLOTS, 128), F32)] * 2
        + [pltpu.VMEM((PACKED + 8, 128), F32)] * SUMS,
        compiler_params=params(58),
        name="scatter_add",
    )(asked, grads)


def unpack_kernel(
    experts_ref,
    small_ref,
    w_in_ref,
    w_out_ref,
    w1_ref,
    b_out_ref,
    gate_ref,
    dense_w_ref,
    dense_b_ref,
    b1_ref,
    w2_ref,
    b2_ref,
    gate_b_ref,
    b_in_ref,
):
    def expert(k, carry):
        rows = [experts_ref[2 * (4 * (k // 2) + at) + k % 2] for at in range(4)]
        rows = jnp.concatenate(rows, axis=0).astype(F32)
        for block in range(4):
            w_in_ref[k, :, pl.ds(block * 128, 128)] = rows[PART * block : PART * block + PART]
        w_out_ref[k] = rows[4 * PART : 5 * PART]
        return carry

    lax.fori_loop(0, EXPERTS, expert, 0)

    def tile(at):
        return small_ref[at]

    for at in range(16):
        w1_ref[at // 8, pl.ds(at % 8 * 8, 8), :] = tile(at)
    b_out_ref[...] = tile(16)
    for at in range(8):
        gate_ref[pl.ds(at % 2 * 8, 8), pl.ds(at // 2 * 128, 128)] = tile(17 + at)
    dense_w_ref[pl.ds(0, 8), :] = tile(25)[:, 0:DPROJ]
    dense_w_ref[pl.ds(8, DENSE - 8), :] = tile(26)[0 : DENSE - 8, 0:DPROJ]
    rest = tile(27)
    dense_b_ref[...] = rest[0:1, 0:DPROJ]
    for t in range(TASKS):
        b1_ref[pl.ds(t, 1), :] = rest[1:2, t * THID : t * THID + THID]
        w2_ref[pl.ds(t, 1), :] = rest[2:3, t * THID : t * THID + THID]
    lane = lax.broadcasted_iota(jnp.int32, (1, 128), 1)
    b2_ref[...] = jnp.where(lane == 0, rest[4:5], rest[5:6])[:, 0:TASKS]
    own = lax.broadcasted_iota(jnp.int32, (8, 128), 0) == lax.broadcasted_iota(
        jnp.int32, (8, 128), 1
    )
    for t in range(TASKS):
        value = jnp.sum(jnp.where(own, tile(28 + t), 0.0), axis=0, keepdims=True)
        gate_b_ref[pl.ds(t, 1), :] = value[:, 0:EXPERTS]
    b_in_ref[...] = tile(30)[:, 0:PART]


def unpack(experts, small):
    return pl.pallas_call(
        unpack_kernel,
        in_specs=[VM, VM],
        out_specs=[VM] * 12,
        out_shape=[
            shape((EXPERTS, PART, DIN), F32),
            shape((EXPERTS, PART, EOUT), F32),
            shape((TASKS, THID, EOUT), F32),
            shape((EXPERTS, EOUT), F32),
            shape((TASKS * EXPERTS, DIN), F32),
            shape((DENSE, DPROJ), F32),
            shape((1, DPROJ), F32),
            shape((TASKS, THID), F32),
            shape((TASKS, THID), F32),
            shape((1, TASKS), F32),
            shape((TASKS, EXPERTS), F32),
            shape((EXPERTS, PART), F32),
        ],
        compiler_params=params(32),
        name="unpack",
    )(experts, small)


def body(
    sparse_ids,
    dense_feats,
    labels,
    tables,
    dense_w,
    dense_b,
    w_in,
    b_in,
    w_out,
    b_out,
    gate_w,
    gate_b,
    tower_w1,
    tower_b1,
    tower_w2,
    tower_b2,
):
    weights = jnp.concatenate([w_in.transpose(0, 2, 1), w_out], axis=2)
    bias = jnp.pad(b_in[:, None, :], ((0, 0), (0, 15), (0, DIN + EOUT - PART)))
    weights = lax.all_gather(jnp.concatenate([weights, bias], axis=1), "mp", axis=0)

    ids = sparse_ids.T
    field = lax.broadcasted_iota(jnp.int32, (FIELDS, ROWS_LOC), 0)
    example = lax.broadcasted_iota(jnp.int32, (FIELDS, ROWS_LOC), 1)
    row = ids & (ROWS_DEV - 1)
    packed = field * 512 + (row >> 10) * 128 + (row & 127)
    key = ((ids >> 12) << 14) | (field * ROWS_LOC + example)
    load = (packed << 3) | ((row >> 7) & 7)
    keys, loads = lax.sort((key.reshape(-1), load.reshape(-1)), num_keys=1, is_stable=False)
    requests, sources, hot_sources, hot, hot_at = route(keys.reshape(-1, 128), loads.reshape(-1, 128))
    sources = sources.reshape(-1)
    answer, asked = look_up(requests, tables.transpose(0, 2, 1))
    feats_t = dense_feats.T
    inputs = embed(sources, hot, ids, answer, feats_t, dense_w, dense_b.reshape(DPROJ, 1))
    task_at = lax.broadcasted_iota(jnp.int32, (TASKS, TASKS * THID), 1) // THID
    task_row = lax.broadcasted_iota(jnp.int32, (TASKS, TASKS * THID), 0)
    w2_bd = jnp.where(task_at == task_row, tower_w2.reshape(1, -1), 0.0)
    incoming, experts, small, grad_dense = model(
        inputs,
        labels.T,
        feats_t,
        dense_w,
        weights,
        b_out.reshape(EXPERTS, 1, EOUT),
        gate_w.transpose(0, 2, 1).reshape(TASKS * EXPERTS, DIN),
        gate_b.reshape(TASKS * EXPERTS, 1),
        tower_w1.transpose(0, 2, 1),
        tower_b1.reshape(1, TASKS * THID),
        w2_bd,
        tower_b2.reshape(TASKS, 1),
        sources,
        hot_sources.reshape(-1),
        hot_at,
    )
    grad_tables = scatter_add(asked, incoming).transpose(0, 2, 1)
    (
        grad_w_in,
        grad_w_out,
        grad_w1,
        grad_b_out,
        grad_gate_w,
        grad_dense_w,
        grad_dense_b,
        grad_b1,
        grad_w2,
        grad_b2,
        grad_gate_b,
        grad_b_in,
    ) = unpack(experts, small)
    return (
        grad_tables,
        grad_dense_w,
        grad_dense_b.reshape(DPROJ),
        grad_w_in.transpose(0, 2, 1),
        grad_b_in,
        grad_w_out,
        grad_b_out,
        grad_gate_w.reshape(TASKS, EXPERTS, DIN).transpose(0, 2, 1),
        grad_gate_b,
        grad_w1.transpose(0, 2, 1),
        grad_b1,
        grad_w2,
        grad_b2.reshape(TASKS),
        grad_dense.T,
    )


def solution(mesh):
    return jax.shard_map(
        body,
        mesh=mesh,
        in_specs=(
            P(ALL, None),
            P(ALL, None),
            P(ALL, None),
            P(None, ALL, None),
            P(),
            P(),
            P(None, None, "mp"),
            P(None, "mp"),
            P(None, "mp", None),
            P(),
            P(),
            P(),
            P(),
            P(),
            P(),
            P(),
        ),
        out_specs=(
            P(None, ALL, None),
            P(),
            P(),
            P(None, None, "mp"),
            P(None, "mp"),
            P(None, "mp", None),
            P(),
            P(),
            P(),
            P(),
            P(),
            P(),
            P(),
            P(ALL, None),
        ),
        check_vma=False,
    )
```

```python
import functools

import jax
import jax.numpy as jnp
from jax import lax
from jax.experimental import pallas as pl
from jax.experimental.pallas import tpu as pltpu
from jax.sharding import PartitionSpec as P

ALL = ("dp", "mp")
EXACT = lax.Precision.HIGHEST
F32 = jnp.float32
BF16 = jnp.bfloat16

OWNERS = 128
FIELDS = 26
EMB = 16
ROWS_LOC = 512
ROWS_DEV = 4096
LOOKUPS = ROWS_LOC * FIELDS
PACKED = FIELDS * ROWS_DEV // 8
CAP = 208
COLD = 96
HOT = 16
SLOTS = 256
GROUPS = SLOTS // 8
EXPERTS = 8
HID = 256
EOUT = 128
TASKS = 2
THID = 64
DIN = 512
DENSE = 13
DPROJ = 96
CHUNK = 80
TILES = 32
CHIPS = OWNERS // 2
SHARE = CHUNK + 16
MODEL_MIB = 50
PART = 64
SUMS = 6

VM = pl.BlockSpec(memory_space=pltpu.VMEM)
SM = pl.BlockSpec(memory_space=pltpu.SMEM)


def params(mib):
    return pltpu.CompilerParams(vmem_limit_bytes=mib * 1024 * 1024)


def shape(dims, dtype):
    return jax.ShapeDtypeStruct(dims, dtype)


def lane_group(rows):
    return lax.broadcasted_iota(jnp.int32, (rows, 128), 1) // EMB


def sublane_group():
    return lax.broadcasted_iota(jnp.int32, (128, 128), 0) // EMB


def eight(index, unit=8):
    return pl.multiple_of(index, unit)


def dot_nt(a, b, precision=None):
    return lax.dot_general(
        a, b, (((1,), (1,)), ((), ())), precision=precision, preferred_element_type=F32
    )


def dot_tn(a, b, precision=None):
    return lax.dot_general(
        a, b, (((0,), (0,)), ((), ())), precision=precision, preferred_element_type=F32
    )


def dot_nn(a, b, precision=None):
    return lax.dot_general(
        a, b, (((1,), (0,)), ((), ())), precision=precision, preferred_element_type=F32
    )


def split3(value):
    high = value.astype(BF16)
    rest = value - high.astype(F32)
    mid = rest.astype(BF16)
    low = (rest - mid.astype(F32)).astype(BF16)
    return high, mid, low


def my_index():
    return lax.axis_index("dp") * lax.axis_size("mp") + lax.axis_index("mp")


def place_of(index):
    return (index // 4, index % 4)


def greet_all(me):
    barrier = pltpu.get_barrier_semaphore()

    def greet(step, carry):
        pl.semaphore_signal(
            barrier,
            inc=1,
            device_id=place_of((me + step + 1) % OWNERS),
            device_id_type=pl.DeviceIdType.MESH,
        )
        return carry

    lax.fori_loop(0, OWNERS - 1, greet, 0)
    return barrier


def block_of(ref, index):
    return ref.at[pl.ds(eight(index * GROUPS, GROUPS), GROUPS), :]


def send_block(ready, landing, me, dest, send_sem, recv_sem):
    pltpu.make_async_remote_copy(
        src_ref=block_of(ready, dest),
        dst_ref=block_of(landing, me),
        send_sem=send_sem,
        recv_sem=recv_sem,
        device_id=place_of(dest),
        device_id_type=pl.DeviceIdType.MESH,
    ).start()


def wait_blocks(ready, landing, send_sem, recv_sem):
    every = pl.ds(0, (OWNERS - 1) * GROUPS)
    pltpu.make_async_copy(ready.at[every, :], ready.at[every, :], send_sem).wait()
    pltpu.make_async_copy(landing.at[every, :], landing.at[every, :], recv_sem).wait()


def remote_params(mib, identity):
    return pltpu.CompilerParams(
        vmem_limit_bytes=mib * 1024 * 1024, collective_id=identity, has_side_effects=True
    )


def route_kernel(
    key_ref,
    load_ref,
    req_ref,
    src_ref,
    hot_src_ref,
    hot_ref,
    hot_at_ref,
    both,
    cut,
    starts_v,
    starts,
    sem,
):
    own = (key_ref[...] & 16383) << 17
    both[pl.ds(0, 104), :] = own | load_ref[...]
    both[pl.ds(104, 8), :] = jnp.zeros((8, 128), jnp.int32)
    owner_at = lax.broadcasted_iota(jnp.int32, (128, 128), 0)

    def count(step, total):
        rows = key_ref[pl.ds(eight(step * 8), 8), :] >> 14
        for at in range(8):
            total = total + (rows[at : at + 1, :] < owner_at).astype(jnp.int32)
        return total

    below = lax.fori_loop(0, 13, count, jnp.zeros((128, 128), jnp.int32))
    first = jnp.sum(below.astype(F32).T, axis=0, keepdims=True).astype(jnp.int32)
    starts_v[...] = jnp.broadcast_to(first, (8, 128))
    copy = pltpu.make_async_copy(starts_v, starts, sem)
    copy.start()
    copy.wait()
    for at in range(2 * HOT):
        hot_ref[at] = 0
    lane = lax.broadcasted_iota(jnp.int32, (1, 128), 1)
    unused = (LOOKUPS << 17) | (PACKED * 8)

    def per_owner(owner, hot_count):
        start = starts[0, owner]
        end = jnp.where(owner == OWNERS - 1, LOOKUPS, starts[0, jnp.minimum(owner + 1, 127)])
        row = start >> 7
        off = start & 127
        pieces = [both[pl.ds(row + at, 1), :] for at in range(3)]
        for half in range(2):
            piece = jnp.where(lane >= off, pieces[half], pieces[half + 1])
            piece = pltpu.roll(piece, (128 - off) & 127, 1)
            piece = jnp.where(lane < end - start - 128 * half, piece, unused)
            cut[pl.ds(2 * owner + half, 1), :] = piece
            hot_src_ref[pl.ds(2 * hot_count + half, 1), :] = piece >> 17
        is_hot = end - start > COLD
        hot_ref[hot_count] = owner
        hot_at_ref[owner] = jnp.where(is_hot & (hot_count < HOT), hot_count, HOT)
        return jnp.minimum(hot_count + is_hot.astype(jnp.int32), 2 * HOT - 1)

    lax.fori_loop(0, OWNERS, per_owner, 0, unroll=8)
    src_ref[...] = cut[...] >> 17
    req_ref[...] = (cut[...] & ((1 << 17) - 1)).reshape(OWNERS, 2, 128)


def route(keys, loads):
    return pl.pallas_call(
        route_kernel,
        in_specs=[VM, VM],
        out_specs=[VM, VM, VM, SM, SM],
        out_shape=[
            shape((OWNERS, 2, 128), jnp.int32),
            shape((2 * OWNERS, 128), jnp.int32),
            shape((4 * HOT, 128), jnp.int32),
            shape((2 * HOT,), jnp.int32),
            shape((OWNERS,), jnp.int32),
        ],
        scratch_shapes=[
            pltpu.VMEM((112, 128), jnp.int32),
            pltpu.VMEM((2 * OWNERS, 128), jnp.int32),
            pltpu.VMEM((8, 128), jnp.int32),
            pltpu.SMEM((8, 128), jnp.int32),
            pltpu.SemaphoreType.DMA,
        ],
        compiler_params=params(8),
        name="route",
    )(keys, loads)


def split_wanted(asked_ref, rows_v, groups):
    rows_v[...] = asked_ref[...] >> 3
    groups[...] = asked_ref[...] & 7


def split_scratch():
    return [
        pltpu.VMEM((OWNERS, 2, 128), jnp.int32),
        pltpu.VMEM((OWNERS, 2, 128), jnp.int32),
        pltpu.SMEM((OWNERS, 2, 128), jnp.int32),
        pltpu.SemaphoreType.DMA((8,)),
    ]


def look_up_kernel(
    wanted_ref,
    tables_ref,
    w_out_ref,
    b_in_ref,
    out_ref,
    asked_ref,
    w_out_all,
    b_in_all,
    b_low,
    b_own,
    fields,
    table,
    rows_v,
    groups,
    rows,
    sem,
    even,
    odd,
    ready,
    field_sem,
    ask_send,
    ask_recv,
    send_sem,
    recv_sem,
    own_sem,
    weight_sems,
):
    me = my_index()
    line = lax.axis_index("dp")
    part = lax.axis_index("mp")

    def field_copy(field):
        return pltpu.make_async_copy(
            tables_ref.at[field], fields.at[field], field_sem.at[field]
        )

    def start_field(field, carry):
        field_copy(field).start()
        return carry

    own_weights = [
        pltpu.make_async_copy(source, target, weight_sems.at[4 + at])
        for at, (source, target) in enumerate(((w_out_ref, w_out_all.at[part]), (b_in_ref, b_low)))
    ]
    for copy in own_weights:
        copy.start()
    lax.fori_loop(0, FIELDS, start_field, 0)
    barrier = greet_all(me)

    def pack(field, carry):
        field_copy(field).wait()
        for part in range(4):
            block = jnp.concatenate(
                [fields[field, :, pl.ds(part * 1024 + k * 128, 128)] for k in range(8)], axis=0
            )
            table[pl.ds(eight(field * 512 + part * 128, 128), 128), :] = block.T
        return carry

    lax.fori_loop(0, 8, pack, 0)
    table[pl.ds(PACKED, 8), :] = jnp.zeros((8, 128), F32)
    asked_ref[me] = wanted_ref[me]
    pl.semaphore_wait(barrier, OWNERS - 1)

    def ask(step, carry):
        owner = (me + step + 1) % OWNERS
        pltpu.make_async_remote_copy(
            src_ref=wanted_ref.at[owner],
            dst_ref=asked_ref.at[me],
            send_sem=ask_send,
            recv_sem=ask_recv,
            device_id=place_of(owner),
            device_id_type=pl.DeviceIdType.MESH,
        ).start()
        return carry

    lax.fori_loop(0, OWNERS - 1, ask, 0)
    for copy in own_weights:
        copy.wait()
    b_own[...] = jnp.zeros_like(b_own)
    b_own[:, pl.ds(0, PART)] = b_low[...].astype(F32)
    b_in_all[part] = b_own[...]

    def weight_copies(step):
        place = (line, (part + step) % 4)
        return [
            pltpu.make_async_remote_copy(
                src_ref=source,
                dst_ref=target.at[part],
                send_sem=weight_sems.at[2 * at],
                recv_sem=weight_sems.at[2 * at + 1],
                device_id=place,
                device_id_type=pl.DeviceIdType.MESH,
            )
            for at, (source, target) in enumerate(((w_out_ref, w_out_all), (b_own, b_in_all)))
        ]

    for step in range(1, 4):
        for copy in weight_copies(step):
            copy.start()
    lax.fori_loop(8, FIELDS, pack, 0)
    others = pl.ds(0, OWNERS - 1)
    pltpu.make_async_copy(asked_ref.at[others], asked_ref.at[others], ask_recv).wait()
    split_wanted(asked_ref, rows_v, groups)

    def rows_copy(step):
        chunk = pl.ds(eight((me // 16 + step) % 8 * 16, 16), 16)
        return pltpu.make_async_copy(rows_v.at[chunk], rows.at[chunk], sem.at[step])

    for step in range(8):
        rows_copy(step).start()
    for step in range(2):
        rows_copy(step).wait()
    at_group = sublane_group()

    def gather(source, found):
        for n in range(CAP):
            at = rows[source, n // 128, n % 128]
            found[pl.ds(n, 1), :] = table[pl.ds(at, 1), :]

    def pick(source, found):
        for half in range(2):
            block = found[pl.ds(half * 128, 128), :].T
            block = jnp.where(at_group == groups[source, pl.ds(half, 1), :], block, 0.0)
            block = jnp.sum(block.reshape(8, EMB, 128), axis=0)
            ready[pl.ds(eight(source * GROUPS + EMB * half, EMB), EMB), :] = block.astype(BF16)

    def send(source):
        send_block(ready, out_ref, me, source, send_sem, recv_sem)

    even[...] = jnp.zeros_like(even)
    odd[...] = jnp.zeros_like(odd)
    gather(me, even)
    gather((me + 1) % OWNERS, odd)
    pick(me, even)
    own = pltpu.make_async_copy(block_of(ready, me), block_of(out_ref, me), own_sem)
    own.start()

    def two_sources(step, carry):
        first = (me + 2 * step + 1) % OWNERS
        second = (me + 2 * step + 2) % OWNERS
        third = (me + 2 * step + 3) % OWNERS
        gather(second, even)
        pick(first, odd)
        send(first)
        gather(third, odd)
        pick(second, even)
        send(second)
        return carry

    lax.fori_loop(0, 6, two_sources, 0)
    for step in range(2, 8):
        rows_copy(step).wait()
    lax.fori_loop(6, OWNERS // 2 - 1, two_sources, 0)
    last = (me + OWNERS - 1) % OWNERS
    pick(last, odd)
    send(last)
    own.wait()
    pltpu.make_async_copy(wanted_ref.at[others], wanted_ref.at[others], ask_send).wait()
    three = pl.ds(0, 3)
    for at, target in enumerate((w_out_all, b_in_all)):
        for sem_at in (2 * at, 2 * at + 1):
            sem = weight_sems.at[sem_at]
            pltpu.make_async_copy(target.at[three], target.at[three], sem).wait()
    wait_blocks(ready, out_ref, send_sem, recv_sem)


def look_up(wanted, tables_t, w_out, b_in):
    return pl.pallas_call(
        look_up_kernel,
        in_specs=[VM] + [pl.BlockSpec(memory_space=pl.ANY)] * 3,
        out_specs=[VM] * 4,
        out_shape=[
            shape((OWNERS * GROUPS, 128), BF16),
            shape((OWNERS, 2, 128), jnp.int32),
            shape((4, EXPERTS, PART, EOUT), BF16),
            shape((4, EXPERTS, 128), F32),
        ],
        scratch_shapes=[
            pltpu.VMEM((EXPERTS, PART), BF16),
            pltpu.VMEM((EXPERTS, 128), F32),
            pltpu.VMEM((FIELDS, EMB, ROWS_DEV), F32),
            pltpu.VMEM((PACKED + 8, 128), F32),
        ]
        + split_scratch()
        + [pltpu.VMEM((SLOTS, 128), F32)] * 2
        + [pltpu.VMEM((OWNERS * GROUPS, 128), BF16)]
        + [pltpu.SemaphoreType.DMA((FIELDS,))]
        + [pltpu.SemaphoreType.DMA] * 5
        + [pltpu.SemaphoreType.DMA((6,))],
        compiler_params=remote_params(48, 0),
        name="look_up",
    )(wanted, tables_t, w_out, b_in)


def embed_kernel(
    src_ref, hot_ref, ids_ref, answer_ref, feats_ref, dw_ref, db_ref, out_ref, slots, rows, x_t
):
    for block in range(32):
        owner, half = block // 2 * 8, block % 2
        parts = [
            answer_ref[pl.ds((owner + u) * GROUPS + EMB * half, EMB), :] for u in range(8)
        ]
        slots[pl.ds(block * 128, 128), :] = jnp.concatenate(parts, axis=0).astype(F32).T

    def cold(step, carry):
        base = step // 6 * SLOTS + step % 6 * 16
        source = step // 6 * (8 * SLOTS) + step % 6 * 16
        for n in range(16):
            row = slots[pl.ds(base + n, 1), :]
            for u in range(8):
                rows[pl.ds(src_ref[source + u * SLOTS + n], 1), :] = row
        return carry

    def hot(at, carry):
        owner = hot_ref[at]
        base = (owner >> 3) * SLOTS
        for n in range(COLD, CAP):
            rows[pl.ds(src_ref[owner * SLOTS + n], 1), :] = slots[pl.ds(base + n, 1), :]
        return carry

    lax.fori_loop(0, OWNERS // 8 * 6, cold, 0)
    lax.fori_loop(0, HOT, hot, 0)
    at_group = sublane_group()

    def field(f, carry):
        group = (ids_ref[pl.ds(f, 1), :] >> 12) & 7
        for part in range(4):
            block = rows[pl.ds(eight(f * ROWS_LOC + part * 128, 128), 128), :].T
            block = jnp.where(at_group == group[:, part * 128 : part * 128 + 128], block, 0.0)
            block = jnp.sum(block.reshape(8, EMB, 128), axis=0)
            x_t[pl.ds(eight(f * EMB, EMB), EMB), pl.ds(part * 128, 128)] = block
        return carry

    lax.fori_loop(0, FIELDS, field, 0)
    top = lax.broadcasted_iota(jnp.int32, (8, DPROJ), 0) == 0
    bias = jnp.where(top, jnp.broadcast_to(db_ref[...], (8, DPROJ)), 0.0)
    x_t[pl.ds(FIELDS * EMB, DPROJ), :] = (
        dot_tn(dw_ref[...], feats_ref[...], EXACT)
        + dot_tn(bias, jnp.ones((8, ROWS_LOC), F32), EXACT)
    )
    out_ref[...] = x_t[...].T.astype(BF16)


def embed(src, hot, ids, answer, feats_t, dense_w, dense_b):
    return pl.pallas_call(
        embed_kernel,
        in_specs=[SM, SM, VM, VM, VM, VM, VM],
        out_specs=VM,
        out_shape=shape((ROWS_LOC, DIN), BF16),
        scratch_shapes=[
            pltpu.VMEM((OWNERS * GROUPS, 128), F32),
            pltpu.VMEM((LOOKUPS + 8, 128), F32),
            pltpu.VMEM((DIN, ROWS_LOC), F32),
        ],
        compiler_params=params(16),
        name="embed",
    )(src, hot, ids, answer, feats_t, dense_w, dense_b)


C0 = 0.7978845608
C1 = 0.7978845608 * 0.044715


def gelu_both(value):
    square = value * value
    bend = jnp.tanh(value * (C0 + C1 * square))
    half = 0.5 * (1.0 + bend)
    slope = half + 0.5 * value * (1.0 - bend * bend) * (C0 + 3.0 * C1 * square)
    return value * half, slope


def two_parts(value):
    high = value.astype(BF16).astype(F32)
    return jnp.concatenate([high, value - high], axis=0).astype(BF16)


def one_of(parts):
    wide = parts.astype(F32)
    return wide[0:8] + wide[8:16]


def model_kernel(
    x_ref,
    labels_ref,
    feats_ref,
    dw_ref,
    w_in_ref,
    w_out_ref,
    b_in_ref,
    b_out_ref,
    gate_w_ref,
    gate_b_ref,
    w1_ref,
    b1_ref,
    w2_ref,
    b2_ref,
    src_ref,
    hot_src_ref,
    hot_at_ref,
    rows_out_ref,
    share_out_ref,
    grad_dense_ref,
    small_ref,
    small_two,
    d_in_ref,
    hidden,
    slope,
    outs,
    probs,
    d_raw,
    prod_hi,
    prod_lo,
    mix,
    stage,
    own_grad,
    pair_send,
    pair_recv,
    share_send,
    first_recv,
    second_send,
    share_recv,
    small_recv,
    small_own,
    small_all,
    rows,
    hot_rows,
    even,
    odd,
    ready,
    landing,
    pair_sems,
    first_sems,
    sems,
):
    x = x_ref[...]
    phase = pl.program_id(0)
    line = lax.axis_index("dp")
    part = lax.axis_index("mp")
    core = line % 2
    chip = line // 2 * 4 + part
    me = my_index()
    at_y, at_x = line // 8, line // 2 % 4

    def weights_in(k):
        return jnp.concatenate(
            [w_in_ref[p, k] for p in range(4)], axis=0
        )

    def weights_out(k):
        return jnp.concatenate(
            [w_out_ref[p, k] for p in range(4)], axis=0
        )

    def forward(k, carry):
        bias = [b_in_ref[p, pl.ds(k, 1), :][:, 0:PART] for p in range(4)]
        pre = dot_nt(x, weights_in(k)) + jnp.concatenate(bias, axis=1)
        act, grad = gelu_both(pre)
        act = act.astype(BF16)
        hidden[k] = act
        slope[k] = grad
        outs[k] = dot_nn(act, weights_out(k)) + b_out_ref[pl.ds(k, 1), :]
        return carry

    def head():
        gate_parts = jnp.concatenate(split3(gate_w_ref[...]), axis=0)
        stage[...] = dot_nt(gate_parts, x)
        own = lax.broadcasted_iota(jnp.int32, (EXPERTS, EXPERTS), 0) == lax.broadcasted_iota(
            jnp.int32, (EXPERTS, EXPERTS), 1
        )
        gate_b = [
            jnp.sum(jnp.where(own, gate_b_ref[pl.ds(t, 1), :], 0.0), axis=1, keepdims=True)
            for t in range(TASKS)
        ]
        logits = stage[0:16] + stage[16:32] + stage[32:48] + jnp.concatenate(gate_b, axis=0)
        logits = logits.reshape(TASKS, EXPERTS, ROWS_LOC)
        gates = jnp.exp(logits - jnp.max(logits, axis=1, keepdims=True))
        gates = gates / jnp.sum(gates, axis=1, keepdims=True)
        gates_t = gates.reshape(TASKS * EXPERTS, ROWS_LOC)
        gate_stack = jnp.concatenate(split3(gates_t), axis=0)
        row_at = lax.broadcasted_iota(jnp.int32, (48, 128), 0) % 16

        def spread(k, carry):
            ones = (row_at == k).astype(F32).astype(BF16)
            probs[k] = dot_tn(gate_stack, ones)
            return carry

        lax.fori_loop(0, TASKS * EXPERTS, spread, 0)

        for t in range(TASKS):
            def add(k, total):
                return total + probs[t * EXPERTS + k] * outs[k]

            mix[:, pl.ds(t * EOUT, EOUT)] = lax.fori_loop(
                1, EXPERTS, add, probs[t * EXPERTS] * outs[0]
            )
        mixture = mix[...]
        zero = jnp.zeros((THID, EOUT), F32)
        w1_bd = jnp.concatenate(
            [
                jnp.concatenate([w1_ref[0], zero], axis=1),
                jnp.concatenate([zero, w1_ref[1]], axis=1),
            ],
            axis=0,
        )
        b1 = jnp.concatenate([b1_ref[pl.ds(t, 1), :] for t in range(TASKS)], axis=1)
        upper, upper_slope = gelu_both(dot_nt(mixture, w1_bd, EXACT) + b1)
        none = jnp.zeros((1, THID), F32)
        w2_bd = jnp.concatenate(
            [
                jnp.concatenate([w2_ref[pl.ds(0, 1), :], none], axis=1),
                jnp.concatenate([none, w2_ref[pl.ds(1, 1), :]], axis=1),
            ],
            axis=0,
        )
        task = lax.broadcasted_iota(jnp.int32, (TASKS, ROWS_LOC), 0)
        logit = dot_nt(w2_bd, upper, EXACT) + jnp.where(task == 0, b2_ref[0], b2_ref[1])
        d_logit = jax.nn.sigmoid(logit) - labels_ref[...].astype(F32)
        d_pre1 = dot_tn(d_logit, w2_bd, EXACT) * upper_slope
        grad_w2 = dot_nn(d_logit, upper, EXACT)
        grad_b1 = jnp.sum(d_pre1, axis=0, keepdims=True)
        grad_w1 = dot_tn(d_pre1, mixture, EXACT)
        d_mix = dot_nn(d_pre1, w1_bd, EXACT)
        mix[...] = d_mix

        def back_raw(k, carry):
            d_one = mix[:, pl.ds(0, EOUT)]
            d_two = mix[:, pl.ds(EOUT, EOUT)]
            grad = probs[k] * d_one + probs[EXPERTS + k] * d_two
            small_ref[pl.ds(128 + k, 1), :] = jnp.sum(grad, axis=0, keepdims=True)
            d_raw[k] = grad.astype(BF16)
            value = outs[k]
            for t, d_task in enumerate((d_one, d_two)):
                product = value * d_task
                high = product.astype(BF16)
                at = pl.ds(pl.multiple_of((t * EXPERTS + k) * EOUT, EOUT), EOUT)
                prod_hi[:, at] = high
                prod_lo[:, at] = (product - high.astype(F32)).astype(BF16)
            return carry

        lax.fori_loop(0, EXPERTS, back_raw, 0)

        wide = TASKS * EXPERTS * EOUT
        column_gate = lax.broadcasted_iota(jnp.int32, (16, wide), 1) // EOUT
        own_gate = lax.broadcasted_iota(jnp.int32, (16, wide), 0)
        ones = (column_gate == own_gate).astype(F32).astype(BF16)
        stage[0:16] = dot_nt(ones, prod_hi[...])
        stage[16:32] = dot_nt(ones, prod_lo[...])
        d_gates = stage[0:16] + stage[16:32]
        d_gates = d_gates.reshape(TASKS, EXPERTS, ROWS_LOC)
        mean = jnp.sum(d_gates * gates, axis=1, keepdims=True)
        d_logits = (gates * (d_gates - mean)).reshape(16, ROWS_LOC)
        d_parts = jnp.concatenate(split3(d_logits), axis=0)
        stage[...] = dot_nn(d_parts, x)
        grad_gate = stage[0:16] + stage[16:32] + stage[32:48]
        d_in_ref[...] = dot_tn(d_logits, gate_w_ref[...], EXACT)
        small_ref[pl.ds(0, THID), :] = grad_w1[0:THID, 0:EOUT]
        small_ref[pl.ds(THID, THID), :] = grad_w1[THID : 2 * THID, EOUT : 2 * EOUT]
        for tile in range(4):
            small_ref[pl.ds(136 + 16 * tile, 16), :] = grad_gate[:, tile * 128 : tile * 128 + 128]
        small_ref[pl.ds(217, 1), :] = grad_b1
        lane = lax.broadcasted_iota(jnp.int32, (1, 128), 1)
        small_ref[pl.ds(218, 1), :] = jnp.where(lane < THID, grad_w2[0:1], grad_w2[1:2])
        small_ref[pl.ds(219, 1), :] = jnp.zeros((1, 128), F32)
        small_ref[pl.ds(240, 16 + 32), :] = jnp.zeros((48, 128), F32)
        small_ref[pl.ds(220, 2), :] = jnp.broadcast_to(
            jnp.sum(d_logit, axis=1, keepdims=True), (2, 128)
        )
        small_ref[pl.ds(222, 2), :] = jnp.zeros((2, 128), F32)
        small_ref[pl.ds(224, 16), :] = jnp.broadcast_to(
            jnp.sum(d_logits, axis=1, keepdims=True), (16, 128)
        )

    def backward(k, store):
        d_out = d_raw[k]
        grad_out = dot_tn(hidden[k], d_out)
        d_pre = (dot_nt(d_out, weights_out(k)) * slope[k]).astype(BF16)
        bias = jnp.sum(d_pre.astype(F32), axis=0, keepdims=True)
        for p in range(4):
            small_ref[pl.ds(8 * (TILES + p) + k, 1), pl.ds(0, PART)] = bias[
                :, PART * p : PART * p + PART
            ]
        grad_in = dot_tn(d_pre, x)
        for p in range(4):
            at = slice(PART * p, PART * p + PART)
            for block in range(4):
                store(p, block, grad_in[at, block * 128 : block * 128 + 128])
            store(p, 4, grad_out[at, :])
        d_in_ref[...] += dot_nn(d_pre, weights_in(k))

    def remote(source, target, sem, place):
        return pltpu.make_async_remote_copy(
            src_ref=source,
            dst_ref=target,
            send_sem=sems.at[sem],
            recv_sem=sems.at[sem + 1],
            device_id=place,
            device_id_type=pl.DeviceIdType.MESH,
        )

    def wait_all(ref, sem):
        pltpu.make_async_copy(ref, ref, sem).wait()

    def quarter(step):
        q = (step + at_y + at_x + part) % 4
        even = 1 - q % 2
        return q, even, even * part + (1 - even) * at_x, even * at_x + (1 - even) * part

    def experts(step, carry):
        q = quarter(step)[0]

        def for_pair(p, block, value):
            pair_send[q, p, pl.ds(PART * block, PART), :] = value.astype(BF16)

        def for_own(p, block, value):
            own_grad[step % 2, p, pl.ds(PART * block, PART), :] = value

        backward(2 * q + 1 - core, for_pair)
        pltpu.make_async_remote_copy(
            src_ref=pair_send.at[q],
            dst_ref=pair_recv.at[q],
            send_sem=sems.at[0],
            recv_sem=pair_sems.at[q],
            device_id=(line + 1 - 2 * core, part),
            device_id_type=pl.DeviceIdType.MESH,
        ).start()

        @pl.when(step > 0)
        def _():
            first_round(step - 1)

        backward(2 * q + core, for_own)
        return carry

    def first_round(step):
        q, even, first, _ = quarter(step)
        wait_all(pair_recv.at[0], pair_sems.at[q])
        for p in range(4):
            total = (own_grad[step % 2, p] + pair_recv[q, p].astype(F32)).astype(BF16)
            for r in range(4):
                piece = total[CHUNK * r : CHUNK * r + CHUNK]
                share_send[q, even * p + (1 - even) * r, even * r + (1 - even) * p] = piece
        for hop in range(1, 4):
            peer = (first + hop) % 4
            pltpu.make_async_remote_copy(
                src_ref=share_send.at[q, peer],
                dst_ref=first_recv.at[q, first],
                send_sem=sems.at[9],
                recv_sem=first_sems.at[q],
                device_id=(line + (1 - even) * 2 * (peer - at_x), even * peer + (1 - even) * part),
                device_id_type=pl.DeviceIdType.MESH,
            ).start()
        first_recv[q, first] = share_send[q, first]

    def second_round(step):
        q, even, _, second = quarter(step)
        three = first_recv.at[0, pl.ds(0, 3)]
        wait_all(three, first_sems.at[q])
        for at in range(4):
            total = first_recv[q, 0, at].astype(F32)
            for f in range(1, 4):
                total = total + first_recv[q, f, at].astype(F32)
            second_send[q, at] = total.astype(BF16)
        for at in range(4):
            target = 2 * (4 * q + even * at + (1 - even) * at_x) + core
            target_part = even * part + (1 - even) * at
            mine = (target == line) & (target_part == part)

            @pl.when(mine)
            def _():
                share_recv[4 * at_y + second] = second_send[q, at]

            @pl.when(jnp.logical_not(mine))
            def _():
                remote(
                    second_send.at[q, at],
                    share_recv.at[4 * at_y + second],
                    1,
                    (target, target_part),
                ).start()

    def tail():
        d_last = d_in_ref[:, pl.ds(DIN - DPROJ, DPROJ)]
        small_ref[pl.ds(200, 16), :] = jnp.zeros((16, 128), F32)
        small_ref[pl.ds(200, DENSE), pl.ds(0, DPROJ)] = dot_nn(feats_ref[...], d_last, EXACT)
        small_ref[pl.ds(216, 1), :] = jnp.zeros((1, 128), F32)
        small_ref[pl.ds(216, 1), pl.ds(0, DPROJ)] = jnp.sum(d_last, axis=0, keepdims=True)
        grad_dense_ref[...] = dot_nt(dw_ref[...], d_last, EXACT)

    def small_pair():
        return pltpu.make_async_remote_copy(
            src_ref=small_ref,
            dst_ref=small_two,
            send_sem=sems.at[5],
            recv_sem=sems.at[6],
            device_id=(line + 1 - 2 * core, part),
            device_id_type=pl.DeviceIdType.MESH,
        )

    adds_small = ((line < 30) & (part == line % 4)) | (line == 30)

    def share_small():
        small_pair().wait()
        small_two[...] = small_two[...] + small_ref[...]

        def share_tile(at, target, p):
            mine = (target == line) & (part == p)

            @pl.when(mine)
            def _():
                small_recv[chip] = small_two[pl.ds(eight(at), 8), :]

            @pl.when(jnp.logical_not(mine))
            def _():
                source = small_two.at[pl.ds(eight(at), 8), :]
                remote(source, small_recv.at[chip], 3, (target, p)).start()

        for a in range(15):
            target = 2 * a + core
            share_tile(8 * target, target, target % 4)

        @pl.when(core == 0)
        def _():
            for p in range(4):
                share_tile(8 * (TILES + p), 30, p)

    def add_up():
        @pl.when(line == TILES - 1)
        def _():
            small_all[...] = jnp.zeros_like(small_all)

        @pl.when(adds_small)
        def _():
            wait_all(small_recv.at[pl.ds(0, CHIPS - 1)], sems.at[4])

            def add_small(at, total):
                return total + small_recv[at]

            small_own[...] = lax.fori_loop(1, CHIPS, add_small, small_recv[0])

            @pl.when(line < 30)
            def _():
                for hop in range(1, 4):
                    remote(small_own, small_all, 10, (line, (part + hop) % 4)).start()

        wait_all(share_recv.at[pl.ds(0, 15)], sems.at[2])
        total = share_recv[0].astype(F32)
        for at in range(1, 16):
            total = total + share_recv[at].astype(F32)
        low = total.astype(BF16)
        for at in range(TILES):
            share_out_ref[at, pl.ds(0, CHUNK), :] = low

    def add_small_up():
        @pl.when((line < 30) & jnp.logical_not(adds_small))
        def _():
            wait_all(small_all, sems.at[11])

        @pl.when(adds_small)
        def _():
            small_all[...] = small_own[...]

        low = two_parts(small_all[...])
        for at in range(TILES):
            share_out_ref[at, pl.ds(CHUNK, 16), :] = low

    def drain():
        wait_all(pair_send, sems.at[0])
        wait_all(first_recv.at[pl.ds(0, 3)], sems.at[9])
        wait_all(share_recv.at[pl.ds(0, 15)], sems.at[1])
        for sends, zero_core in ((15, 1), (19, 0)):
            for mine in (0, 1):

                @pl.when((core == zero_core) & (adds_small == (mine == 1)))
                def _():
                    wait_all(small_recv.at[pl.ds(0, sends - mine)], sems.at[3])

        @pl.when(adds_small & (line < 30))
        def _():
            wait_all(small_recv.at[pl.ds(0, 3)], sems.at[10])

    def spread():
        lane_from = lax.broadcasted_iota(jnp.int32, (128, 128), 0)
        lane_to = lax.broadcasted_iota(jnp.int32, (128, 128), 1)
        for field in range(FIELDS):
            take = lane_from == EMB * (field % 8) + lane_to % EMB
            copies = dot_nn(d_in_ref[:, pl.ds(field // 8 * 128, 128)].astype(BF16), take.astype(F32).astype(BF16))
            rows[pl.ds(field * ROWS_LOC, ROWS_LOC), :] = copies
        rows[pl.ds(LOOKUPS, 8), :] = jnp.zeros((8, 128), F32)
        group = lane_group(1)
        wide_group = lane_group(CAP - COLD)

        def hot(at, carry):
            for n in range(COLD, CAP):
                row = rows[pl.ds(hot_src_ref[at * SLOTS + n], 1), :]
                hot_rows[at, pl.ds(n - COLD, 1), :] = row
            return carry

        second_round(0)
        lax.fori_loop(0, HOT, hot, 0)
        second_round(1)
        hot_rows[HOT] = jnp.zeros((CAP - COLD, 128), F32)

        def group_at(step):
            return (3 * (line // 2) + part + 4 * core + step) % 16

        def collect(step, slots):
            source = group_at(step) * (8 * SLOTS)
            for n in range(COLD):
                total = rows[pl.ds(src_ref[source + n], 1), :]
                for u in range(1, 8):
                    row = rows[pl.ds(src_ref[source + u * SLOTS + n], 1), :]
                    total = jnp.where(group == u, row, total)
                slots[pl.ds(n, 1), :] = total

        def finish(step, slots):
            first = group_at(step) * 8
            total = jnp.zeros((CAP - COLD, 128), F32)
            for u in range(8):
                total = jnp.where(wide_group == u, hot_rows[hot_at_ref[first + u]], total)
            slots[pl.ds(COLD, CAP - COLD), :] = total
            for half in range(2):
                turned = slots[pl.ds(half * 128, 128), :].T.astype(BF16)
                for u in range(8):
                    at = eight((first + u) * GROUPS + EMB * half, EMB)
                    ready[pl.ds(at, EMB), :] = turned[EMB * u : EMB * u + EMB]

        def send(step):
            first = group_at(step) * 8
            for u in range(8):
                dest = first + (me + u) % 8

                @pl.when(dest != me)
                def _():
                    send_block(ready, landing, me, dest, sems.at[7], sems.at[8])

        for slots in (even, odd):
            slots[pl.ds(CAP, SLOTS - CAP), :] = jnp.zeros((SLOTS - CAP, 128), F32)
        share_small()
        second_round(2)
        collect(0, even)
        second_round(3)

        def two_groups(pair, carry):
            step = 2 * pair
            collect(step + 1, odd)
            finish(step, even)
            send(step)
            collect(jnp.minimum(step + 2, 15), even)
            finish(step + 1, odd)
            send(step + 1)
            return carry

        lax.fori_loop(0, 6, two_groups, 0)
        add_up()
        lax.fori_loop(6, 8, two_groups, 0)
        add_small_up()
        wait_blocks(ready, landing, sems.at[7], sems.at[8])
        rows_out_ref[...] = landing[...]
        mine = pl.ds(eight(me * GROUPS, GROUPS), GROUPS)
        rows_out_ref[mine, :] = ready[mine, :]
        drain()

    @pl.when(phase == 0)
    def _():
        greet_all(me)
        lax.fori_loop(0, EXPERTS, forward, 0)

    @pl.when(phase == 1)
    def _():
        head()

    @pl.when(phase == 2)
    def _():
        pl.semaphore_wait(pltpu.get_barrier_semaphore(), OWNERS - 1)
        lax.fori_loop(0, 4, experts, 0)
        first_round(3)
        tail()
        small_pair().start()
        spread()


def model(*operands):
    return pl.pallas_call(
        model_kernel,
        grid=(3,),
        in_specs=[VM] * (len(operands) - 4) + [SM] * 4,
        out_specs=[VM] * 3,
        out_shape=[
            shape((OWNERS * GROUPS, 128), BF16),
            shape((TILES, SHARE, 128), BF16),
            shape((DENSE, ROWS_LOC), F32),
        ],
        scratch_shapes=[
            pltpu.VMEM((8 * (TILES + 4), 128), F32),
            pltpu.VMEM((8 * (TILES + 4), 128), F32),
            pltpu.VMEM((ROWS_LOC, DIN), F32),
            pltpu.VMEM((EXPERTS, ROWS_LOC, HID), BF16),
            pltpu.VMEM((EXPERTS, ROWS_LOC, HID), F32),
            pltpu.VMEM((EXPERTS, ROWS_LOC, EOUT), F32),
            pltpu.VMEM((TASKS * EXPERTS, ROWS_LOC, EOUT), F32),
            pltpu.VMEM((EXPERTS, ROWS_LOC, EOUT), BF16),
            pltpu.VMEM((ROWS_LOC, TASKS * EXPERTS * EOUT), BF16),
            pltpu.VMEM((ROWS_LOC, TASKS * EXPERTS * EOUT), BF16),
            pltpu.VMEM((ROWS_LOC, TASKS * EOUT), F32),
            pltpu.VMEM((48, DIN), F32),
            pltpu.VMEM((2, 4, 4 * CHUNK, 128), F32),
            pltpu.VMEM((4, 4, 4 * CHUNK, 128), BF16),
            pltpu.VMEM((4, 4, 4 * CHUNK, 128), BF16),
            pltpu.VMEM((4, 4, 4, CHUNK, 128), BF16),
            pltpu.VMEM((4, 4, 4, CHUNK, 128), BF16),
            pltpu.VMEM((4, 4, CHUNK, 128), BF16),
            pltpu.VMEM((16, CHUNK, 128), BF16),
            pltpu.VMEM((CHIPS, 8, 128), F32),
            pltpu.VMEM((8, 128), F32),
            pltpu.VMEM((8, 128), F32),
            pltpu.VMEM((LOOKUPS + 8, 128), F32),
            pltpu.VMEM((HOT + 1, CAP - COLD, 128), F32),
            pltpu.VMEM((SLOTS, 128), F32),
            pltpu.VMEM((SLOTS, 128), F32),
            pltpu.VMEM((OWNERS * GROUPS, 128), BF16),
            pltpu.VMEM((OWNERS * GROUPS, 128), BF16),
            pltpu.SemaphoreType.DMA((4,)),
            pltpu.SemaphoreType.DMA((4,)),
            pltpu.SemaphoreType.DMA((12,)),
        ],
        compiler_params=remote_params(MODEL_MIB, 1),
        name="model",
    )(*operands)


def scatter_kernel(
    asked_ref, grads_ref, out_ref, rows_v, groups, rows, sem, even, odd, *sums
):
    split_wanted(asked_ref, rows_v, groups)
    rows_copy = pltpu.make_async_copy(rows_v, rows, sem.at[0])
    rows_copy.start()
    at_group = sublane_group()

    def clear(step, carry):
        for total in sums:
            total[pl.ds(eight(step * 512), 512), :] = jnp.zeros((512, 128), F32)
        return carry

    lax.fori_loop(0, PACKED // 512, clear, 0)
    rows_copy.wait()

    def place(source, found):
        for half in range(2):
            block = grads_ref[pl.ds(eight(source * GROUPS + EMB * half, EMB), EMB), :].astype(F32)
            block = jnp.broadcast_to(block[None], (8, EMB, 128)).reshape(128, 128)
            block = jnp.where(at_group == groups[source, pl.ds(half, 1), :], block, 0.0)
            found[pl.ds(half * 128, 128), :] = block.T

    def add(source, found):
        for n in range(CAP):
            at = pl.ds(rows[source, n // 128, n % 128], 1)
            total = sums[n % SUMS]
            total[at, :] = total[at, :] + found[pl.ds(n, 1), :]

    place(0, even)

    def two_sources(step, carry):
        source = 2 * step
        place(source + 1, odd)
        add(source, even)
        place(jnp.minimum(source + 2, OWNERS - 1), even)
        add(source + 1, odd)
        return carry

    lax.fori_loop(0, OWNERS // 2, two_sources, 0)

    def write(field, carry):
        for part in range(4):
            at = pl.ds(eight(field * 512 + part * 128, 128), 128)
            block = sums[0][at, :]
            for total in sums[1:]:
                block = block + total[at, :]
            block = block.T
            for k in range(8):
                out_ref[field, :, pl.ds(part * 1024 + k * 128, 128)] = block[16 * k : 16 * k + 16]
        return carry

    lax.fori_loop(0, FIELDS, write, 0)


def scatter_add(asked, grads):
    return pl.pallas_call(
        scatter_kernel,
        in_specs=[VM, VM],
        out_specs=VM,
        out_shape=shape((FIELDS, EMB, ROWS_DEV), F32),
        scratch_shapes=split_scratch()
        + [pltpu.VMEM((SLOTS, 128), F32)] * 2
        + [pltpu.VMEM((PACKED + 8, 128), F32)] * SUMS,
        compiler_params=params(58),
        name="scatter_add",
    )(asked, grads)


def unpack_kernel(
    shares_ref,
    w_in_ref,
    w_out_ref,
    w1_ref,
    b_out_ref,
    gate_ref,
    dense_w_ref,
    dense_b_ref,
    b1_ref,
    w2_ref,
    b2_ref,
    gate_b_ref,
    b_in_ref,
):
    def expert(k, carry):
        lines = [2 * (4 * (k // 2) + at) + k % 2 for at in range(4)]
        rows = [shares_ref[at, pl.ds(0, CHUNK), :] for at in lines]
        rows = jnp.concatenate(rows, axis=0).astype(F32)
        for block in range(4):
            w_in_ref[k, :, pl.ds(block * 128, 128)] = rows[PART * block : PART * block + PART]
        w_out_ref[k] = rows[4 * PART : 5 * PART]
        return carry

    lax.fori_loop(0, EXPERTS, expert, 0)

    def tile(at):
        return one_of(shares_ref[at, pl.ds(CHUNK, 16), :])

    for at in range(16):
        w1_ref[at // 8, pl.ds(at % 8 * 8, 8), :] = tile(at)
    b_out_ref[...] = tile(16)
    for at in range(8):
        gate_ref[pl.ds(at % 2 * 8, 8), pl.ds(at // 2 * 128, 128)] = tile(17 + at)
    dense_w_ref[pl.ds(0, 8), :] = tile(25)[:, 0:DPROJ]
    dense_w_ref[pl.ds(8, DENSE - 8), :] = tile(26)[0 : DENSE - 8, 0:DPROJ]
    rest = tile(27)
    dense_b_ref[...] = rest[0:1, 0:DPROJ]
    for t in range(TASKS):
        b1_ref[pl.ds(t, 1), :] = rest[1:2, t * THID : t * THID + THID]
        w2_ref[pl.ds(t, 1), :] = rest[2:3, t * THID : t * THID + THID]
    lane = lax.broadcasted_iota(jnp.int32, (1, 128), 1)
    b2_ref[...] = jnp.where(lane == 0, rest[4:5], rest[5:6])[:, 0:TASKS]
    own = lax.broadcasted_iota(jnp.int32, (8, 128), 0) == lax.broadcasted_iota(
        jnp.int32, (8, 128), 1
    )
    for t in range(TASKS):
        value = jnp.sum(jnp.where(own, tile(28 + t), 0.0), axis=0, keepdims=True)
        gate_b_ref[pl.ds(t, 1), :] = value[:, 0:EXPERTS]
    b_in_ref[...] = tile(30)[:, 0:PART]


def unpack(shares):
    return pl.pallas_call(
        unpack_kernel,
        in_specs=[VM],
        out_specs=[VM] * 12,
        out_shape=[
            shape((EXPERTS, PART, DIN), F32),
            shape((EXPERTS, PART, EOUT), F32),
            shape((TASKS, THID, EOUT), F32),
            shape((EXPERTS, EOUT), F32),
            shape((TASKS * EXPERTS, DIN), F32),
            shape((DENSE, DPROJ), F32),
            shape((1, DPROJ), F32),
            shape((TASKS, THID), F32),
            shape((TASKS, THID), F32),
            shape((1, TASKS), F32),
            shape((TASKS, EXPERTS), F32),
            shape((EXPERTS, PART), F32),
        ],
        compiler_params=params(32),
        name="unpack",
    )(shares)


def body(
    sparse_ids,
    dense_feats,
    labels,
    tables,
    dense_w,
    dense_b,
    w_in,
    b_in,
    w_out,
    b_out,
    gate_w,
    gate_b,
    tower_w1,
    tower_b1,
    tower_w2,
    tower_b2,
):
    w_in_all = lax.all_gather(w_in.transpose(0, 2, 1), "mp", axis=0)
    ids = sparse_ids.T
    field = lax.broadcasted_iota(jnp.int32, (FIELDS, ROWS_LOC), 0)
    example = lax.broadcasted_iota(jnp.int32, (FIELDS, ROWS_LOC), 1)
    row = ids & (ROWS_DEV - 1)
    packed = field * 512 + (row >> 10) * 128 + (row & 127)
    key = ((ids >> 12) << 14) | (field * ROWS_LOC + example)
    load = (packed << 3) | ((row >> 7) & 7)
    keys, loads = lax.sort((key.reshape(-1), load.reshape(-1)), num_keys=1, is_stable=False)
    requests, sources, hot_sources, hot, hot_at = route(keys.reshape(-1, 128), loads.reshape(-1, 128))
    sources = sources.reshape(-1)
    answer, asked, w_out_all, b_in_all = look_up(
        requests, tables.transpose(0, 2, 1), w_out, b_in
    )
    feats_t = dense_feats.T
    inputs = embed(sources, hot, ids, answer, feats_t, dense_w, dense_b.reshape(1, DPROJ))
    incoming, share, grad_dense = model(
        inputs,
        labels.T,
        feats_t,
        dense_w,
        w_in_all,
        w_out_all,
        b_in_all,
        b_out,
        gate_w.transpose(0, 2, 1).reshape(TASKS * EXPERTS, DIN),
        gate_b,
        tower_w1.transpose(0, 2, 1),
        tower_b1,
        tower_w2,
        tower_b2,
        sources,
        hot_sources.reshape(-1),
        hot_at,
    )
    shares = lax.all_to_all(share, "dp", split_axis=0, concat_axis=0, tiled=True)
    grad_tables = scatter_add(asked, incoming).transpose(0, 2, 1)
    (
        grad_w_in,
        grad_w_out,
        grad_w1,
        grad_b_out,
        grad_gate_w,
        grad_dense_w,
        grad_dense_b,
        grad_b1,
        grad_w2,
        grad_b2,
        grad_gate_b,
        grad_b_in,
    ) = unpack(shares)
    return (
        grad_tables,
        grad_dense_w,
        grad_dense_b.reshape(DPROJ),
        grad_w_in.transpose(0, 2, 1),
        grad_b_in,
        grad_w_out,
        grad_b_out,
        grad_gate_w.reshape(TASKS, EXPERTS, DIN).transpose(0, 2, 1),
        grad_gate_b,
        grad_w1.transpose(0, 2, 1),
        grad_b1,
        grad_w2,
        grad_b2.reshape(TASKS),
        grad_dense.T,
    )


def solution(mesh):
    return jax.shard_map(
        body,
        mesh=mesh,
        in_specs=(
            P(ALL, None),
            P(ALL, None),
            P(ALL, None),
            P(None, ALL, None),
            P(),
            P(),
            P(None, None, "mp"),
            P(None, "mp"),
            P(None, "mp", None),
            P(),
            P(),
            P(),
            P(),
            P(),
            P(),
            P(),
        ),
        out_specs=(
            P(None, ALL, None),
            P(),
            P(),
            P(None, None, "mp"),
            P(None, "mp"),
            P(None, "mp", None),
            P(),
            P(),
            P(),
            P(),
            P(),
            P(),
            P(),
            P(ALL, None),
        ),
        check_vma=False,
    )
```

```python
import functools

import jax
import jax.numpy as jnp
from jax import lax
from jax.experimental import pallas as pl
from jax.experimental.pallas import tpu as pltpu
from jax.sharding import PartitionSpec as P

ALL = ("dp", "mp")
EXACT = lax.Precision.HIGHEST
F32 = jnp.float32
BF16 = jnp.bfloat16

OWNERS = 128
FIELDS = 26
EMB = 16
ROWS_LOC = 512
ROWS_DEV = 4096
LOOKUPS = ROWS_LOC * FIELDS
PACKED = FIELDS * ROWS_DEV // 8
CAP = 208
COLD = 96
HOT = 16
SLOTS = 256
GROUPS = SLOTS // 8
EXPERTS = 8
HID = 256
EOUT = 128
TASKS = 2
THID = 64
DIN = 512
DENSE = 13
DPROJ = 96
CHUNK = 80
TILES = 32
CHIPS = OWNERS // 2
SHARE = CHUNK + 16
MODEL_MIB = 50
PART = 64
SUMS = 6

VM = pl.BlockSpec(memory_space=pltpu.VMEM)
SM = pl.BlockSpec(memory_space=pltpu.SMEM)


def params(mib):
    return pltpu.CompilerParams(vmem_limit_bytes=mib * 1024 * 1024)


def shape(dims, dtype):
    return jax.ShapeDtypeStruct(dims, dtype)


def lane_group(rows):
    return lax.broadcasted_iota(jnp.int32, (rows, 128), 1) // EMB


def sublane_group():
    return lax.broadcasted_iota(jnp.int32, (128, 128), 0) // EMB


def eight(index, unit=8):
    return pl.multiple_of(index, unit)


def dot_nt(a, b, precision=None):
    return lax.dot_general(
        a, b, (((1,), (1,)), ((), ())), precision=precision, preferred_element_type=F32
    )


def dot_tn(a, b, precision=None):
    return lax.dot_general(
        a, b, (((0,), (0,)), ((), ())), precision=precision, preferred_element_type=F32
    )


def dot_nn(a, b, precision=None):
    return lax.dot_general(
        a, b, (((1,), (0,)), ((), ())), precision=precision, preferred_element_type=F32
    )


def split3(value):
    high = value.astype(BF16)
    rest = value - high.astype(F32)
    mid = rest.astype(BF16)
    low = (rest - mid.astype(F32)).astype(BF16)
    return high, mid, low


def my_index():
    return lax.axis_index("dp") * lax.axis_size("mp") + lax.axis_index("mp")


def place_of(index):
    return (index // 4, index % 4)


def greet_all(me):
    barrier = pltpu.get_barrier_semaphore()

    def greet(step, carry):
        pl.semaphore_signal(
            barrier,
            inc=1,
            device_id=place_of((me + step + 1) % OWNERS),
            device_id_type=pl.DeviceIdType.MESH,
        )
        return carry

    lax.fori_loop(0, OWNERS - 1, greet, 0)
    return barrier


def block_of(ref, index):
    return ref.at[pl.ds(eight(index * GROUPS, GROUPS), GROUPS), :]


def send_block(ready, landing, me, dest, send_sem, recv_sem):
    pltpu.make_async_remote_copy(
        src_ref=block_of(ready, dest),
        dst_ref=block_of(landing, me),
        send_sem=send_sem,
        recv_sem=recv_sem,
        device_id=place_of(dest),
        device_id_type=pl.DeviceIdType.MESH,
    ).start()


def wait_blocks(ready, landing, send_sem, recv_sem):
    every = pl.ds(0, (OWNERS - 1) * GROUPS)
    pltpu.make_async_copy(ready.at[every, :], ready.at[every, :], send_sem).wait()
    pltpu.make_async_copy(landing.at[every, :], landing.at[every, :], recv_sem).wait()


def remote_params(mib, identity):
    return pltpu.CompilerParams(
        vmem_limit_bytes=mib * 1024 * 1024, collective_id=identity, has_side_effects=True
    )


def route_kernel(
    key_ref,
    load_ref,
    req_ref,
    src_ref,
    hot_src_ref,
    hot_ref,
    hot_at_ref,
    both,
    cut,
    starts_v,
    starts,
    sem,
):
    own = (key_ref[...] & 16383) << 17
    both[pl.ds(0, 104), :] = own | load_ref[...]
    both[pl.ds(104, 8), :] = jnp.zeros((8, 128), jnp.int32)
    owner_at = lax.broadcasted_iota(jnp.int32, (128, 128), 0)

    def count(step, total):
        rows = key_ref[pl.ds(eight(step * 8), 8), :] >> 14
        for at in range(8):
            total = total + (rows[at : at + 1, :] < owner_at).astype(jnp.int32)
        return total

    below = lax.fori_loop(0, 13, count, jnp.zeros((128, 128), jnp.int32))
    first = jnp.sum(below.astype(F32).T, axis=0, keepdims=True).astype(jnp.int32)
    starts_v[...] = jnp.broadcast_to(first, (8, 128))
    copy = pltpu.make_async_copy(starts_v, starts, sem)
    copy.start()
    copy.wait()
    for at in range(2 * HOT):
        hot_ref[at] = 0
    lane = lax.broadcasted_iota(jnp.int32, (1, 128), 1)
    unused = (LOOKUPS << 17) | (PACKED * 8)

    def per_owner(owner, hot_count):
        start = starts[0, owner]
        end = jnp.where(owner == OWNERS - 1, LOOKUPS, starts[0, jnp.minimum(owner + 1, 127)])
        row = start >> 7
        off = start & 127
        pieces = [both[pl.ds(row + at, 1), :] for at in range(3)]
        for half in range(2):
            piece = jnp.where(lane >= off, pieces[half], pieces[half + 1])
            piece = pltpu.roll(piece, (128 - off) & 127, 1)
            piece = jnp.where(lane < end - start - 128 * half, piece, unused)
            cut[pl.ds(2 * owner + half, 1), :] = piece
            hot_src_ref[pl.ds(2 * hot_count + half, 1), :] = piece >> 17
        is_hot = end - start > COLD
        hot_ref[hot_count] = owner
        hot_at_ref[owner] = jnp.where(is_hot & (hot_count < HOT), hot_count, HOT)
        return jnp.minimum(hot_count + is_hot.astype(jnp.int32), 2 * HOT - 1)

    lax.fori_loop(0, OWNERS, per_owner, 0, unroll=8)
    src_ref[...] = cut[...] >> 17
    req_ref[...] = (cut[...] & ((1 << 17) - 1)).reshape(OWNERS, 2, 128)


def route(keys, loads):
    return pl.pallas_call(
        route_kernel,
        in_specs=[VM, VM],
        out_specs=[VM, VM, VM, SM, SM],
        out_shape=[
            shape((OWNERS, 2, 128), jnp.int32),
            shape((2 * OWNERS, 128), jnp.int32),
            shape((4 * HOT, 128), jnp.int32),
            shape((2 * HOT,), jnp.int32),
            shape((OWNERS,), jnp.int32),
        ],
        scratch_shapes=[
            pltpu.VMEM((112, 128), jnp.int32),
            pltpu.VMEM((2 * OWNERS, 128), jnp.int32),
            pltpu.VMEM((8, 128), jnp.int32),
            pltpu.SMEM((8, 128), jnp.int32),
            pltpu.SemaphoreType.DMA,
        ],
        compiler_params=params(8),
        name="route",
    )(keys, loads)


def split_wanted(asked_ref, rows_v, groups):
    rows_v[...] = asked_ref[...] >> 3
    groups[...] = asked_ref[...] & 7


def split_scratch():
    return [
        pltpu.VMEM((OWNERS, 2, 128), jnp.int32),
        pltpu.VMEM((OWNERS, 2, 128), jnp.int32),
        pltpu.SMEM((OWNERS, 2, 128), jnp.int32),
        pltpu.SemaphoreType.DMA((8,)),
    ]


def look_up_kernel(
    wanted_ref,
    tables_ref,
    w_out_ref,
    b_in_ref,
    out_ref,
    asked_ref,
    w_out_all,
    b_in_all,
    b_low,
    b_own,
    fields,
    table,
    rows_v,
    groups,
    rows,
    sem,
    even,
    odd,
    ready,
    field_sem,
    ask_send,
    ask_recv,
    send_sem,
    recv_sem,
    own_sem,
    weight_sems,
):
    me = my_index()
    line = lax.axis_index("dp")
    part = lax.axis_index("mp")

    def field_copy(field):
        return pltpu.make_async_copy(
            tables_ref.at[field], fields.at[field], field_sem.at[field]
        )

    def start_field(field, carry):
        field_copy(field).start()
        return carry

    own_weights = [
        pltpu.make_async_copy(source, target, weight_sems.at[4 + at])
        for at, (source, target) in enumerate(((w_out_ref, w_out_all.at[part]), (b_in_ref, b_low)))
    ]
    for copy in own_weights:
        copy.start()
    lax.fori_loop(0, FIELDS, start_field, 0)
    barrier = greet_all(me)

    def pack(field, carry):
        field_copy(field).wait()
        for part in range(4):
            block = jnp.concatenate(
                [fields[field, :, pl.ds(part * 1024 + k * 128, 128)] for k in range(8)], axis=0
            )
            table[pl.ds(eight(field * 512 + part * 128, 128), 128), :] = block.T
        return carry

    lax.fori_loop(0, 8, pack, 0)
    table[pl.ds(PACKED, 8), :] = jnp.zeros((8, 128), F32)
    asked_ref[me] = wanted_ref[me]
    pl.semaphore_wait(barrier, OWNERS - 1)

    def ask(step, carry):
        owner = (me + step + 1) % OWNERS
        pltpu.make_async_remote_copy(
            src_ref=wanted_ref.at[owner],
            dst_ref=asked_ref.at[me],
            send_sem=ask_send,
            recv_sem=ask_recv,
            device_id=place_of(owner),
            device_id_type=pl.DeviceIdType.MESH,
        ).start()
        return carry

    lax.fori_loop(0, OWNERS - 1, ask, 0)
    for copy in own_weights:
        copy.wait()
    b_own[...] = jnp.zeros_like(b_own)
    b_own[:, pl.ds(0, PART)] = b_low[...].astype(F32)
    b_in_all[part] = b_own[...]

    def weight_copies(step):
        place = (line, (part + step) % 4)
        return [
            pltpu.make_async_remote_copy(
                src_ref=source,
                dst_ref=target.at[part],
                send_sem=weight_sems.at[2 * at],
                recv_sem=weight_sems.at[2 * at + 1],
                device_id=place,
                device_id_type=pl.DeviceIdType.MESH,
            )
            for at, (source, target) in enumerate(((w_out_ref, w_out_all), (b_own, b_in_all)))
        ]

    for step in range(1, 4):
        for copy in weight_copies(step):
            copy.start()
    lax.fori_loop(8, FIELDS, pack, 0)
    others = pl.ds(0, OWNERS - 1)
    pltpu.make_async_copy(asked_ref.at[others], asked_ref.at[others], ask_recv).wait()
    split_wanted(asked_ref, rows_v, groups)

    def rows_copy(step):
        chunk = pl.ds(eight((me // 16 + step) % 8 * 16, 16), 16)
        return pltpu.make_async_copy(rows_v.at[chunk], rows.at[chunk], sem.at[step])

    for step in range(8):
        rows_copy(step).start()
    for step in range(2):
        rows_copy(step).wait()
    at_group = sublane_group()

    def gather(source, found):
        for n in range(CAP):
            at = rows[source, n // 128, n % 128]
            found[pl.ds(n, 1), :] = table[pl.ds(at, 1), :]

    def pick(source, found):
        for half in range(2):
            block = found[pl.ds(half * 128, 128), :].T
            block = jnp.where(at_group == groups[source, pl.ds(half, 1), :], block, 0.0)
            block = jnp.sum(block.reshape(8, EMB, 128), axis=0)
            ready[pl.ds(eight(source * GROUPS + EMB * half, EMB), EMB), :] = block.astype(BF16)

    def send(source):
        send_block(ready, out_ref, me, source, send_sem, recv_sem)

    even[...] = jnp.zeros_like(even)
    odd[...] = jnp.zeros_like(odd)
    gather(me, even)
    gather((me + 1) % OWNERS, odd)
    pick(me, even)
    own = pltpu.make_async_copy(block_of(ready, me), block_of(out_ref, me), own_sem)
    own.start()

    def two_sources(step, carry):
        first = (me + 2 * step + 1) % OWNERS
        second = (me + 2 * step + 2) % OWNERS
        third = (me + 2 * step + 3) % OWNERS
        gather(second, even)
        pick(first, odd)
        send(first)
        gather(third, odd)
        pick(second, even)
        send(second)
        return carry

    lax.fori_loop(0, 6, two_sources, 0)
    for step in range(2, 8):
        rows_copy(step).wait()
    lax.fori_loop(6, OWNERS // 2 - 1, two_sources, 0)
    last = (me + OWNERS - 1) % OWNERS
    pick(last, odd)
    send(last)
    own.wait()
    pltpu.make_async_copy(wanted_ref.at[others], wanted_ref.at[others], ask_send).wait()
    three = pl.ds(0, 3)
    for at, target in enumerate((w_out_all, b_in_all)):
        for sem_at in (2 * at, 2 * at + 1):
            sem = weight_sems.at[sem_at]
            pltpu.make_async_copy(target.at[three], target.at[three], sem).wait()
    wait_blocks(ready, out_ref, send_sem, recv_sem)


def look_up(wanted, tables_t, w_out, b_in):
    return pl.pallas_call(
        look_up_kernel,
        in_specs=[VM] + [pl.BlockSpec(memory_space=pl.ANY)] * 3,
        out_specs=[VM] * 4,
        out_shape=[
            shape((OWNERS * GROUPS, 128), BF16),
            shape((OWNERS, 2, 128), jnp.int32),
            shape((4, EXPERTS, PART, EOUT), BF16),
            shape((4, EXPERTS, 128), F32),
        ],
        scratch_shapes=[
            pltpu.VMEM((EXPERTS, PART), BF16),
            pltpu.VMEM((EXPERTS, 128), F32),
            pltpu.VMEM((FIELDS, EMB, ROWS_DEV), F32),
            pltpu.VMEM((PACKED + 8, 128), F32),
        ]
        + split_scratch()
        + [pltpu.VMEM((SLOTS, 128), F32)] * 2
        + [pltpu.VMEM((OWNERS * GROUPS, 128), BF16)]
        + [pltpu.SemaphoreType.DMA((FIELDS,))]
        + [pltpu.SemaphoreType.DMA] * 5
        + [pltpu.SemaphoreType.DMA((6,))],
        compiler_params=remote_params(48, 0),
        name="look_up",
    )(wanted, tables_t, w_out, b_in)


def embed_kernel(
    src_ref, hot_ref, ids_ref, answer_ref, feats_ref, dw_ref, db_ref, out_ref, slots, rows, x_t
):
    for block in range(32):
        owner, half = block // 2 * 8, block % 2
        parts = [
            answer_ref[pl.ds((owner + u) * GROUPS + EMB * half, EMB), :] for u in range(8)
        ]
        slots[pl.ds(block * 128, 128), :] = jnp.concatenate(parts, axis=0).astype(F32).T

    def cold(step, carry):
        base = step // 6 * SLOTS + step % 6 * 16
        source = step // 6 * (8 * SLOTS) + step % 6 * 16
        for n in range(16):
            row = slots[pl.ds(base + n, 1), :]
            for u in range(8):
                rows[pl.ds(src_ref[source + u * SLOTS + n], 1), :] = row
        return carry

    def hot(at, carry):
        owner = hot_ref[at]
        base = (owner >> 3) * SLOTS
        for n in range(COLD, CAP):
            rows[pl.ds(src_ref[owner * SLOTS + n], 1), :] = slots[pl.ds(base + n, 1), :]
        return carry

    lax.fori_loop(0, OWNERS // 8 * 6, cold, 0)
    lax.fori_loop(0, HOT, hot, 0)
    at_group = sublane_group()

    def field(f, carry):
        group = (ids_ref[pl.ds(f, 1), :] >> 12) & 7
        for part in range(4):
            block = rows[pl.ds(eight(f * ROWS_LOC + part * 128, 128), 128), :].T
            block = jnp.where(at_group == group[:, part * 128 : part * 128 + 128], block, 0.0)
            block = jnp.sum(block.reshape(8, EMB, 128), axis=0)
            x_t[pl.ds(eight(f * EMB, EMB), EMB), pl.ds(part * 128, 128)] = block
        return carry

    lax.fori_loop(0, FIELDS, field, 0)
    top = lax.broadcasted_iota(jnp.int32, (8, DPROJ), 0) == 0
    bias = jnp.where(top, jnp.broadcast_to(db_ref[...], (8, DPROJ)), 0.0)
    x_t[pl.ds(FIELDS * EMB, DPROJ), :] = (
        dot_tn(dw_ref[...], feats_ref[...], EXACT)
        + dot_tn(bias, jnp.ones((8, ROWS_LOC), F32), EXACT)
    )
    out_ref[...] = x_t[...].T.astype(BF16)


def embed(src, hot, ids, answer, feats_t, dense_w, dense_b):
    return pl.pallas_call(
        embed_kernel,
        in_specs=[SM, SM, VM, VM, VM, VM, VM],
        out_specs=VM,
        out_shape=shape((ROWS_LOC, DIN), BF16),
        scratch_shapes=[
            pltpu.VMEM((OWNERS * GROUPS, 128), F32),
            pltpu.VMEM((LOOKUPS + 8, 128), F32),
            pltpu.VMEM((DIN, ROWS_LOC), F32),
        ],
        compiler_params=params(16),
        name="embed",
    )(src, hot, ids, answer, feats_t, dense_w, dense_b)


C0 = 0.7978845608
C1 = 0.7978845608 * 0.044715


def gelu_both(value):
    square = value * value
    bend = jnp.tanh(value * (C0 + C1 * square))
    half = 0.5 * (1.0 + bend)
    slope = half + 0.5 * value * (1.0 - bend * bend) * (C0 + 3.0 * C1 * square)
    return value * half, slope


def two_parts(value):
    high = value.astype(BF16).astype(F32)
    return jnp.concatenate([high, value - high], axis=0).astype(BF16)


def one_of(parts):
    wide = parts.astype(F32)
    return wide[0:8] + wide[8:16]


def model_kernel(
    x_ref,
    labels_ref,
    feats_ref,
    dw_ref,
    w_in_ref,
    w_out_ref,
    b_in_ref,
    b_out_ref,
    gate_w_ref,
    gate_b_ref,
    w1_ref,
    b1_ref,
    w2_ref,
    b2_ref,
    src_ref,
    hot_src_ref,
    hot_at_ref,
    rows_out_ref,
    share_out_ref,
    grad_dense_ref,
    small_ref,
    small_two,
    d_in_ref,
    hidden,
    slope,
    outs,
    probs,
    d_raw,
    products,
    mix,
    stage,
    own_grad,
    pair_send,
    pair_recv,
    share_send,
    first_recv,
    second_send,
    share_recv,
    small_recv,
    small_own,
    small_all,
    rows,
    hot_rows,
    even,
    odd,
    ready,
    landing,
    pair_sems,
    first_sems,
    sems,
):
    x = x_ref[...]
    phase = pl.program_id(0)
    line = lax.axis_index("dp")
    part = lax.axis_index("mp")
    core = line % 2
    chip = line // 2 * 4 + part
    me = my_index()
    at_y, at_x = line // 8, line // 2 % 4

    def weights_in(k):
        return jnp.concatenate(
            [w_in_ref[p, k] for p in range(4)], axis=0
        )

    def weights_out(k):
        return jnp.concatenate(
            [w_out_ref[p, k] for p in range(4)], axis=0
        )

    def forward(k, carry):
        bias = [b_in_ref[p, pl.ds(k, 1), :][:, 0:PART] for p in range(4)]
        pre = dot_nt(x, weights_in(k)) + jnp.concatenate(bias, axis=1)
        act, grad = gelu_both(pre)
        act = act.astype(BF16)
        hidden[k] = act
        slope[k] = grad
        outs[k] = dot_nn(act, weights_out(k)) + b_out_ref[pl.ds(k, 1), :]
        return carry

    def head():
        gate_parts = jnp.concatenate(split3(gate_w_ref[...]), axis=0)
        stage[...] = dot_nt(gate_parts, x)
        own = lax.broadcasted_iota(jnp.int32, (EXPERTS, EXPERTS), 0) == lax.broadcasted_iota(
            jnp.int32, (EXPERTS, EXPERTS), 1
        )
        gate_b = [
            jnp.sum(jnp.where(own, gate_b_ref[pl.ds(t, 1), :], 0.0), axis=1, keepdims=True)
            for t in range(TASKS)
        ]
        logits = stage[0:16] + stage[16:32] + stage[32:48] + jnp.concatenate(gate_b, axis=0)
        logits = logits.reshape(TASKS, EXPERTS, ROWS_LOC)
        gates = jnp.exp(logits - jnp.max(logits, axis=1, keepdims=True))
        gates = gates / jnp.sum(gates, axis=1, keepdims=True)
        gates_t = gates.reshape(TASKS * EXPERTS, ROWS_LOC)
        gate_parts = [part.astype(F32) for part in split3(gates_t)]
        gate_parts.append(jnp.zeros((80, ROWS_LOC), F32))
        gate_columns = jnp.concatenate(gate_parts, axis=0).T.astype(BF16)
        row_at = lax.broadcasted_iota(jnp.int32, (128, 256), 0)
        column_at = lax.broadcasted_iota(jnp.int32, (128, 256), 1) // EOUT
        row_at = jnp.where(row_at < 48, row_at % 16, -1)

        def spread_gates(pair, carry):
            take = (row_at == 2 * pair + column_at).astype(F32).astype(BF16)
            both = dot_nn(gate_columns, take)
            probs[2 * pair] = both[:, 0:EOUT]
            probs[2 * pair + 1] = both[:, EOUT : 2 * EOUT]
            return carry

        lax.fori_loop(0, TASKS * EXPERTS // 2, spread_gates, 0)

        for t in range(TASKS):
            def add(k, total):
                return total + probs[t * EXPERTS + k] * outs[k]

            mix[:, pl.ds(t * EOUT, EOUT)] = lax.fori_loop(
                1, EXPERTS, add, probs[t * EXPERTS] * outs[0]
            )
        mixture = mix[...]
        zero = jnp.zeros((THID, EOUT), F32)
        w1_bd = jnp.concatenate(
            [
                jnp.concatenate([w1_ref[0], zero], axis=1),
                jnp.concatenate([zero, w1_ref[1]], axis=1),
            ],
            axis=0,
        )
        b1 = jnp.concatenate([b1_ref[pl.ds(t, 1), :] for t in range(TASKS)], axis=1)
        upper, upper_slope = gelu_both(dot_nt(mixture, w1_bd, EXACT) + b1)
        none = jnp.zeros((1, THID), F32)
        w2_bd = jnp.concatenate(
            [
                jnp.concatenate([w2_ref[pl.ds(0, 1), :], none], axis=1),
                jnp.concatenate([none, w2_ref[pl.ds(1, 1), :]], axis=1),
            ],
            axis=0,
        )
        task = lax.broadcasted_iota(jnp.int32, (TASKS, ROWS_LOC), 0)
        logit = dot_nt(w2_bd, upper, EXACT) + jnp.where(task == 0, b2_ref[0], b2_ref[1])
        d_logit = jax.nn.sigmoid(logit) - labels_ref[...].astype(F32)
        d_pre1 = dot_tn(d_logit, w2_bd, EXACT) * upper_slope
        grad_w2 = dot_nn(d_logit, upper, EXACT)
        grad_b1 = jnp.sum(d_pre1, axis=0, keepdims=True)
        grad_w1 = dot_tn(d_pre1, mixture, EXACT)
        d_mix = dot_nn(d_pre1, w1_bd, EXACT)
        mix[...] = d_mix

        def back_raw(k, carry):
            d_one = mix[:, pl.ds(0, EOUT)]
            d_two = mix[:, pl.ds(EOUT, EOUT)]
            grad = probs[k] * d_one + probs[EXPERTS + k] * d_two
            small_ref[pl.ds(128 + k, 1), :] = jnp.sum(grad, axis=0, keepdims=True)
            d_raw[k] = grad.astype(BF16)
            value = outs[k]
            for t, d_task in enumerate((d_one, d_two)):
                at = pl.ds(pl.multiple_of((t * EXPERTS + k) * EOUT, EOUT), EOUT)
                products[:, at] = (value * d_task).astype(BF16)
            return carry

        lax.fori_loop(0, EXPERTS, back_raw, 0)

        wide = TASKS * EXPERTS * EOUT
        own_gate = lax.broadcasted_iota(jnp.int32, (wide, 128), 0) // EOUT
        column_gate = lax.broadcasted_iota(jnp.int32, (wide, 128), 1)
        ones = (column_gate == own_gate).astype(F32).astype(BF16)
        d_gates = dot_nn(products[...], ones).T[0:16]
        d_gates = d_gates.reshape(TASKS, EXPERTS, ROWS_LOC)
        mean = jnp.sum(d_gates * gates, axis=1, keepdims=True)
        d_logits = (gates * (d_gates - mean)).reshape(16, ROWS_LOC)
        d_parts = jnp.concatenate(split3(d_logits), axis=0)
        stage[...] = dot_nn(d_parts, x)
        grad_gate = stage[0:16] + stage[16:32] + stage[32:48]
        gate_high, gate_mid, _ = split3(gate_w_ref[...])
        left = jnp.concatenate([d_parts[0:32], d_parts[0:16]], axis=0)
        right = jnp.concatenate([gate_high, gate_high, gate_mid], axis=0)
        d_in_ref[...] = dot_tn(left, right)
        small_ref[pl.ds(0, THID), :] = grad_w1[0:THID, 0:EOUT]
        small_ref[pl.ds(THID, THID), :] = grad_w1[THID : 2 * THID, EOUT : 2 * EOUT]
        for tile in range(4):
            small_ref[pl.ds(136 + 16 * tile, 16), :] = grad_gate[:, tile * 128 : tile * 128 + 128]
        small_ref[pl.ds(217, 1), :] = grad_b1
        lane = lax.broadcasted_iota(jnp.int32, (1, 128), 1)
        small_ref[pl.ds(218, 1), :] = jnp.where(lane < THID, grad_w2[0:1], grad_w2[1:2])
        small_ref[pl.ds(219, 1), :] = jnp.zeros((1, 128), F32)
        small_ref[pl.ds(240, 16 + 32), :] = jnp.zeros((48, 128), F32)
        small_ref[pl.ds(220, 2), :] = jnp.broadcast_to(
            jnp.sum(d_logit, axis=1, keepdims=True), (2, 128)
        )
        small_ref[pl.ds(222, 2), :] = jnp.zeros((2, 128), F32)
        small_ref[pl.ds(224, 16), :] = jnp.broadcast_to(
            jnp.sum(d_logits, axis=1, keepdims=True), (16, 128)
        )

    def backward(k, store):
        d_out = d_raw[k]
        grad_out = dot_tn(hidden[k], d_out)
        d_pre = (dot_nt(d_out, weights_out(k)) * slope[k]).astype(BF16)
        bias = jnp.sum(d_pre.astype(F32), axis=0, keepdims=True)
        for p in range(4):
            small_ref[pl.ds(8 * (TILES + p) + k, 1), pl.ds(0, PART)] = bias[
                :, PART * p : PART * p + PART
            ]
        grad_in = dot_tn(d_pre, x)
        for p in range(4):
            at = slice(PART * p, PART * p + PART)
            for block in range(4):
                store(p, block, grad_in[at, block * 128 : block * 128 + 128])
            store(p, 4, grad_out[at, :])
        d_in_ref[...] += dot_nn(d_pre, weights_in(k))

    def remote(source, target, sem, place):
        return pltpu.make_async_remote_copy(
            src_ref=source,
            dst_ref=target,
            send_sem=sems.at[sem],
            recv_sem=sems.at[sem + 1],
            device_id=place,
            device_id_type=pl.DeviceIdType.MESH,
        )

    def wait_all(ref, sem):
        pltpu.make_async_copy(ref, ref, sem).wait()

    def quarter(step):
        q = (step + at_y + at_x + part) % 4
        even = 1 - q % 2
        return q, even, even * part + (1 - even) * at_x, even * at_x + (1 - even) * part

    def experts(step, carry):
        q = quarter(step)[0]

        def for_pair(p, block, value):
            pair_send[q, p, pl.ds(PART * block, PART), :] = value.astype(BF16)

        def for_own(p, block, value):
            own_grad[step % 2, p, pl.ds(PART * block, PART), :] = value

        backward(2 * q + 1 - core, for_pair)
        pltpu.make_async_remote_copy(
            src_ref=pair_send.at[q],
            dst_ref=pair_recv.at[q],
            send_sem=sems.at[0],
            recv_sem=pair_sems.at[q],
            device_id=(line + 1 - 2 * core, part),
            device_id_type=pl.DeviceIdType.MESH,
        ).start()

        @pl.when(step > 0)
        def _():
            first_round(step - 1)

        backward(2 * q + core, for_own)
        return carry

    def first_round(step):
        q, even, first, _ = quarter(step)
        wait_all(pair_recv.at[0], pair_sems.at[q])
        for p in range(4):
            total = (own_grad[step % 2, p] + pair_recv[q, p].astype(F32)).astype(BF16)
            for r in range(4):
                piece = total[CHUNK * r : CHUNK * r + CHUNK]
                share_send[q, even * p + (1 - even) * r, even * r + (1 - even) * p] = piece
        for hop in range(1, 4):
            peer = (first + hop) % 4
            pltpu.make_async_remote_copy(
                src_ref=share_send.at[q, peer],
                dst_ref=first_recv.at[q, first],
                send_sem=sems.at[9],
                recv_sem=first_sems.at[q],
                device_id=(line + (1 - even) * 2 * (peer - at_x), even * peer + (1 - even) * part),
                device_id_type=pl.DeviceIdType.MESH,
            ).start()
        first_recv[q, first] = share_send[q, first]

    def second_round(step):
        q, even, _, second = quarter(step)
        three = first_recv.at[0, pl.ds(0, 3)]
        wait_all(three, first_sems.at[q])
        for at in range(4):
            total = first_recv[q, 0, at].astype(F32)
            for f in range(1, 4):
                total = total + first_recv[q, f, at].astype(F32)
            second_send[q, at] = total.astype(BF16)
        for at in range(4):
            target = 2 * (4 * q + even * at + (1 - even) * at_x) + core
            target_part = even * part + (1 - even) * at
            mine = (target == line) & (target_part == part)

            @pl.when(mine)
            def _():
                share_recv[4 * at_y + second] = second_send[q, at]

            @pl.when(jnp.logical_not(mine))
            def _():
                remote(
                    second_send.at[q, at],
                    share_recv.at[4 * at_y + second],
                    1,
                    (target, target_part),
                ).start()

    def tail():
        d_last = d_in_ref[:, pl.ds(DIN - DPROJ, DPROJ)]
        small_ref[pl.ds(200, 16), :] = jnp.zeros((16, 128), F32)
        small_ref[pl.ds(200, DENSE), pl.ds(0, DPROJ)] = dot_nn(feats_ref[...], d_last, EXACT)
        small_ref[pl.ds(216, 1), :] = jnp.zeros((1, 128), F32)
        small_ref[pl.ds(216, 1), pl.ds(0, DPROJ)] = jnp.sum(d_last, axis=0, keepdims=True)
        grad_dense_ref[...] = dot_nt(dw_ref[...], d_last, EXACT)

    def small_pair():
        return pltpu.make_async_remote_copy(
            src_ref=small_ref,
            dst_ref=small_two,
            send_sem=sems.at[5],
            recv_sem=sems.at[6],
            device_id=(line + 1 - 2 * core, part),
            device_id_type=pl.DeviceIdType.MESH,
        )

    adds_small = ((line < 30) & (part == line % 4)) | (line == 30)

    def share_small():
        small_pair().wait()
        small_two[...] = small_two[...] + small_ref[...]

        def share_tile(at, target, p):
            mine = (target == line) & (part == p)

            @pl.when(mine)
            def _():
                small_recv[chip] = small_two[pl.ds(eight(at), 8), :]

            @pl.when(jnp.logical_not(mine))
            def _():
                source = small_two.at[pl.ds(eight(at), 8), :]
                remote(source, small_recv.at[chip], 3, (target, p)).start()

        for a in range(15):
            target = 2 * a + core
            share_tile(8 * target, target, target % 4)

        @pl.when(core == 0)
        def _():
            for p in range(4):
                share_tile(8 * (TILES + p), 30, p)

    def add_up():
        @pl.when(line == TILES - 1)
        def _():
            small_all[...] = jnp.zeros_like(small_all)

        @pl.when(adds_small)
        def _():
            wait_all(small_recv.at[pl.ds(0, CHIPS - 1)], sems.at[4])

            def add_small(at, total):
                return total + small_recv[at]

            small_own[...] = lax.fori_loop(1, CHIPS, add_small, small_recv[0])

            @pl.when(line < 30)
            def _():
                for hop in range(1, 4):
                    remote(small_own, small_all, 10, (line, (part + hop) % 4)).start()

        wait_all(share_recv.at[pl.ds(0, 15)], sems.at[2])
        total = share_recv[0].astype(F32)
        for at in range(1, 16):
            total = total + share_recv[at].astype(F32)
        low = total.astype(BF16)
        for at in range(TILES):
            share_out_ref[at, pl.ds(0, CHUNK), :] = low

    def add_small_up():
        @pl.when((line < 30) & jnp.logical_not(adds_small))
        def _():
            wait_all(small_all, sems.at[11])

        @pl.when(adds_small)
        def _():
            small_all[...] = small_own[...]

        low = two_parts(small_all[...])
        for at in range(TILES):
            share_out_ref[at, pl.ds(CHUNK, 16), :] = low

    def drain():
        wait_all(pair_send, sems.at[0])
        wait_all(first_recv.at[pl.ds(0, 3)], sems.at[9])
        wait_all(share_recv.at[pl.ds(0, 15)], sems.at[1])
        for sends, zero_core in ((15, 1), (19, 0)):
            for mine in (0, 1):

                @pl.when((core == zero_core) & (adds_small == (mine == 1)))
                def _():
                    wait_all(small_recv.at[pl.ds(0, sends - mine)], sems.at[3])

        @pl.when(adds_small & (line < 30))
        def _():
            wait_all(small_recv.at[pl.ds(0, 3)], sems.at[10])

    def spread():
        lane_from = lax.broadcasted_iota(jnp.int32, (128, 128), 0)
        lane_to = lax.broadcasted_iota(jnp.int32, (128, 128), 1)
        for field in range(FIELDS):
            take = lane_from == EMB * (field % 8) + lane_to % EMB
            copies = dot_nn(d_in_ref[:, pl.ds(field // 8 * 128, 128)].astype(BF16), take.astype(F32).astype(BF16))
            rows[pl.ds(field * ROWS_LOC, ROWS_LOC), :] = copies
        rows[pl.ds(LOOKUPS, 8), :] = jnp.zeros((8, 128), F32)
        group = lane_group(1)
        wide_group = lane_group(CAP - COLD)

        def hot(at, carry):
            for n in range(COLD, CAP):
                row = rows[pl.ds(hot_src_ref[at * SLOTS + n], 1), :]
                hot_rows[at, pl.ds(n - COLD, 1), :] = row
            return carry

        second_round(0)
        lax.fori_loop(0, HOT, hot, 0)
        second_round(1)
        hot_rows[HOT] = jnp.zeros((CAP - COLD, 128), F32)

        def group_at(step):
            return (3 * (line // 2) + part + 4 * core + step) % 16

        def collect(step, slots):
            source = group_at(step) * (8 * SLOTS)
            for n in range(COLD):
                total = rows[pl.ds(src_ref[source + n], 1), :]
                for u in range(1, 8):
                    row = rows[pl.ds(src_ref[source + u * SLOTS + n], 1), :]
                    total = jnp.where(group == u, row, total)
                slots[pl.ds(n, 1), :] = total

        def finish(step, slots):
            first = group_at(step) * 8
            total = jnp.zeros((CAP - COLD, 128), F32)
            for u in range(8):
                total = jnp.where(wide_group == u, hot_rows[hot_at_ref[first + u]], total)
            slots[pl.ds(COLD, CAP - COLD), :] = total
            for half in range(2):
                turned = slots[pl.ds(half * 128, 128), :].T.astype(BF16)
                for u in range(8):
                    at = eight((first + u) * GROUPS + EMB * half, EMB)
                    ready[pl.ds(at, EMB), :] = turned[EMB * u : EMB * u + EMB]

        def send(step):
            first = group_at(step) * 8
            for u in range(8):
                dest = first + (me + u) % 8

                @pl.when(dest != me)
                def _():
                    send_block(ready, landing, me, dest, sems.at[7], sems.at[8])

        for slots in (even, odd):
            slots[pl.ds(CAP, SLOTS - CAP), :] = jnp.zeros((SLOTS - CAP, 128), F32)
        share_small()
        second_round(2)
        collect(0, even)
        second_round(3)

        def two_groups(pair, carry):
            step = 2 * pair
            collect(step + 1, odd)
            finish(step, even)
            send(step)
            collect(jnp.minimum(step + 2, 15), even)
            finish(step + 1, odd)
            send(step + 1)
            return carry

        lax.fori_loop(0, 8, two_groups, 0)
        add_up()
        add_small_up()
        wait_blocks(ready, landing, sems.at[7], sems.at[8])
        rows_out_ref[...] = landing[...]
        mine = pl.ds(eight(me * GROUPS, GROUPS), GROUPS)
        rows_out_ref[mine, :] = ready[mine, :]
        drain()

    @pl.when(phase == 0)
    def _():
        greet_all(me)
        lax.fori_loop(0, EXPERTS, forward, 0)

    @pl.when(phase == 1)
    def _():
        head()

    @pl.when(phase == 2)
    def _():
        pl.semaphore_wait(pltpu.get_barrier_semaphore(), OWNERS - 1)
        lax.fori_loop(0, 4, experts, 0)
        first_round(3)
        tail()
        small_pair().start()
        spread()


def model(*operands):
    return pl.pallas_call(
        model_kernel,
        grid=(3,),
        in_specs=[VM] * (len(operands) - 4) + [SM] * 4,
        out_specs=[VM] * 3,
        out_shape=[
            shape((OWNERS * GROUPS, 128), BF16),
            shape((TILES, SHARE, 128), BF16),
            shape((DENSE, ROWS_LOC), F32),
        ],
        scratch_shapes=[
            pltpu.VMEM((8 * (TILES + 4), 128), F32),
            pltpu.VMEM((8 * (TILES + 4), 128), F32),
            pltpu.VMEM((ROWS_LOC, DIN), F32),
            pltpu.VMEM((EXPERTS, ROWS_LOC, HID), BF16),
            pltpu.VMEM((EXPERTS, ROWS_LOC, HID), F32),
            pltpu.VMEM((EXPERTS, ROWS_LOC, EOUT), F32),
            pltpu.VMEM((TASKS * EXPERTS, ROWS_LOC, EOUT), F32),
            pltpu.VMEM((EXPERTS, ROWS_LOC, EOUT), BF16),
            pltpu.VMEM((ROWS_LOC, TASKS * EXPERTS * EOUT), BF16),
            pltpu.VMEM((ROWS_LOC, TASKS * EOUT), F32),
            pltpu.VMEM((48, DIN), F32),
            pltpu.VMEM((2, 4, 4 * CHUNK, 128), F32),
            pltpu.VMEM((4, 4, 4 * CHUNK, 128), BF16),
            pltpu.VMEM((4, 4, 4 * CHUNK, 128), BF16),
            pltpu.VMEM((4, 4, 4, CHUNK, 128), BF16),
            pltpu.VMEM((4, 4, 4, CHUNK, 128), BF16),
            pltpu.VMEM((4, 4, CHUNK, 128), BF16),
            pltpu.VMEM((16, CHUNK, 128), BF16),
            pltpu.VMEM((CHIPS, 8, 128), F32),
            pltpu.VMEM((8, 128), F32),
            pltpu.VMEM((8, 128), F32),
            pltpu.VMEM((LOOKUPS + 8, 128), F32),
            pltpu.VMEM((HOT + 1, CAP - COLD, 128), F32),
            pltpu.VMEM((SLOTS, 128), F32),
            pltpu.VMEM((SLOTS, 128), F32),
            pltpu.VMEM((OWNERS * GROUPS, 128), BF16),
            pltpu.VMEM((OWNERS * GROUPS, 128), BF16),
            pltpu.SemaphoreType.DMA((4,)),
            pltpu.SemaphoreType.DMA((4,)),
            pltpu.SemaphoreType.DMA((12,)),
        ],
        compiler_params=remote_params(MODEL_MIB, 1),
        name="model",
    )(*operands)


def scatter_kernel(
    asked_ref, grads_ref, out_ref, rows_v, groups, rows, sem, even, odd, *sums
):
    split_wanted(asked_ref, rows_v, groups)
    rows_copy = pltpu.make_async_copy(rows_v, rows, sem.at[0])
    rows_copy.start()
    at_group = sublane_group()

    def clear(step, carry):
        for total in sums:
            total[pl.ds(eight(step * 512), 512), :] = jnp.zeros((512, 128), F32)
        return carry

    lax.fori_loop(0, PACKED // 512, clear, 0)
    rows_copy.wait()

    def place(source, found):
        for half in range(2):
            block = grads_ref[pl.ds(eight(source * GROUPS + EMB * half, EMB), EMB), :].astype(F32)
            block = jnp.broadcast_to(block[None], (8, EMB, 128)).reshape(128, 128)
            block = jnp.where(at_group == groups[source, pl.ds(half, 1), :], block, 0.0)
            found[pl.ds(half * 128, 128), :] = block.T

    def add(source, found):
        for n in range(CAP):
            at = pl.ds(rows[source, n // 128, n % 128], 1)
            total = sums[n % SUMS]
            total[at, :] = total[at, :] + found[pl.ds(n, 1), :]

    place(0, even)

    def two_sources(step, carry):
        source = 2 * step
        place(source + 1, odd)
        add(source, even)
        place(jnp.minimum(source + 2, OWNERS - 1), even)
        add(source + 1, odd)
        return carry

    lax.fori_loop(0, OWNERS // 2, two_sources, 0)

    def write(field, carry):
        for part in range(4):
            at = pl.ds(eight(field * 512 + part * 128, 128), 128)
            block = sums[0][at, :]
            for total in sums[1:]:
                block = block + total[at, :]
            block = block.T
            for k in range(8):
                out_ref[field, :, pl.ds(part * 1024 + k * 128, 128)] = block[16 * k : 16 * k + 16]
        return carry

    lax.fori_loop(0, FIELDS, write, 0)


def scatter_add(asked, grads):
    return pl.pallas_call(
        scatter_kernel,
        in_specs=[VM, VM],
        out_specs=VM,
        out_shape=shape((FIELDS, EMB, ROWS_DEV), F32),
        scratch_shapes=split_scratch()
        + [pltpu.VMEM((SLOTS, 128), F32)] * 2
        + [pltpu.VMEM((PACKED + 8, 128), F32)] * SUMS,
        compiler_params=params(58),
        name="scatter_add",
    )(asked, grads)


def unpack_kernel(
    shares_ref,
    w_in_ref,
    w_out_ref,
    w1_ref,
    b_out_ref,
    gate_ref,
    dense_w_ref,
    dense_b_ref,
    b1_ref,
    w2_ref,
    b2_ref,
    gate_b_ref,
    b_in_ref,
):
    def expert(k, carry):
        lines = [2 * (4 * (k // 2) + at) + k % 2 for at in range(4)]
        rows = [shares_ref[at, pl.ds(0, CHUNK), :] for at in lines]
        rows = jnp.concatenate(rows, axis=0).astype(F32)
        for block in range(4):
            w_in_ref[k, :, pl.ds(block * 128, 128)] = rows[PART * block : PART * block + PART]
        w_out_ref[k] = rows[4 * PART : 5 * PART]
        return carry

    lax.fori_loop(0, EXPERTS, expert, 0)

    def tile(at):
        return one_of(shares_ref[at, pl.ds(CHUNK, 16), :])

    for at in range(16):
        w1_ref[at // 8, pl.ds(at % 8 * 8, 8), :] = tile(at)
    b_out_ref[...] = tile(16)
    for at in range(8):
        gate_ref[pl.ds(at % 2 * 8, 8), pl.ds(at // 2 * 128, 128)] = tile(17 + at)
    dense_w_ref[pl.ds(0, 8), :] = tile(25)[:, 0:DPROJ]
    dense_w_ref[pl.ds(8, DENSE - 8), :] = tile(26)[0 : DENSE - 8, 0:DPROJ]
    rest = tile(27)
    dense_b_ref[...] = rest[0:1, 0:DPROJ]
    for t in range(TASKS):
        b1_ref[pl.ds(t, 1), :] = rest[1:2, t * THID : t * THID + THID]
        w2_ref[pl.ds(t, 1), :] = rest[2:3, t * THID : t * THID + THID]
    lane = lax.broadcasted_iota(jnp.int32, (1, 128), 1)
    b2_ref[...] = jnp.where(lane == 0, rest[4:5], rest[5:6])[:, 0:TASKS]
    own = lax.broadcasted_iota(jnp.int32, (8, 128), 0) == lax.broadcasted_iota(
        jnp.int32, (8, 128), 1
    )
    for t in range(TASKS):
        value = jnp.sum(jnp.where(own, tile(28 + t), 0.0), axis=0, keepdims=True)
        gate_b_ref[pl.ds(t, 1), :] = value[:, 0:EXPERTS]
    b_in_ref[...] = tile(30)[:, 0:PART]


def unpack(shares):
    return pl.pallas_call(
        unpack_kernel,
        in_specs=[VM],
        out_specs=[VM] * 12,
        out_shape=[
            shape((EXPERTS, PART, DIN), F32),
            shape((EXPERTS, PART, EOUT), F32),
            shape((TASKS, THID, EOUT), F32),
            shape((EXPERTS, EOUT), F32),
            shape((TASKS * EXPERTS, DIN), F32),
            shape((DENSE, DPROJ), F32),
            shape((1, DPROJ), F32),
            shape((TASKS, THID), F32),
            shape((TASKS, THID), F32),
            shape((1, TASKS), F32),
            shape((TASKS, EXPERTS), F32),
            shape((EXPERTS, PART), F32),
        ],
        compiler_params=params(32),
        name="unpack",
    )(shares)


def body(
    sparse_ids,
    dense_feats,
    labels,
    tables,
    dense_w,
    dense_b,
    w_in,
    b_in,
    w_out,
    b_out,
    gate_w,
    gate_b,
    tower_w1,
    tower_b1,
    tower_w2,
    tower_b2,
):
    w_in_all = lax.all_gather(w_in.transpose(0, 2, 1), "mp", axis=0)
    ids = sparse_ids.T
    field = lax.broadcasted_iota(jnp.int32, (FIELDS, ROWS_LOC), 0)
    example = lax.broadcasted_iota(jnp.int32, (FIELDS, ROWS_LOC), 1)
    row = ids & (ROWS_DEV - 1)
    packed = field * 512 + (row >> 10) * 128 + (row & 127)
    key = ((ids >> 12) << 14) | (field * ROWS_LOC + example)
    load = (packed << 3) | ((row >> 7) & 7)
    keys, loads = lax.sort((key.reshape(-1), load.reshape(-1)), num_keys=1, is_stable=False)
    requests, sources, hot_sources, hot, hot_at = route(keys.reshape(-1, 128), loads.reshape(-1, 128))
    sources = sources.reshape(-1)
    answer, asked, w_out_all, b_in_all = look_up(
        requests, tables.transpose(0, 2, 1), w_out, b_in
    )
    feats_t = dense_feats.T
    inputs = embed(sources, hot, ids, answer, feats_t, dense_w, dense_b.reshape(1, DPROJ))
    incoming, share, grad_dense = model(
        inputs,
        labels.T,
        feats_t,
        dense_w,
        w_in_all,
        w_out_all,
        b_in_all,
        b_out,
        gate_w.transpose(0, 2, 1).reshape(TASKS * EXPERTS, DIN),
        gate_b,
        tower_w1.transpose(0, 2, 1),
        tower_b1,
        tower_w2,
        tower_b2,
        sources,
        hot_sources.reshape(-1),
        hot_at,
    )
    shares = lax.all_to_all(share, "dp", split_axis=0, concat_axis=0, tiled=True)
    grad_tables = scatter_add(asked, incoming).transpose(0, 2, 1)
    (
        grad_w_in,
        grad_w_out,
        grad_w1,
        grad_b_out,
        grad_gate_w,
        grad_dense_w,
        grad_dense_b,
        grad_b1,
        grad_w2,
        grad_b2,
        grad_gate_b,
        grad_b_in,
    ) = unpack(shares)
    return (
        grad_tables,
        grad_dense_w,
        grad_dense_b.reshape(DPROJ),
        grad_w_in.transpose(0, 2, 1),
        grad_b_in,
        grad_w_out,
        grad_b_out,
        grad_gate_w.reshape(TASKS, EXPERTS, DIN).transpose(0, 2, 1),
        grad_gate_b,
        grad_w1.transpose(0, 2, 1),
        grad_b1,
        grad_w2,
        grad_b2.reshape(TASKS),
        grad_dense.T,
    )


def solution(mesh):
    return jax.shard_map(
        body,
        mesh=mesh,
        in_specs=(
            P(ALL, None),
            P(ALL, None),
            P(ALL, None),
            P(None, ALL, None),
            P(),
            P(),
            P(None, None, "mp"),
            P(None, "mp"),
            P(None, "mp", None),
            P(),
            P(),
            P(),
            P(),
            P(),
            P(),
            P(),
        ),
        out_specs=(
            P(None, ALL, None),
            P(),
            P(),
            P(None, None, "mp"),
            P(None, "mp"),
            P(None, "mp", None),
            P(),
            P(),
            P(),
            P(),
            P(),
            P(),
            P(),
            P(ALL, None),
        ),
        check_vma=False,
    )
```

```python
import functools

import jax
import jax.numpy as jnp
from jax import lax
from jax.experimental import pallas as pl
from jax.experimental.pallas import tpu as pltpu
from jax.sharding import PartitionSpec as P

ALL = ("dp", "mp")
EXACT = lax.Precision.HIGHEST
F32 = jnp.float32
BF16 = jnp.bfloat16

OWNERS = 128
FIELDS = 26
EMB = 16
ROWS_LOC = 512
ROWS_DEV = 4096
LOOKUPS = ROWS_LOC * FIELDS
PACKED = FIELDS * ROWS_DEV // 8
CAP = 208
NEAR = 90
COLD = 96
HOT = 16
SLOTS = 256
GROUPS = SLOTS // 8
EXPERTS = 8
HID = 256
EOUT = 128
TASKS = 2
THID = 64
DIN = 512
DENSE = 13
DPROJ = 96
CHUNK = 80
TILES = 32
CHIPS = OWNERS // 2
SHARE = CHUNK + 16
MODEL_MIB = 50
PART = 64
SUMS = 6

VM = pl.BlockSpec(memory_space=pltpu.VMEM)
SM = pl.BlockSpec(memory_space=pltpu.SMEM)
ANY = pl.BlockSpec(memory_space=pl.ANY)


def params(mib):
    return pltpu.CompilerParams(vmem_limit_bytes=mib * 1024 * 1024)


def shape(dims, dtype):
    return jax.ShapeDtypeStruct(dims, dtype)


def lane_group(rows):
    return lax.broadcasted_iota(jnp.int32, (rows, 128), 1) // EMB


def sublane_group():
    return lax.broadcasted_iota(jnp.int32, (128, 128), 0) // EMB


def eight(index, unit=8):
    return pl.multiple_of(index, unit)


def dot_nt(a, b, precision=None):
    return lax.dot_general(
        a, b, (((1,), (1,)), ((), ())), precision=precision, preferred_element_type=F32
    )


def dot_tn(a, b, precision=None):
    return lax.dot_general(
        a, b, (((0,), (0,)), ((), ())), precision=precision, preferred_element_type=F32
    )


def dot_nn(a, b, precision=None):
    return lax.dot_general(
        a, b, (((1,), (0,)), ((), ())), precision=precision, preferred_element_type=F32
    )


def split3(value):
    high = value.astype(BF16)
    rest = value - high.astype(F32)
    mid = rest.astype(BF16)
    low = (rest - mid.astype(F32)).astype(BF16)
    return high, mid, low


def my_index():
    return lax.axis_index("dp") * lax.axis_size("mp") + lax.axis_index("mp")


def place_of(index):
    return (index // 4, index % 4)


def greet_all(me):
    barrier = pltpu.get_barrier_semaphore()

    def greet(step, carry):
        pl.semaphore_signal(
            barrier,
            inc=1,
            device_id=place_of((me + step + 1) % OWNERS),
            device_id_type=pl.DeviceIdType.MESH,
        )
        return carry

    lax.fori_loop(0, OWNERS - 1, greet, 0)
    return barrier


def block_of(ref, index):
    return ref.at[pl.ds(eight(index * GROUPS, GROUPS), GROUPS), :]


def send_block(ready, landing, me, dest, send_sem, recv_sem):
    pltpu.make_async_remote_copy(
        src_ref=block_of(ready, dest),
        dst_ref=block_of(landing, me),
        send_sem=send_sem,
        recv_sem=recv_sem,
        device_id=place_of(dest),
        device_id_type=pl.DeviceIdType.MESH,
    ).start()


def wait_blocks(ready, landing, send_sem, recv_sem):
    every = pl.ds(0, (OWNERS - 1) * GROUPS)
    pltpu.make_async_copy(ready.at[every, :], ready.at[every, :], send_sem).wait()
    pltpu.make_async_copy(landing.at[every, :], landing.at[every, :], recv_sem).wait()


def remote_params(mib, identity):
    return pltpu.CompilerParams(
        vmem_limit_bytes=mib * 1024 * 1024, collective_id=identity, has_side_effects=True
    )


def route_kernel(
    key_ref,
    load_ref,
    req_ref,
    src_ref,
    hot_src_ref,
    hot_ref,
    hot_at_ref,
    both,
    cut,
    starts_v,
    starts,
    sem,
):
    own = (key_ref[...] & 16383) << 17
    both[pl.ds(0, 104), :] = own | load_ref[...]
    both[pl.ds(104, 8), :] = jnp.zeros((8, 128), jnp.int32)
    owner_at = lax.broadcasted_iota(jnp.int32, (128, 128), 0)

    def count(step, total):
        rows = key_ref[pl.ds(eight(step * 8), 8), :] >> 14
        for at in range(8):
            total = total + (rows[at : at + 1, :] < owner_at).astype(jnp.int32)
        return total

    below = lax.fori_loop(0, 13, count, jnp.zeros((128, 128), jnp.int32))
    first = jnp.sum(below.astype(F32).T, axis=0, keepdims=True).astype(jnp.int32)
    starts_v[...] = jnp.broadcast_to(first, (8, 128))
    copy = pltpu.make_async_copy(starts_v, starts, sem)
    copy.start()
    copy.wait()
    for at in range(2 * HOT):
        hot_ref[at] = 0
    lane = lax.broadcasted_iota(jnp.int32, (1, 128), 1)
    unused = (LOOKUPS << 17) | (PACKED * 8)

    def per_owner(owner, hot_count):
        start = starts[0, owner]
        end = jnp.where(owner == OWNERS - 1, LOOKUPS, starts[0, jnp.minimum(owner + 1, 127)])
        row = start >> 7
        off = start & 127
        pieces = [both[pl.ds(row + at, 1), :] for at in range(3)]
        for half in range(2):
            piece = jnp.where(lane >= off, pieces[half], pieces[half + 1])
            piece = pltpu.roll(piece, (128 - off) & 127, 1)
            piece = jnp.where(lane < end - start - 128 * half, piece, unused)
            cut[pl.ds(2 * owner + half, 1), :] = piece
            hot_src_ref[pl.ds(2 * hot_count + half, 1), :] = piece >> 17
        is_hot = end - start > COLD
        hot_ref[hot_count] = owner
        hot_at_ref[owner] = jnp.where(is_hot & (hot_count < HOT), hot_count, HOT)
        return jnp.minimum(hot_count + is_hot.astype(jnp.int32), 2 * HOT - 1)

    lax.fori_loop(0, OWNERS, per_owner, 0, unroll=8)
    src_ref[...] = cut[...] >> 17
    req_ref[...] = (cut[...] & ((1 << 17) - 1)).reshape(OWNERS, 2, 128)


def route(keys, loads):
    return pl.pallas_call(
        route_kernel,
        in_specs=[VM, VM],
        out_specs=[VM, VM, VM, SM, SM],
        out_shape=[
            shape((OWNERS, 2, 128), jnp.int32),
            shape((2 * OWNERS, 128), jnp.int32),
            shape((4 * HOT, 128), jnp.int32),
            shape((2 * HOT,), jnp.int32),
            shape((OWNERS,), jnp.int32),
        ],
        scratch_shapes=[
            pltpu.VMEM((112, 128), jnp.int32),
            pltpu.VMEM((2 * OWNERS, 128), jnp.int32),
            pltpu.VMEM((8, 128), jnp.int32),
            pltpu.SMEM((8, 128), jnp.int32),
            pltpu.SemaphoreType.DMA,
        ],
        compiler_params=params(8),
        name="route",
    )(keys, loads)


def split_wanted(asked_ref, rows_v, groups):
    rows_v[...] = asked_ref[...] >> 3
    groups[...] = asked_ref[...] & 7


def split_scratch():
    return [
        pltpu.VMEM((OWNERS, 2, 128), jnp.int32),
        pltpu.VMEM((OWNERS, 2, 128), jnp.int32),
        pltpu.SMEM((OWNERS, 2, 128), jnp.int32),
        pltpu.SemaphoreType.DMA((8,)),
    ]


def look_up_kernel(
    wanted_ref,
    tables_ref,
    w_out_ref,
    b_in_ref,
    out_ref,
    asked_ref,
    w_out_all,
    b_in_all,
    b_low,
    b_own,
    fields,
    table,
    rows_v,
    groups,
    rows,
    sem,
    even,
    odd,
    ready,
    field_sem,
    ask_send,
    ask_recv,
    send_sem,
    recv_sem,
    own_sem,
    weight_sems,
):
    me = my_index()
    line = lax.axis_index("dp")
    part = lax.axis_index("mp")

    def field_copy(field):
        return pltpu.make_async_copy(
            tables_ref.at[field], fields.at[field], field_sem.at[field]
        )

    def start_field(field, carry):
        field_copy(field).start()
        return carry

    own_weights = [
        pltpu.make_async_copy(source, target, weight_sems.at[4 + at])
        for at, (source, target) in enumerate(((w_out_ref, w_out_all.at[part]), (b_in_ref, b_low)))
    ]
    for copy in own_weights:
        copy.start()
    lax.fori_loop(0, FIELDS, start_field, 0)
    barrier = greet_all(me)

    def pack(field, carry):
        field_copy(field).wait()
        for part in range(4):
            block = jnp.concatenate(
                [fields[field, :, pl.ds(part * 1024 + k * 128, 128)] for k in range(8)], axis=0
            )
            table[pl.ds(eight(field * 512 + part * 128, 128), 128), :] = block.T
        return carry

    lax.fori_loop(0, 8, pack, 0)
    table[pl.ds(PACKED, 8), :] = jnp.zeros((8, 128), F32)
    asked_ref[me] = wanted_ref[me]
    pl.semaphore_wait(barrier, OWNERS - 1)

    def ask(step, carry):
        owner = (me + step + 1) % OWNERS
        pltpu.make_async_remote_copy(
            src_ref=wanted_ref.at[owner],
            dst_ref=asked_ref.at[me],
            send_sem=ask_send,
            recv_sem=ask_recv,
            device_id=place_of(owner),
            device_id_type=pl.DeviceIdType.MESH,
        ).start()
        return carry

    lax.fori_loop(0, OWNERS - 1, ask, 0)
    for copy in own_weights:
        copy.wait()
    b_own[...] = jnp.zeros_like(b_own)
    b_own[:, pl.ds(0, PART)] = b_low[...].astype(F32)
    b_in_all[part] = b_own[...]

    def weight_copies(step):
        place = (line, (part + step) % 4)
        return [
            pltpu.make_async_remote_copy(
                src_ref=source,
                dst_ref=target.at[part],
                send_sem=weight_sems.at[2 * at],
                recv_sem=weight_sems.at[2 * at + 1],
                device_id=place,
                device_id_type=pl.DeviceIdType.MESH,
            )
            for at, (source, target) in enumerate(((w_out_ref, w_out_all), (b_own, b_in_all)))
        ]

    for step in range(1, 4):
        for copy in weight_copies(step):
            copy.start()
    lax.fori_loop(8, FIELDS, pack, 0)
    others = pl.ds(0, OWNERS - 1)
    pltpu.make_async_copy(asked_ref.at[others], asked_ref.at[others], ask_recv).wait()
    split_wanted(asked_ref, rows_v, groups)

    def rows_copy(step):
        chunk = pl.ds(eight((me // 16 + step) % 8 * 16, 16), 16)
        return pltpu.make_async_copy(rows_v.at[chunk], rows.at[chunk], sem.at[step])

    for step in range(8):
        rows_copy(step).start()
    for step in range(2):
        rows_copy(step).wait()
    at_group = sublane_group()

    def gather(source, found):
        for n in range(CAP):
            at = rows[source, n // 128, n % 128]
            found[pl.ds(n, 1), :] = table[pl.ds(at, 1), :]

    def pick(source, found):
        for half in range(2):
            block = found[pl.ds(half * 128, 128), :].T
            block = jnp.where(at_group == groups[source, pl.ds(half, 1), :], block, 0.0)
            block = jnp.sum(block.reshape(8, EMB, 128), axis=0)
            ready[pl.ds(eight(source * GROUPS + EMB * half, EMB), EMB), :] = block.astype(BF16)

    def send(source):
        send_block(ready, out_ref, me, source, send_sem, recv_sem)

    even[...] = jnp.zeros_like(even)
    odd[...] = jnp.zeros_like(odd)
    gather(me, even)
    gather((me + 1) % OWNERS, odd)
    pick(me, even)
    own = pltpu.make_async_copy(block_of(ready, me), block_of(out_ref, me), own_sem)
    own.start()

    def two_sources(step, carry):
        first = (me + 2 * step + 1) % OWNERS
        second = (me + 2 * step + 2) % OWNERS
        third = (me + 2 * step + 3) % OWNERS
        gather(second, even)
        pick(first, odd)
        send(first)
        gather(third, odd)
        pick(second, even)
        send(second)
        return carry

    lax.fori_loop(0, 6, two_sources, 0)
    for step in range(2, 8):
        rows_copy(step).wait()
    lax.fori_loop(6, OWNERS // 2 - 1, two_sources, 0)
    last = (me + OWNERS - 1) % OWNERS
    pick(last, odd)
    send(last)
    own.wait()
    pltpu.make_async_copy(wanted_ref.at[others], wanted_ref.at[others], ask_send).wait()
    three = pl.ds(0, 3)
    for at, target in enumerate((w_out_all, b_in_all)):
        for sem_at in (2 * at, 2 * at + 1):
            sem = weight_sems.at[sem_at]
            pltpu.make_async_copy(target.at[three], target.at[three], sem).wait()
    wait_blocks(ready, out_ref, send_sem, recv_sem)


def look_up(wanted, tables_t, w_out, b_in):
    return pl.pallas_call(
        look_up_kernel,
        in_specs=[VM] + [pl.BlockSpec(memory_space=pl.ANY)] * 3,
        out_specs=[VM] * 4,
        out_shape=[
            shape((OWNERS * GROUPS, 128), BF16),
            shape((OWNERS, 2, 128), jnp.int32),
            shape((4, EXPERTS, PART, EOUT), BF16),
            shape((4, EXPERTS, 128), F32),
        ],
        scratch_shapes=[
            pltpu.VMEM((EXPERTS, PART), BF16),
            pltpu.VMEM((EXPERTS, 128), F32),
            pltpu.VMEM((FIELDS, EMB, ROWS_DEV), F32),
            pltpu.VMEM((PACKED + 8, 128), F32),
        ]
        + split_scratch()
        + [pltpu.VMEM((SLOTS, 128), F32)] * 2
        + [pltpu.VMEM((OWNERS * GROUPS, 128), BF16)]
        + [pltpu.SemaphoreType.DMA((FIELDS,))]
        + [pltpu.SemaphoreType.DMA] * 5
        + [pltpu.SemaphoreType.DMA((6,))],
        compiler_params=remote_params(48, 0),
        name="look_up",
    )(wanted, tables_t, w_out, b_in)


def embed_kernel(
    source_ref,
    hot_ref,
    ids_ref,
    answer_ref,
    feats_ref,
    dw_ref,
    db_ref,
    out_ref,
    slots,
    rows,
    x_t,
    src_ref,
    sem,
):
    copy = pltpu.make_async_copy(source_ref, src_ref, sem)
    copy.start()
    for block in range(32):
        owner, half = block // 2 * 8, block % 2
        parts = [
            answer_ref[pl.ds((owner + u) * GROUPS + EMB * half, EMB), :] for u in range(8)
        ]
        slots[pl.ds(block * 128, 128), :] = jnp.concatenate(parts, axis=0).astype(F32).T

    copy.wait()

    def cold(step, carry):
        base = step // 6 * SLOTS + step % 6 * (NEAR // 6)
        source = step // 6 * (8 * SLOTS) + step % 6 * (NEAR // 6)
        for n in range(NEAR // 6):
            row = slots[pl.ds(base + n, 1), :]
            for u in range(8):
                rows[pl.ds(src_ref[source + u * SLOTS + n], 1), :] = row
        return carry

    def hot(at, carry):
        owner = hot_ref[at]
        base = (owner >> 3) * SLOTS
        for n in range(NEAR, CAP):
            rows[pl.ds(src_ref[owner * SLOTS + n], 1), :] = slots[pl.ds(base + n, 1), :]
        return carry

    lax.fori_loop(0, OWNERS // 8 * 6, cold, 0)
    lax.fori_loop(0, HOT, hot, 0)
    at_group = sublane_group()

    def field(f, carry):
        group = (ids_ref[pl.ds(f, 1), :] >> 12) & 7
        for part in range(4):
            block = rows[pl.ds(eight(f * ROWS_LOC + part * 128, 128), 128), :].T
            block = jnp.where(at_group == group[:, part * 128 : part * 128 + 128], block, 0.0)
            block = jnp.sum(block.reshape(8, EMB, 128), axis=0)
            x_t[pl.ds(eight(f * EMB, EMB), EMB), pl.ds(part * 128, 128)] = block
        return carry

    lax.fori_loop(0, FIELDS, field, 0)
    top = lax.broadcasted_iota(jnp.int32, (8, DPROJ), 0) == 0
    bias = jnp.where(top, jnp.broadcast_to(db_ref[...], (8, DPROJ)), 0.0)
    x_t[pl.ds(FIELDS * EMB, DPROJ), :] = (
        dot_tn(dw_ref[...], feats_ref[...], EXACT)
        + dot_tn(bias, jnp.ones((8, ROWS_LOC), F32), EXACT)
    )
    out_ref[...] = x_t[...].T.astype(BF16)


def embed(src, hot, ids, answer, feats_t, dense_w, dense_b):
    return pl.pallas_call(
        embed_kernel,
        in_specs=[ANY, SM, VM, VM, VM, VM, VM],
        out_specs=VM,
        out_shape=shape((ROWS_LOC, DIN), BF16),
        scratch_shapes=[
            pltpu.VMEM((OWNERS * GROUPS, 128), F32),
            pltpu.VMEM((LOOKUPS + 8, 128), F32),
            pltpu.VMEM((DIN, ROWS_LOC), F32),
            pltpu.SMEM((OWNERS * SLOTS,), jnp.int32),
            pltpu.SemaphoreType.DMA,
        ],
        compiler_params=params(16),
        name="embed",
    )(src, hot, ids, answer, feats_t, dense_w, dense_b)


C0 = 0.7978845608
C1 = 0.7978845608 * 0.044715


def gelu_both(value):
    square = value * value
    bend = jnp.tanh(value * (C0 + C1 * square))
    half = 0.5 * (1.0 + bend)
    slope = half + 0.5 * value * (1.0 - bend * bend) * (C0 + 3.0 * C1 * square)
    return value * half, slope


def two_parts(value):
    high = value.astype(BF16).astype(F32)
    return jnp.concatenate([high, value - high], axis=0).astype(BF16)


def one_of(parts):
    wide = parts.astype(F32)
    return wide[0:8] + wide[8:16]


def model_kernel(
    x_ref,
    labels_ref,
    feats_ref,
    dw_ref,
    w_in_hbm,
    w_out_hbm,
    b_in_ref,
    b_out_ref,
    gate_w_ref,
    gate_b_ref,
    w1_ref,
    b1_ref,
    w2_ref,
    b2_ref,
    hot_at_ref,
    src_hbm,
    hot_src_hbm,
    rows_out_ref,
    share_out_ref,
    grad_dense_ref,
    small_ref,
    small_two,
    d_in_ref,
    hidden,
    slope,
    outs,
    probs,
    d_raw,
    products,
    mix,
    stage,
    own_grad,
    pair_send,
    pair_recv,
    share_send,
    first_recv,
    second_send,
    share_recv,
    small_recv,
    small_own,
    small_all,
    rows,
    hot_rows,
    even,
    odd,
    ready,
    landing,
    w_in_ref,
    w_out_ref,
    src_ref,
    hot_src_ref,
    load_sems,
    pair_sems,
    first_sems,
    sems,
):
    x = x_ref[...]
    phase = pl.program_id(0)
    line = lax.axis_index("dp")
    part = lax.axis_index("mp")
    core = line % 2
    chip = line // 2 * 4 + part
    me = my_index()
    at_y, at_x = line // 8, line // 2 % 4

    def load_w_in(k):
        return pltpu.make_async_copy(w_in_hbm.at[:, k], w_in_ref.at[:, k], load_sems.at[k])

    loads = [
        pltpu.make_async_copy(source, target, load_sems.at[EXPERTS + at])
        for at, (source, target) in enumerate(
            ((w_out_hbm, w_out_ref), (src_hbm, src_ref), (hot_src_hbm, hot_src_ref))
        )
    ]

    def weights_in(k):
        return jnp.concatenate(
            [w_in_ref[p, k] for p in range(4)], axis=0
        )

    def weights_out(k):
        return jnp.concatenate(
            [w_out_ref[p, k] for p in range(4)], axis=0
        )

    def forward(k, carry):
        load_w_in(k).wait()
        bias = [b_in_ref[p, pl.ds(k, 1), :][:, 0:PART] for p in range(4)]
        pre = dot_nt(x, weights_in(k)) + jnp.concatenate(bias, axis=1)
        act, grad = gelu_both(pre)
        act = act.astype(BF16)
        hidden[k] = act
        slope[k] = grad
        outs[k] = dot_nn(act, weights_out(k)) + b_out_ref[pl.ds(k, 1), :]
        return carry

    def head():
        gate_parts = jnp.concatenate(split3(gate_w_ref[...]), axis=0)
        stage[...] = dot_nt(gate_parts, x)
        own = lax.broadcasted_iota(jnp.int32, (EXPERTS, EXPERTS), 0) == lax.broadcasted_iota(
            jnp.int32, (EXPERTS, EXPERTS), 1
        )
        gate_b = [
            jnp.sum(jnp.where(own, gate_b_ref[pl.ds(t, 1), :], 0.0), axis=1, keepdims=True)
            for t in range(TASKS)
        ]
        logits = stage[0:16] + stage[16:32] + stage[32:48] + jnp.concatenate(gate_b, axis=0)
        logits = logits.reshape(TASKS, EXPERTS, ROWS_LOC)
        gates = jnp.exp(logits - jnp.max(logits, axis=1, keepdims=True))
        gates = gates / jnp.sum(gates, axis=1, keepdims=True)
        gates_t = gates.reshape(TASKS * EXPERTS, ROWS_LOC)
        gate_parts = [part.astype(F32) for part in split3(gates_t)]
        gate_parts.append(jnp.zeros((80, ROWS_LOC), F32))
        gate_columns = jnp.concatenate(gate_parts, axis=0).T.astype(BF16)
        row_at = lax.broadcasted_iota(jnp.int32, (128, 256), 0)
        column_at = lax.broadcasted_iota(jnp.int32, (128, 256), 1) // EOUT
        row_at = jnp.where(row_at < 48, row_at % 16, -1)

        def spread_gates(pair, carry):
            take = (row_at == 2 * pair + column_at).astype(F32).astype(BF16)
            both = dot_nn(gate_columns, take)
            probs[2 * pair] = both[:, 0:EOUT]
            probs[2 * pair + 1] = both[:, EOUT : 2 * EOUT]
            return carry

        lax.fori_loop(0, TASKS * EXPERTS // 2, spread_gates, 0)

        for t in range(TASKS):
            def add(k, total):
                return total + probs[t * EXPERTS + k] * outs[k]

            mix[:, pl.ds(t * EOUT, EOUT)] = lax.fori_loop(
                1, EXPERTS, add, probs[t * EXPERTS] * outs[0]
            )
        mixture = mix[...]
        zero = jnp.zeros((THID, EOUT), F32)
        w1_bd = jnp.concatenate(
            [
                jnp.concatenate([w1_ref[0], zero], axis=1),
                jnp.concatenate([zero, w1_ref[1]], axis=1),
            ],
            axis=0,
        )
        b1 = jnp.concatenate([b1_ref[pl.ds(t, 1), :] for t in range(TASKS)], axis=1)
        upper, upper_slope = gelu_both(dot_nt(mixture, w1_bd, EXACT) + b1)
        none = jnp.zeros((1, THID), F32)
        w2_bd = jnp.concatenate(
            [
                jnp.concatenate([w2_ref[pl.ds(0, 1), :], none], axis=1),
                jnp.concatenate([none, w2_ref[pl.ds(1, 1), :]], axis=1),
            ],
            axis=0,
        )
        task = lax.broadcasted_iota(jnp.int32, (TASKS, ROWS_LOC), 0)
        logit = dot_nt(w2_bd, upper, EXACT) + jnp.where(task == 0, b2_ref[0], b2_ref[1])
        d_logit = jax.nn.sigmoid(logit) - labels_ref[...].astype(F32)
        d_pre1 = dot_tn(d_logit, w2_bd, EXACT) * upper_slope
        grad_w2 = dot_nn(d_logit, upper, EXACT)
        grad_b1 = jnp.sum(d_pre1, axis=0, keepdims=True)
        grad_w1 = dot_tn(d_pre1, mixture, EXACT)
        d_mix = dot_nn(d_pre1, w1_bd, EXACT)
        mix[...] = d_mix

        def back_raw(k, carry):
            d_one = mix[:, pl.ds(0, EOUT)]
            d_two = mix[:, pl.ds(EOUT, EOUT)]
            grad = probs[k] * d_one + probs[EXPERTS + k] * d_two
            small_ref[pl.ds(128 + k, 1), :] = jnp.sum(grad, axis=0, keepdims=True)
            d_raw[k] = grad.astype(BF16)
            value = outs[k]
            for t, d_task in enumerate((d_one, d_two)):
                at = pl.ds(pl.multiple_of((t * EXPERTS + k) * EOUT, EOUT), EOUT)
                products[:, at] = (value * d_task).astype(BF16)
            return carry

        lax.fori_loop(0, EXPERTS, back_raw, 0)

        wide = TASKS * EXPERTS * EOUT
        own_gate = lax.broadcasted_iota(jnp.int32, (wide, 128), 0) // EOUT
        column_gate = lax.broadcasted_iota(jnp.int32, (wide, 128), 1)
        ones = (column_gate == own_gate).astype(F32).astype(BF16)
        d_gates = dot_nn(products[...], ones).T[0:16]
        d_gates = d_gates.reshape(TASKS, EXPERTS, ROWS_LOC)
        mean = jnp.sum(d_gates * gates, axis=1, keepdims=True)
        d_logits = (gates * (d_gates - mean)).reshape(16, ROWS_LOC)
        d_parts = jnp.concatenate(split3(d_logits), axis=0)
        stage[...] = dot_nn(d_parts, x)
        grad_gate = stage[0:16] + stage[16:32] + stage[32:48]
        gate_high, gate_mid, _ = split3(gate_w_ref[...])
        left = jnp.concatenate([d_parts[0:32], d_parts[0:16]], axis=0)
        right = jnp.concatenate([gate_high, gate_high, gate_mid], axis=0)
        d_in_ref[...] = dot_tn(left, right)
        small_ref[pl.ds(0, THID), :] = grad_w1[0:THID, 0:EOUT]
        small_ref[pl.ds(THID, THID), :] = grad_w1[THID : 2 * THID, EOUT : 2 * EOUT]
        for tile in range(4):
            small_ref[pl.ds(136 + 16 * tile, 16), :] = grad_gate[:, tile * 128 : tile * 128 + 128]
        small_ref[pl.ds(217, 1), :] = grad_b1
        lane = lax.broadcasted_iota(jnp.int32, (1, 128), 1)
        small_ref[pl.ds(218, 1), :] = jnp.where(lane < THID, grad_w2[0:1], grad_w2[1:2])
        small_ref[pl.ds(219, 1), :] = jnp.zeros((1, 128), F32)
        small_ref[pl.ds(240, 16 + 32), :] = jnp.zeros((48, 128), F32)
        small_ref[pl.ds(220, 2), :] = jnp.broadcast_to(
            jnp.sum(d_logit, axis=1, keepdims=True), (2, 128)
        )
        small_ref[pl.ds(222, 2), :] = jnp.zeros((2, 128), F32)
        small_ref[pl.ds(224, 16), :] = jnp.broadcast_to(
            jnp.sum(d_logits, axis=1, keepdims=True), (16, 128)
        )

    def backward(k, store):
        d_out = d_raw[k]
        grad_out = dot_tn(hidden[k], d_out)
        d_pre = (dot_nt(d_out, weights_out(k)) * slope[k]).astype(BF16)
        bias = jnp.sum(d_pre.astype(F32), axis=0, keepdims=True)
        for p in range(4):
            small_ref[pl.ds(8 * (TILES + p) + k, 1), pl.ds(0, PART)] = bias[
                :, PART * p : PART * p + PART
            ]
        grad_in = dot_tn(d_pre, x)
        for p in range(4):
            at = slice(PART * p, PART * p + PART)
            for block in range(4):
                store(p, block, grad_in[at, block * 128 : block * 128 + 128])
            store(p, 4, grad_out[at, :])
        d_in_ref[...] += dot_nn(d_pre, weights_in(k))

    def remote(source, target, sem, place):
        return pltpu.make_async_remote_copy(
            src_ref=source,
            dst_ref=target,
            send_sem=sems.at[sem],
            recv_sem=sems.at[sem + 1],
            device_id=place,
            device_id_type=pl.DeviceIdType.MESH,
        )

    def wait_all(ref, sem):
        pltpu.make_async_copy(ref, ref, sem).wait()

    def quarter(step):
        q = (step + at_y + at_x + part) % 4
        even = 1 - q % 2
        return q, even, even * part + (1 - even) * at_x, even * at_x + (1 - even) * part

    def experts(step, carry):
        q = quarter(step)[0]

        def for_pair(p, block, value):
            pair_send[q, p, pl.ds(PART * block, PART), :] = value.astype(BF16)

        def for_own(p, block, value):
            own_grad[step % 2, p, pl.ds(PART * block, PART), :] = value

        backward(2 * q + 1 - core, for_pair)
        pltpu.make_async_remote_copy(
            src_ref=pair_send.at[q],
            dst_ref=pair_recv.at[q],
            send_sem=sems.at[0],
            recv_sem=pair_sems.at[q],
            device_id=(line + 1 - 2 * core, part),
            device_id_type=pl.DeviceIdType.MESH,
        ).start()

        @pl.when(step > 0)
        def _():
            first_round(step - 1)

        backward(2 * q + core, for_own)
        return carry

    def first_round(step):
        q, even, first, _ = quarter(step)
        wait_all(pair_recv.at[0], pair_sems.at[q])
        for p in range(4):
            total = (own_grad[step % 2, p] + pair_recv[q, p].astype(F32)).astype(BF16)
            for r in range(4):
                piece = total[CHUNK * r : CHUNK * r + CHUNK]
                share_send[q, even * p + (1 - even) * r, even * r + (1 - even) * p] = piece
        for hop in range(1, 4):
            peer = (first + hop) % 4
            pltpu.make_async_remote_copy(
                src_ref=share_send.at[q, peer],
                dst_ref=first_recv.at[q, first],
                send_sem=sems.at[9],
                recv_sem=first_sems.at[q],
                device_id=(line + (1 - even) * 2 * (peer - at_x), even * peer + (1 - even) * part),
                device_id_type=pl.DeviceIdType.MESH,
            ).start()
        first_recv[q, first] = share_send[q, first]

    def second_round(step):
        q, even, _, second = quarter(step)
        three = first_recv.at[0, pl.ds(0, 3)]
        wait_all(three, first_sems.at[q])
        for at in range(4):
            total = first_recv[q, 0, at].astype(F32)
            for f in range(1, 4):
                total = total + first_recv[q, f, at].astype(F32)
            second_send[q, at] = total.astype(BF16)
        for at in range(4):
            target = 2 * (4 * q + even * at + (1 - even) * at_x) + core
            target_part = even * part + (1 - even) * at
            mine = (target == line) & (target_part == part)

            @pl.when(mine)
            def _():
                share_recv[4 * at_y + second] = second_send[q, at]

            @pl.when(jnp.logical_not(mine))
            def _():
                remote(
                    second_send.at[q, at],
                    share_recv.at[4 * at_y + second],
                    1,
                    (target, target_part),
                ).start()

    def tail():
        d_last = d_in_ref[:, pl.ds(DIN - DPROJ, DPROJ)]
        small_ref[pl.ds(200, 16), :] = jnp.zeros((16, 128), F32)
        small_ref[pl.ds(200, DENSE), pl.ds(0, DPROJ)] = dot_nn(feats_ref[...], d_last, EXACT)
        small_ref[pl.ds(216, 1), :] = jnp.zeros((1, 128), F32)
        small_ref[pl.ds(216, 1), pl.ds(0, DPROJ)] = jnp.sum(d_last, axis=0, keepdims=True)
        grad_dense_ref[...] = dot_nt(dw_ref[...], d_last, EXACT)

    def small_pair():
        return pltpu.make_async_remote_copy(
            src_ref=small_ref,
            dst_ref=small_two,
            send_sem=sems.at[5],
            recv_sem=sems.at[6],
            device_id=(line + 1 - 2 * core, part),
            device_id_type=pl.DeviceIdType.MESH,
        )

    adds_small = ((line < 30) & (part == line % 4)) | (line == 30)

    def share_small():
        small_pair().wait()
        small_two[...] = small_two[...] + small_ref[...]

        def share_tile(at, target, p):
            mine = (target == line) & (part == p)

            @pl.when(mine)
            def _():
                small_recv[chip] = small_two[pl.ds(eight(at), 8), :]

            @pl.when(jnp.logical_not(mine))
            def _():
                source = small_two.at[pl.ds(eight(at), 8), :]
                remote(source, small_recv.at[chip], 3, (target, p)).start()

        for a in range(15):
            target = 2 * a + core
            share_tile(8 * target, target, target % 4)

        @pl.when(core == 0)
        def _():
            for p in range(4):
                share_tile(8 * (TILES + p), 30, p)

    def add_up():
        @pl.when(line == TILES - 1)
        def _():
            small_all[...] = jnp.zeros_like(small_all)

        @pl.when(adds_small)
        def _():
            wait_all(small_recv.at[pl.ds(0, CHIPS - 1)], sems.at[4])

            def add_small(at, total):
                return total + small_recv[at]

            small_own[...] = lax.fori_loop(1, CHIPS, add_small, small_recv[0])

            @pl.when(line < 30)
            def _():
                for hop in range(1, 4):
                    remote(small_own, small_all, 10, (line, (part + hop) % 4)).start()

        wait_all(share_recv.at[pl.ds(0, 15)], sems.at[2])
        total = share_recv[0].astype(F32)
        for at in range(1, 16):
            total = total + share_recv[at].astype(F32)
        low = total.astype(BF16)
        for at in range(TILES):
            share_out_ref[at, pl.ds(0, CHUNK), :] = low

    def add_small_up():
        @pl.when((line < 30) & jnp.logical_not(adds_small))
        def _():
            wait_all(small_all, sems.at[11])

        @pl.when(adds_small)
        def _():
            small_all[...] = small_own[...]

        low = two_parts(small_all[...])
        for at in range(TILES):
            share_out_ref[at, pl.ds(CHUNK, 16), :] = low

    def drain():
        wait_all(pair_send, sems.at[0])
        wait_all(first_recv.at[pl.ds(0, 3)], sems.at[9])
        wait_all(share_recv.at[pl.ds(0, 15)], sems.at[1])
        for sends, zero_core in ((15, 1), (19, 0)):
            for mine in (0, 1):

                @pl.when((core == zero_core) & (adds_small == (mine == 1)))
                def _():
                    wait_all(small_recv.at[pl.ds(0, sends - mine)], sems.at[3])

        @pl.when(adds_small & (line < 30))
        def _():
            wait_all(small_recv.at[pl.ds(0, 3)], sems.at[10])

    def spread():
        lane_from = lax.broadcasted_iota(jnp.int32, (128, 128), 0)
        lane_to = lax.broadcasted_iota(jnp.int32, (128, 128), 1)
        for field in range(FIELDS):
            take = lane_from == EMB * (field % 8) + lane_to % EMB
            copies = dot_nn(d_in_ref[:, pl.ds(field // 8 * 128, 128)].astype(BF16), take.astype(F32).astype(BF16))
            rows[pl.ds(field * ROWS_LOC, ROWS_LOC), :] = copies
        rows[pl.ds(LOOKUPS, 8), :] = jnp.zeros((8, 128), F32)
        group = lane_group(1)
        wide_group = lane_group(CAP - COLD)

        def hot(at, carry):
            for n in range(COLD, CAP):
                row = rows[pl.ds(hot_src_ref[at * SLOTS + n], 1), :]
                hot_rows[at, pl.ds(n - COLD, 1), :] = row
            return carry

        second_round(0)
        lax.fori_loop(0, HOT, hot, 0)
        second_round(1)
        hot_rows[HOT] = jnp.zeros((CAP - COLD, 128), F32)

        def group_at(step):
            return (3 * (line // 2) + part + 4 * core + step) % 16

        def collect(step, slots):
            source = group_at(step) * (8 * SLOTS)
            for n in range(COLD):
                total = rows[pl.ds(src_ref[source + n], 1), :]
                for u in range(1, 8):
                    row = rows[pl.ds(src_ref[source + u * SLOTS + n], 1), :]
                    total = jnp.where(group == u, row, total)
                slots[pl.ds(n, 1), :] = total

        def finish(step, slots):
            first = group_at(step) * 8
            total = jnp.zeros((CAP - COLD, 128), F32)
            for u in range(8):
                total = jnp.where(wide_group == u, hot_rows[hot_at_ref[first + u]], total)
            slots[pl.ds(COLD, CAP - COLD), :] = total
            for half in range(2):
                turned = slots[pl.ds(half * 128, 128), :].T.astype(BF16)
                for u in range(8):
                    at = eight((first + u) * GROUPS + EMB * half, EMB)
                    ready[pl.ds(at, EMB), :] = turned[EMB * u : EMB * u + EMB]

        def send(step):
            first = group_at(step) * 8
            for u in range(8):
                dest = first + (me + u) % 8

                @pl.when(dest != me)
                def _():
                    send_block(ready, landing, me, dest, sems.at[7], sems.at[8])

        for slots in (even, odd):
            slots[pl.ds(CAP, SLOTS - CAP), :] = jnp.zeros((SLOTS - CAP, 128), F32)
        share_small()
        second_round(2)
        collect(0, even)
        second_round(3)

        def two_groups(pair, carry):
            step = 2 * pair
            collect(step + 1, odd)
            finish(step, even)
            send(step)
            collect(jnp.minimum(step + 2, 15), even)
            finish(step + 1, odd)
            send(step + 1)
            return carry

        lax.fori_loop(0, 8, two_groups, 0)
        add_up()
        add_small_up()
        wait_blocks(ready, landing, sems.at[7], sems.at[8])
        rows_out_ref[...] = landing[...]
        mine = pl.ds(eight(me * GROUPS, GROUPS), GROUPS)
        rows_out_ref[mine, :] = ready[mine, :]
        drain()

    @pl.when(phase == 0)
    def _():
        for k in range(EXPERTS):
            load_w_in(k).start()
        for load in loads:
            load.start()
        greet_all(me)
        loads[0].wait()
        lax.fori_loop(0, EXPERTS, forward, 0)

    @pl.when(phase == 1)
    def _():
        head()

    @pl.when(phase == 2)
    def _():
        pl.semaphore_wait(pltpu.get_barrier_semaphore(), OWNERS - 1)
        lax.fori_loop(0, 4, experts, 0)
        for load in loads[1:]:
            load.wait()
        first_round(3)
        tail()
        small_pair().start()
        spread()


def model(*operands):
    return pl.pallas_call(
        model_kernel,
        grid=(3,),
        in_specs=[VM] * 4 + [ANY] * 2 + [VM] * 7 + [SM] * 2 + [ANY] * 2,
        out_specs=[VM] * 3,
        out_shape=[
            shape((OWNERS * GROUPS, 128), BF16),
            shape((TILES, SHARE, 128), BF16),
            shape((DENSE, ROWS_LOC), F32),
        ],
        scratch_shapes=[
            pltpu.VMEM((8 * (TILES + 4), 128), F32),
            pltpu.VMEM((8 * (TILES + 4), 128), F32),
            pltpu.VMEM((ROWS_LOC, DIN), F32),
            pltpu.VMEM((EXPERTS, ROWS_LOC, HID), BF16),
            pltpu.VMEM((EXPERTS, ROWS_LOC, HID), F32),
            pltpu.VMEM((EXPERTS, ROWS_LOC, EOUT), F32),
            pltpu.VMEM((TASKS * EXPERTS, ROWS_LOC, EOUT), F32),
            pltpu.VMEM((EXPERTS, ROWS_LOC, EOUT), BF16),
            pltpu.VMEM((ROWS_LOC, TASKS * EXPERTS * EOUT), BF16),
            pltpu.VMEM((ROWS_LOC, TASKS * EOUT), F32),
            pltpu.VMEM((48, DIN), F32),
            pltpu.VMEM((2, 4, 4 * CHUNK, 128), F32),
            pltpu.VMEM((4, 4, 4 * CHUNK, 128), BF16),
            pltpu.VMEM((4, 4, 4 * CHUNK, 128), BF16),
            pltpu.VMEM((4, 4, 4, CHUNK, 128), BF16),
            pltpu.VMEM((4, 4, 4, CHUNK, 128), BF16),
            pltpu.VMEM((4, 4, CHUNK, 128), BF16),
            pltpu.VMEM((16, CHUNK, 128), BF16),
            pltpu.VMEM((CHIPS, 8, 128), F32),
            pltpu.VMEM((8, 128), F32),
            pltpu.VMEM((8, 128), F32),
            pltpu.VMEM((LOOKUPS + 8, 128), F32),
            pltpu.VMEM((HOT + 1, CAP - COLD, 128), F32),
            pltpu.VMEM((SLOTS, 128), F32),
            pltpu.VMEM((SLOTS, 128), F32),
            pltpu.VMEM((OWNERS * GROUPS, 128), BF16),
            pltpu.VMEM((OWNERS * GROUPS, 128), BF16),
            pltpu.VMEM((4, EXPERTS, PART, DIN), BF16),
            pltpu.VMEM((4, EXPERTS, PART, EOUT), BF16),
            pltpu.SMEM((OWNERS * SLOTS,), jnp.int32),
            pltpu.SMEM((2 * HOT * SLOTS,), jnp.int32),
            pltpu.SemaphoreType.DMA((EXPERTS + 3,)),
            pltpu.SemaphoreType.DMA((4,)),
            pltpu.SemaphoreType.DMA((4,)),
            pltpu.SemaphoreType.DMA((12,)),
        ],
        compiler_params=remote_params(MODEL_MIB, 1),
        name="model",
    )(*operands)


def scatter_kernel(
    asked_hbm,
    grads_hbm,
    out_hbm,
    rows_v,
    groups,
    rows,
    sem,
    even,
    odd,
    asked_ref,
    grads_ref,
    out_ref,
    out_sem,
    *sums,
):
    asked_copy = pltpu.make_async_copy(asked_hbm, asked_ref, sem.at[1])
    asked_copy.start()
    grads_copy = pltpu.make_async_copy(grads_hbm, grads_ref, sem.at[2])
    grads_copy.start()
    asked_copy.wait()
    split_wanted(asked_ref, rows_v, groups)
    rows_copy = pltpu.make_async_copy(rows_v, rows, sem.at[0])
    rows_copy.start()
    at_group = sublane_group()

    def clear(step, carry):
        for total in sums:
            total[pl.ds(eight(step * 512), 512), :] = jnp.zeros((512, 128), F32)
        return carry

    lax.fori_loop(0, PACKED // 512, clear, 0)
    grads_copy.wait()
    rows_copy.wait()

    def place(source, found):
        for half in range(2):
            block = grads_ref[pl.ds(eight(source * GROUPS + EMB * half, EMB), EMB), :].astype(F32)
            block = jnp.broadcast_to(block[None], (8, EMB, 128)).reshape(128, 128)
            block = jnp.where(at_group == groups[source, pl.ds(half, 1), :], block, 0.0)
            found[pl.ds(half * 128, 128), :] = block.T

    def add(source, found):
        for n in range(CAP):
            at = pl.ds(rows[source, n // 128, n % 128], 1)
            total = sums[n % SUMS]
            total[at, :] = total[at, :] + found[pl.ds(n, 1), :]

    place(0, even)

    def two_sources(step, carry):
        source = 2 * step
        place(source + 1, odd)
        add(source, even)
        place(jnp.minimum(source + 2, OWNERS - 1), even)
        add(source + 1, odd)
        return carry

    lax.fori_loop(0, OWNERS // 2, two_sources, 0)

    def write(field, carry):
        for part in range(4):
            at = pl.ds(eight(field * 512 + part * 128, 128), 128)
            block = sums[0][at, :]
            for total in sums[1:]:
                block = block + total[at, :]
            block = block.T
            for k in range(8):
                out_ref[field, :, pl.ds(part * 1024 + k * 128, 128)] = block[16 * k : 16 * k + 16]
        pltpu.make_async_copy(out_ref.at[field], out_hbm.at[field], out_sem).start()
        return carry

    lax.fori_loop(0, FIELDS, write, 0)
    pltpu.make_async_copy(out_ref, out_hbm, out_sem).wait()


def scatter_add(asked, grads):
    return pl.pallas_call(
        scatter_kernel,
        in_specs=[ANY, ANY],
        out_specs=ANY,
        out_shape=shape((FIELDS, EMB, ROWS_DEV), F32),
        scratch_shapes=split_scratch()
        + [pltpu.VMEM((SLOTS, 128), F32)] * 2
        + [
            pltpu.VMEM((OWNERS, 2, 128), jnp.int32),
            pltpu.VMEM((OWNERS * GROUPS, 128), BF16),
            pltpu.VMEM((FIELDS, EMB, ROWS_DEV), F32),
            pltpu.SemaphoreType.DMA,
        ]
        + [pltpu.VMEM((PACKED + 8, 128), F32)] * SUMS,
        compiler_params=params(58),
        name="scatter_add",
    )(asked, grads)


def unpack_kernel(
    shares_ref,
    w_in_ref,
    w_out_ref,
    w1_ref,
    b_out_ref,
    gate_ref,
    dense_w_ref,
    dense_b_ref,
    b1_ref,
    w2_ref,
    b2_ref,
    gate_b_ref,
    b_in_ref,
):
    def expert(k, carry):
        lines = [2 * (4 * (k // 2) + at) + k % 2 for at in range(4)]
        rows = [shares_ref[at, pl.ds(0, CHUNK), :] for at in lines]
        rows = jnp.concatenate(rows, axis=0).astype(F32)
        for block in range(4):
            w_in_ref[k, :, pl.ds(block * 128, 128)] = rows[PART * block : PART * block + PART]
        w_out_ref[k] = rows[4 * PART : 5 * PART]
        return carry

    lax.fori_loop(0, EXPERTS, expert, 0)

    def tile(at):
        return one_of(shares_ref[at, pl.ds(CHUNK, 16), :])

    for at in range(16):
        w1_ref[at // 8, pl.ds(at % 8 * 8, 8), :] = tile(at)
    b_out_ref[...] = tile(16)
    for at in range(8):
        gate_ref[pl.ds(at % 2 * 8, 8), pl.ds(at // 2 * 128, 128)] = tile(17 + at)
    dense_w_ref[pl.ds(0, 8), :] = tile(25)[:, 0:DPROJ]
    dense_w_ref[pl.ds(8, DENSE - 8), :] = tile(26)[0 : DENSE - 8, 0:DPROJ]
    rest = tile(27)
    dense_b_ref[...] = rest[0:1, 0:DPROJ]
    for t in range(TASKS):
        b1_ref[pl.ds(t, 1), :] = rest[1:2, t * THID : t * THID + THID]
        w2_ref[pl.ds(t, 1), :] = rest[2:3, t * THID : t * THID + THID]
    lane = lax.broadcasted_iota(jnp.int32, (1, 128), 1)
    b2_ref[...] = jnp.where(lane == 0, rest[4:5], rest[5:6])[:, 0:TASKS]
    own = lax.broadcasted_iota(jnp.int32, (8, 128), 0) == lax.broadcasted_iota(
        jnp.int32, (8, 128), 1
    )
    for t in range(TASKS):
        value = jnp.sum(jnp.where(own, tile(28 + t), 0.0), axis=0, keepdims=True)
        gate_b_ref[pl.ds(t, 1), :] = value[:, 0:EXPERTS]
    b_in_ref[...] = tile(30)[:, 0:PART]


def unpack(shares):
    return pl.pallas_call(
        unpack_kernel,
        in_specs=[VM],
        out_specs=[VM] * 12,
        out_shape=[
            shape((EXPERTS, PART, DIN), F32),
            shape((EXPERTS, PART, EOUT), F32),
            shape((TASKS, THID, EOUT), F32),
            shape((EXPERTS, EOUT), F32),
            shape((TASKS * EXPERTS, DIN), F32),
            shape((DENSE, DPROJ), F32),
            shape((1, DPROJ), F32),
            shape((TASKS, THID), F32),
            shape((TASKS, THID), F32),
            shape((1, TASKS), F32),
            shape((TASKS, EXPERTS), F32),
            shape((EXPERTS, PART), F32),
        ],
        compiler_params=params(32),
        name="unpack",
    )(shares)


def body(
    sparse_ids,
    dense_feats,
    labels,
    tables,
    dense_w,
    dense_b,
    w_in,
    b_in,
    w_out,
    b_out,
    gate_w,
    gate_b,
    tower_w1,
    tower_b1,
    tower_w2,
    tower_b2,
):
    w_in_all = lax.all_gather(w_in.transpose(0, 2, 1), "mp", axis=0)
    ids = sparse_ids.T
    field = lax.broadcasted_iota(jnp.int32, (FIELDS, ROWS_LOC), 0)
    example = lax.broadcasted_iota(jnp.int32, (FIELDS, ROWS_LOC), 1)
    row = ids & (ROWS_DEV - 1)
    packed = field * 512 + (row >> 10) * 128 + (row & 127)
    key = ((ids >> 12) << 14) | (field * ROWS_LOC + example)
    load = (packed << 3) | ((row >> 7) & 7)
    keys, loads = lax.sort((key.reshape(-1), load.reshape(-1)), num_keys=1, is_stable=False)
    requests, sources, hot_sources, hot, hot_at = route(keys.reshape(-1, 128), loads.reshape(-1, 128))
    sources = sources.reshape(-1)
    answer, asked, w_out_all, b_in_all = look_up(
        requests, tables.transpose(0, 2, 1), w_out, b_in
    )
    feats_t = dense_feats.T
    inputs = embed(sources, hot, ids, answer, feats_t, dense_w, dense_b.reshape(1, DPROJ))
    incoming, share, grad_dense = model(
        inputs,
        labels.T,
        feats_t,
        dense_w,
        w_in_all,
        w_out_all,
        b_in_all,
        b_out,
        gate_w.transpose(0, 2, 1).reshape(TASKS * EXPERTS, DIN),
        gate_b,
        tower_w1.transpose(0, 2, 1),
        tower_b1,
        tower_w2,
        tower_b2,
        hot_at,
        sources,
        hot_sources.reshape(-1),
    )
    shares = lax.all_to_all(share, "dp", split_axis=0, concat_axis=0, tiled=True)
    grad_tables = scatter_add(asked, incoming).transpose(0, 2, 1)
    (
        grad_w_in,
        grad_w_out,
        grad_w1,
        grad_b_out,
        grad_gate_w,
        grad_dense_w,
        grad_dense_b,
        grad_b1,
        grad_w2,
        grad_b2,
        grad_gate_b,
        grad_b_in,
    ) = unpack(shares)
    return (
        grad_tables,
        grad_dense_w,
        grad_dense_b.reshape(DPROJ),
        grad_w_in.transpose(0, 2, 1),
        grad_b_in,
        grad_w_out,
        grad_b_out,
        grad_gate_w.reshape(TASKS, EXPERTS, DIN).transpose(0, 2, 1),
        grad_gate_b,
        grad_w1.transpose(0, 2, 1),
        grad_b1,
        grad_w2,
        grad_b2.reshape(TASKS),
        grad_dense.T,
    )


def solution(mesh):
    return jax.shard_map(
        body,
        mesh=mesh,
        in_specs=(
            P(ALL, None),
            P(ALL, None),
            P(ALL, None),
            P(None, ALL, None),
            P(),
            P(),
            P(None, None, "mp"),
            P(None, "mp"),
            P(None, "mp", None),
            P(),
            P(),
            P(),
            P(),
            P(),
            P(),
            P(),
        ),
        out_specs=(
            P(None, ALL, None),
            P(),
            P(),
            P(None, None, "mp"),
            P(None, "mp"),
            P(None, "mp", None),
            P(),
            P(),
            P(),
            P(),
            P(),
            P(),
            P(),
            P(ALL, None),
        ),
        check_vma=False,
    )
```

```python
import functools

import jax
import jax.numpy as jnp
from jax import lax
from jax.experimental import pallas as pl
from jax.experimental.pallas import tpu as pltpu
from jax.sharding import PartitionSpec as P

ALL = ("dp", "mp")
EXACT = lax.Precision.HIGHEST
F32 = jnp.float32
BF16 = jnp.bfloat16

OWNERS = 128
FIELDS = 26
EMB = 16
ROWS_LOC = 512
ROWS_DEV = 4096
LOOKUPS = ROWS_LOC * FIELDS
PACKED = FIELDS * ROWS_DEV // 8
CAP = 208
NEAR = 90
COLD = 96
HOT = 16
SLOTS = 256
GROUPS = SLOTS // 8
EXPERTS = 8
HID = 256
EOUT = 128
TASKS = 2
THID = 64
DIN = 512
DENSE = 13
DPROJ = 96
CHUNK = 80
TILES = 32
CHIPS = OWNERS // 2
SHARE = CHUNK + 16
MODEL_MIB = 50
PART = 64
SUMS = 6

VM = pl.BlockSpec(memory_space=pltpu.VMEM)
SM = pl.BlockSpec(memory_space=pltpu.SMEM)
ANY = pl.BlockSpec(memory_space=pl.ANY)


def params(mib):
    return pltpu.CompilerParams(vmem_limit_bytes=mib * 1024 * 1024)


def shape(dims, dtype):
    return jax.ShapeDtypeStruct(dims, dtype)


def lane_group(rows):
    return lax.broadcasted_iota(jnp.int32, (rows, 128), 1) // EMB


def sublane_group():
    return lax.broadcasted_iota(jnp.int32, (128, 128), 0) // EMB


def eight(index, unit=8):
    return pl.multiple_of(index, unit)


def dot_nt(a, b, precision=None):
    return lax.dot_general(
        a, b, (((1,), (1,)), ((), ())), precision=precision, preferred_element_type=F32
    )


def dot_tn(a, b, precision=None):
    return lax.dot_general(
        a, b, (((0,), (0,)), ((), ())), precision=precision, preferred_element_type=F32
    )


def dot_nn(a, b, precision=None):
    return lax.dot_general(
        a, b, (((1,), (0,)), ((), ())), precision=precision, preferred_element_type=F32
    )


def split3(value):
    high = value.astype(BF16)
    rest = value - high.astype(F32)
    mid = rest.astype(BF16)
    low = (rest - mid.astype(F32)).astype(BF16)
    return high, mid, low


def my_index():
    return lax.axis_index("dp") * lax.axis_size("mp") + lax.axis_index("mp")


def place_of(index):
    return (index // 4, index % 4)


def greet_all(me):
    barrier = pltpu.get_barrier_semaphore()

    def greet(step, carry):
        pl.semaphore_signal(
            barrier,
            inc=1,
            device_id=place_of((me + step + 1) % OWNERS),
            device_id_type=pl.DeviceIdType.MESH,
        )
        return carry

    lax.fori_loop(0, OWNERS - 1, greet, 0)
    return barrier


def block_of(ref, index):
    return ref.at[pl.ds(eight(index * GROUPS, GROUPS), GROUPS), :]


def send_block(ready, landing, me, dest, send_sem, recv_sem):
    pltpu.make_async_remote_copy(
        src_ref=block_of(ready, dest),
        dst_ref=block_of(landing, me),
        send_sem=send_sem,
        recv_sem=recv_sem,
        device_id=place_of(dest),
        device_id_type=pl.DeviceIdType.MESH,
    ).start()


def wait_blocks(ready, landing, send_sem, recv_sem):
    every = pl.ds(0, (OWNERS - 1) * GROUPS)
    pltpu.make_async_copy(ready.at[every, :], ready.at[every, :], send_sem).wait()
    pltpu.make_async_copy(landing.at[every, :], landing.at[every, :], recv_sem).wait()


def remote_params(mib, identity):
    return pltpu.CompilerParams(
        vmem_limit_bytes=mib * 1024 * 1024, collective_id=identity, has_side_effects=True
    )


def route_kernel(
    key_ref,
    load_ref,
    req_ref,
    src_ref,
    hot_src_ref,
    hot_ref,
    hot_at_ref,
    both,
    cut,
    starts_v,
    starts,
    sem,
):
    own = (key_ref[...] & 16383) << 17
    both[pl.ds(0, 104), :] = own | load_ref[...]
    both[pl.ds(104, 8), :] = jnp.zeros((8, 128), jnp.int32)
    owner_at = lax.broadcasted_iota(jnp.int32, (128, 128), 0)

    def count(step, total):
        rows = key_ref[pl.ds(eight(step * 8), 8), :] >> 14
        for at in range(8):
            total = total + (rows[at : at + 1, :] < owner_at).astype(jnp.int32)
        return total

    below = lax.fori_loop(0, 13, count, jnp.zeros((128, 128), jnp.int32))
    first = jnp.sum(below.astype(F32).T, axis=0, keepdims=True).astype(jnp.int32)
    starts_v[...] = jnp.broadcast_to(first, (8, 128))
    copy = pltpu.make_async_copy(starts_v, starts, sem)
    copy.start()
    copy.wait()
    for at in range(2 * HOT):
        hot_ref[at] = 0
    lane = lax.broadcasted_iota(jnp.int32, (1, 128), 1)
    unused = (LOOKUPS << 17) | (PACKED * 8)

    def per_owner(owner, hot_count):
        start = starts[0, owner]
        end = jnp.where(owner == OWNERS - 1, LOOKUPS, starts[0, jnp.minimum(owner + 1, 127)])
        row = start >> 7
        off = start & 127
        pieces = [both[pl.ds(row + at, 1), :] for at in range(3)]
        for half in range(2):
            piece = jnp.where(lane >= off, pieces[half], pieces[half + 1])
            piece = pltpu.roll(piece, (128 - off) & 127, 1)
            piece = jnp.where(lane < end - start - 128 * half, piece, unused)
            cut[pl.ds(2 * owner + half, 1), :] = piece
            hot_src_ref[pl.ds(2 * hot_count + half, 1), :] = piece >> 17
        is_hot = end - start > COLD
        hot_ref[hot_count] = owner
        hot_at_ref[owner] = jnp.where(is_hot & (hot_count < HOT), hot_count, HOT)
        return jnp.minimum(hot_count + is_hot.astype(jnp.int32), 2 * HOT - 1)

    lax.fori_loop(0, OWNERS, per_owner, 0, unroll=8)
    src_ref[...] = cut[...] >> 17
    req_ref[...] = (cut[...] & ((1 << 17) - 1)).reshape(OWNERS, 2, 128)


def route(keys, loads):
    return pl.pallas_call(
        route_kernel,
        in_specs=[VM, VM],
        out_specs=[VM, VM, VM, SM, SM],
        out_shape=[
            shape((OWNERS, 2, 128), jnp.int32),
            shape((2 * OWNERS, 128), jnp.int32),
            shape((4 * HOT, 128), jnp.int32),
            shape((2 * HOT,), jnp.int32),
            shape((OWNERS,), jnp.int32),
        ],
        scratch_shapes=[
            pltpu.VMEM((112, 128), jnp.int32),
            pltpu.VMEM((2 * OWNERS, 128), jnp.int32),
            pltpu.VMEM((8, 128), jnp.int32),
            pltpu.SMEM((8, 128), jnp.int32),
            pltpu.SemaphoreType.DMA,
        ],
        compiler_params=params(8),
        name="route",
    )(keys, loads)


def split_wanted(asked_ref, rows_v, groups):
    rows_v[...] = asked_ref[...] >> 3
    groups[...] = asked_ref[...] & 7


def split_scratch():
    return [
        pltpu.VMEM((OWNERS, 2, 128), jnp.int32),
        pltpu.VMEM((OWNERS, 2, 128), jnp.int32),
        pltpu.SMEM((OWNERS, 2, 128), jnp.int32),
        pltpu.SemaphoreType.DMA((8,)),
    ]


def look_up_kernel(
    wanted_ref,
    tables_ref,
    w_out_ref,
    b_in_ref,
    out_ref,
    asked_ref,
    w_out_all,
    b_in_all,
    b_low,
    b_own,
    fields,
    table,
    rows_v,
    groups,
    rows,
    sem,
    even,
    odd,
    ready,
    field_sem,
    ask_send,
    ask_recv,
    send_sem,
    recv_sem,
    own_sem,
    weight_sems,
):
    me = my_index()
    line = lax.axis_index("dp")
    part = lax.axis_index("mp")

    def field_copy(field):
        return pltpu.make_async_copy(
            tables_ref.at[field], fields.at[field], field_sem.at[field]
        )

    def start_field(field, carry):
        field_copy(field).start()
        return carry

    own_weights = [
        pltpu.make_async_copy(source, target, weight_sems.at[4 + at])
        for at, (source, target) in enumerate(((w_out_ref, w_out_all.at[part]), (b_in_ref, b_low)))
    ]
    for copy in own_weights:
        copy.start()
    lax.fori_loop(0, FIELDS, start_field, 0)
    barrier = greet_all(me)

    def pack(field, carry):
        field_copy(field).wait()
        for part in range(4):
            block = jnp.concatenate(
                [fields[field, :, pl.ds(part * 1024 + k * 128, 128)] for k in range(8)], axis=0
            )
            table[pl.ds(eight(field * 512 + part * 128, 128), 128), :] = block.T
        return carry

    lax.fori_loop(0, 8, pack, 0)
    table[pl.ds(PACKED, 8), :] = jnp.zeros((8, 128), F32)
    asked_ref[me] = wanted_ref[me]
    pl.semaphore_wait(barrier, OWNERS - 1)

    def ask(step, carry):
        owner = (me + step + 1) % OWNERS
        pltpu.make_async_remote_copy(
            src_ref=wanted_ref.at[owner],
            dst_ref=asked_ref.at[me],
            send_sem=ask_send,
            recv_sem=ask_recv,
            device_id=place_of(owner),
            device_id_type=pl.DeviceIdType.MESH,
        ).start()
        return carry

    lax.fori_loop(0, OWNERS - 1, ask, 0)
    for copy in own_weights:
        copy.wait()
    b_own[...] = jnp.zeros_like(b_own)
    b_own[:, pl.ds(0, PART)] = b_low[...].astype(F32)
    b_in_all[part] = b_own[...]

    def weight_copies(step):
        place = (line, (part + step) % 4)
        return [
            pltpu.make_async_remote_copy(
                src_ref=source,
                dst_ref=target.at[part],
                send_sem=weight_sems.at[2 * at],
                recv_sem=weight_sems.at[2 * at + 1],
                device_id=place,
                device_id_type=pl.DeviceIdType.MESH,
            )
            for at, (source, target) in enumerate(((w_out_ref, w_out_all), (b_own, b_in_all)))
        ]

    for step in range(1, 4):
        for copy in weight_copies(step):
            copy.start()
    lax.fori_loop(8, FIELDS, pack, 0)
    others = pl.ds(0, OWNERS - 1)
    pltpu.make_async_copy(asked_ref.at[others], asked_ref.at[others], ask_recv).wait()
    split_wanted(asked_ref, rows_v, groups)

    def rows_copy(step):
        chunk = pl.ds(eight((me // 16 + step) % 8 * 16, 16), 16)
        return pltpu.make_async_copy(rows_v.at[chunk], rows.at[chunk], sem.at[step])

    for step in range(8):
        rows_copy(step).start()
    for step in range(2):
        rows_copy(step).wait()
    at_group = sublane_group()

    def gather(source, found):
        for n in range(CAP):
            at = rows[source, n // 128, n % 128]
            found[pl.ds(n, 1), :] = table[pl.ds(at, 1), :]

    def pick(source, found):
        for half in range(2):
            block = found[pl.ds(half * 128, 128), :].T
            block = jnp.where(at_group == groups[source, pl.ds(half, 1), :], block, 0.0)
            block = jnp.sum(block.reshape(8, EMB, 128), axis=0)
            ready[pl.ds(eight(source * GROUPS + EMB * half, EMB), EMB), :] = block.astype(BF16)

    def send(source):
        send_block(ready, out_ref, me, source, send_sem, recv_sem)

    even[...] = jnp.zeros_like(even)
    odd[...] = jnp.zeros_like(odd)
    gather(me, even)
    gather((me + 1) % OWNERS, odd)
    pick(me, even)
    own = pltpu.make_async_copy(block_of(ready, me), block_of(out_ref, me), own_sem)
    own.start()

    def two_sources(step, carry):
        first = (me + 2 * step + 1) % OWNERS
        second = (me + 2 * step + 2) % OWNERS
        third = (me + 2 * step + 3) % OWNERS
        gather(second, even)
        pick(first, odd)
        send(first)
        gather(third, odd)
        pick(second, even)
        send(second)
        return carry

    lax.fori_loop(0, 6, two_sources, 0)
    for step in range(2, 8):
        rows_copy(step).wait()
    lax.fori_loop(6, OWNERS // 2 - 1, two_sources, 0)
    last = (me + OWNERS - 1) % OWNERS
    pick(last, odd)
    send(last)
    own.wait()
    pltpu.make_async_copy(wanted_ref.at[others], wanted_ref.at[others], ask_send).wait()
    three = pl.ds(0, 3)
    for at, target in enumerate((w_out_all, b_in_all)):
        for sem_at in (2 * at, 2 * at + 1):
            sem = weight_sems.at[sem_at]
            pltpu.make_async_copy(target.at[three], target.at[three], sem).wait()
    wait_blocks(ready, out_ref, send_sem, recv_sem)


def look_up(wanted, tables_t, w_out, b_in):
    return pl.pallas_call(
        look_up_kernel,
        in_specs=[VM] + [pl.BlockSpec(memory_space=pl.ANY)] * 3,
        out_specs=[VM] * 4,
        out_shape=[
            shape((OWNERS * GROUPS, 128), BF16),
            shape((OWNERS, 2, 128), jnp.int32),
            shape((4, EXPERTS, PART, EOUT), BF16),
            shape((4, EXPERTS, 128), F32),
        ],
        scratch_shapes=[
            pltpu.VMEM((EXPERTS, PART), BF16),
            pltpu.VMEM((EXPERTS, 128), F32),
            pltpu.VMEM((FIELDS, EMB, ROWS_DEV), F32),
            pltpu.VMEM((PACKED + 8, 128), F32),
        ]
        + split_scratch()
        + [pltpu.VMEM((SLOTS, 128), F32)] * 2
        + [pltpu.VMEM((OWNERS * GROUPS, 128), BF16)]
        + [pltpu.SemaphoreType.DMA((FIELDS,))]
        + [pltpu.SemaphoreType.DMA] * 5
        + [pltpu.SemaphoreType.DMA((6,))],
        compiler_params=remote_params(48, 0),
        name="look_up",
    )(wanted, tables_t, w_out, b_in)


def embed_kernel(
    source_ref,
    hot_ref,
    ids_ref,
    answer_ref,
    feats_ref,
    dw_ref,
    db_ref,
    out_ref,
    slots,
    rows,
    x_t,
    src_ref,
    sem,
):
    copy = pltpu.make_async_copy(source_ref, src_ref, sem)
    copy.start()
    for block in range(32):
        owner, half = block // 2 * 8, block % 2
        parts = [
            answer_ref[pl.ds((owner + u) * GROUPS + EMB * half, EMB), :] for u in range(8)
        ]
        slots[pl.ds(block * 128, 128), :] = jnp.concatenate(parts, axis=0).astype(F32).T

    copy.wait()

    def cold(step, carry):
        base = step // 6 * SLOTS + step % 6 * (NEAR // 6)
        source = step // 6 * (8 * SLOTS) + step % 6 * (NEAR // 6)
        for n in range(NEAR // 6):
            row = slots[pl.ds(base + n, 1), :]
            for u in range(8):
                rows[pl.ds(src_ref[source + u * SLOTS + n], 1), :] = row
        return carry

    def hot(at, carry):
        owner = hot_ref[at]
        base = (owner >> 3) * SLOTS
        for n in range(NEAR, CAP):
            rows[pl.ds(src_ref[owner * SLOTS + n], 1), :] = slots[pl.ds(base + n, 1), :]
        return carry

    lax.fori_loop(0, OWNERS // 8 * 6, cold, 0)
    lax.fori_loop(0, HOT, hot, 0)
    at_group = sublane_group()

    def field(f, carry):
        group = (ids_ref[pl.ds(f, 1), :] >> 12) & 7
        for part in range(4):
            block = rows[pl.ds(eight(f * ROWS_LOC + part * 128, 128), 128), :].T
            block = jnp.where(at_group == group[:, part * 128 : part * 128 + 128], block, 0.0)
            block = jnp.sum(block.reshape(8, EMB, 128), axis=0)
            x_t[pl.ds(eight(f * EMB, EMB), EMB), pl.ds(part * 128, 128)] = block
        return carry

    lax.fori_loop(0, FIELDS, field, 0)
    top = lax.broadcasted_iota(jnp.int32, (8, DPROJ), 0) == 0
    bias = jnp.where(top, jnp.broadcast_to(db_ref[...], (8, DPROJ)), 0.0)
    x_t[pl.ds(FIELDS * EMB, DPROJ), :] = (
        dot_tn(dw_ref[...], feats_ref[...], EXACT)
        + dot_tn(bias, jnp.ones((8, ROWS_LOC), F32), EXACT)
    )
    out_ref[...] = x_t[...].T.astype(BF16)


def embed(src, hot, ids, answer, feats_t, dense_w, dense_b):
    return pl.pallas_call(
        embed_kernel,
        in_specs=[ANY, SM, VM, VM, VM, VM, VM],
        out_specs=VM,
        out_shape=shape((ROWS_LOC, DIN), BF16),
        scratch_shapes=[
            pltpu.VMEM((OWNERS * GROUPS, 128), F32),
            pltpu.VMEM((LOOKUPS + 8, 128), F32),
            pltpu.VMEM((DIN, ROWS_LOC), F32),
            pltpu.SMEM((OWNERS * SLOTS,), jnp.int32),
            pltpu.SemaphoreType.DMA,
        ],
        compiler_params=params(16),
        name="embed",
    )(src, hot, ids, answer, feats_t, dense_w, dense_b)


C0 = 0.7978845608
C1 = 0.7978845608 * 0.044715


def gelu_both(value):
    square = value * value
    bend = jnp.tanh(value * (C0 + C1 * square))
    half = 0.5 * (1.0 + bend)
    slope = half + 0.5 * value * (1.0 - bend * bend) * (C0 + 3.0 * C1 * square)
    return value * half, slope


def two_parts(value):
    high = value.astype(BF16).astype(F32)
    return jnp.concatenate([high, value - high], axis=0).astype(BF16)


def one_of(parts):
    wide = parts.astype(F32)
    return wide[0:8] + wide[8:16]


def model_kernel(
    x_ref,
    labels_ref,
    feats_ref,
    dw_ref,
    w_in_hbm,
    w_out_hbm,
    b_in_ref,
    b_out_ref,
    gate_w_ref,
    gate_b_ref,
    w1_ref,
    b1_ref,
    w2_ref,
    b2_ref,
    hot_at_ref,
    src_hbm,
    hot_src_hbm,
    rows_out_ref,
    share_out_ref,
    grad_dense_ref,
    small_ref,
    small_two,
    d_in_ref,
    hidden,
    slope,
    outs,
    probs,
    d_raw,
    products,
    mix,
    stage,
    own_grad,
    pair_send,
    pair_recv,
    share_send,
    first_recv,
    second_send,
    share_recv,
    small_recv,
    small_own,
    small_all,
    rows,
    hot_rows,
    even,
    odd,
    ready,
    landing,
    w_in_ref,
    w_out_ref,
    src_ref,
    hot_src_ref,
    load_sems,
    pair_sems,
    first_sems,
    sems,
):
    x = x_ref[...]
    phase = pl.program_id(0)
    line = lax.axis_index("dp")
    part = lax.axis_index("mp")
    core = line % 2
    chip = line // 2 * 4 + part
    me = my_index()
    at_y, at_x = line // 8, line // 2 % 4

    def load_w_in(k):
        return pltpu.make_async_copy(w_in_hbm.at[:, k], w_in_ref.at[:, k], load_sems.at[k])

    loads = [
        pltpu.make_async_copy(source, target, load_sems.at[EXPERTS + at])
        for at, (source, target) in enumerate(
            ((w_out_hbm, w_out_ref), (src_hbm, src_ref), (hot_src_hbm, hot_src_ref))
        )
    ]

    def weights_in(k):
        return jnp.concatenate(
            [w_in_ref[p, k] for p in range(4)], axis=0
        )

    def weights_out(k):
        return jnp.concatenate(
            [w_out_ref[p, k] for p in range(4)], axis=0
        )

    def forward(k, carry):
        load_w_in(k).wait()
        bias = [b_in_ref[p, pl.ds(k, 1), :][:, 0:PART] for p in range(4)]
        pre = dot_nt(x, weights_in(k)) + jnp.concatenate(bias, axis=1)
        act, grad = gelu_both(pre)
        act = act.astype(BF16)
        hidden[k] = act
        slope[k] = grad
        outs[k] = dot_nn(act, weights_out(k)) + b_out_ref[pl.ds(k, 1), :]
        return carry

    def head():
        gate_parts = jnp.concatenate(split3(gate_w_ref[...]), axis=0)
        stage[...] = dot_nt(gate_parts, x)
        own = lax.broadcasted_iota(jnp.int32, (EXPERTS, EXPERTS), 0) == lax.broadcasted_iota(
            jnp.int32, (EXPERTS, EXPERTS), 1
        )
        gate_b = [
            jnp.sum(jnp.where(own, gate_b_ref[pl.ds(t, 1), :], 0.0), axis=1, keepdims=True)
            for t in range(TASKS)
        ]
        logits = stage[0:16] + stage[16:32] + stage[32:48] + jnp.concatenate(gate_b, axis=0)
        logits = logits.reshape(TASKS, EXPERTS, ROWS_LOC)
        gates = jnp.exp(logits - jnp.max(logits, axis=1, keepdims=True))
        gates = gates / jnp.sum(gates, axis=1, keepdims=True)
        gates_t = gates.reshape(TASKS * EXPERTS, ROWS_LOC)
        gate_parts = [part.astype(F32) for part in split3(gates_t)]
        gate_parts.append(jnp.zeros((80, ROWS_LOC), F32))
        gate_columns = jnp.concatenate(gate_parts, axis=0).T.astype(BF16)
        row_at = lax.broadcasted_iota(jnp.int32, (128, 256), 0)
        column_at = lax.broadcasted_iota(jnp.int32, (128, 256), 1) // EOUT
        row_at = jnp.where(row_at < 48, row_at % 16, -1)

        def spread_gates(pair, carry):
            take = (row_at == 2 * pair + column_at).astype(F32).astype(BF16)
            both = dot_nn(gate_columns, take)
            probs[2 * pair] = both[:, 0:EOUT]
            probs[2 * pair + 1] = both[:, EOUT : 2 * EOUT]
            return carry

        lax.fori_loop(0, TASKS * EXPERTS // 2, spread_gates, 0)

        for t in range(TASKS):
            def add(k, total):
                return total + probs[t * EXPERTS + k] * outs[k]

            mix[:, pl.ds(t * EOUT, EOUT)] = lax.fori_loop(
                1, EXPERTS, add, probs[t * EXPERTS] * outs[0]
            )
        mixture = mix[...]
        zero = jnp.zeros((THID, EOUT), F32)
        w1_bd = jnp.concatenate(
            [
                jnp.concatenate([w1_ref[0], zero], axis=1),
                jnp.concatenate([zero, w1_ref[1]], axis=1),
            ],
            axis=0,
        )
        b1 = jnp.concatenate([b1_ref[pl.ds(t, 1), :] for t in range(TASKS)], axis=1)
        upper, upper_slope = gelu_both(dot_nt(mixture, w1_bd, EXACT) + b1)
        none = jnp.zeros((1, THID), F32)
        w2_bd = jnp.concatenate(
            [
                jnp.concatenate([w2_ref[pl.ds(0, 1), :], none], axis=1),
                jnp.concatenate([none, w2_ref[pl.ds(1, 1), :]], axis=1),
            ],
            axis=0,
        )
        task = lax.broadcasted_iota(jnp.int32, (TASKS, ROWS_LOC), 0)
        logit = dot_nt(w2_bd, upper, EXACT) + jnp.where(task == 0, b2_ref[0], b2_ref[1])
        d_logit = jax.nn.sigmoid(logit) - labels_ref[...].astype(F32)
        d_pre1 = dot_tn(d_logit, w2_bd, EXACT) * upper_slope
        grad_w2 = dot_nn(d_logit, upper, EXACT)
        grad_b1 = jnp.sum(d_pre1, axis=0, keepdims=True)
        grad_w1 = dot_tn(d_pre1, mixture, EXACT)
        d_mix = dot_nn(d_pre1, w1_bd, EXACT)
        mix[...] = d_mix

        def back_raw(k, carry):
            d_one = mix[:, pl.ds(0, EOUT)]
            d_two = mix[:, pl.ds(EOUT, EOUT)]
            grad = probs[k] * d_one + probs[EXPERTS + k] * d_two
            small_ref[pl.ds(128 + k, 1), :] = jnp.sum(grad, axis=0, keepdims=True)
            d_raw[k] = grad.astype(BF16)
            value = outs[k]
            for t, d_task in enumerate((d_one, d_two)):
                at = pl.ds(pl.multiple_of((t * EXPERTS + k) * EOUT, EOUT), EOUT)
                products[:, at] = (value * d_task).astype(BF16)
            return carry

        lax.fori_loop(0, EXPERTS, back_raw, 0)

        wide = TASKS * EXPERTS * EOUT
        own_gate = lax.broadcasted_iota(jnp.int32, (wide, 128), 0) // EOUT
        column_gate = lax.broadcasted_iota(jnp.int32, (wide, 128), 1)
        ones = (column_gate == own_gate).astype(F32).astype(BF16)
        d_gates = dot_nn(products[...], ones).T[0:16]
        d_gates = d_gates.reshape(TASKS, EXPERTS, ROWS_LOC)
        mean = jnp.sum(d_gates * gates, axis=1, keepdims=True)
        d_logits = (gates * (d_gates - mean)).reshape(16, ROWS_LOC)
        d_parts = jnp.concatenate(split3(d_logits), axis=0)
        stage[...] = dot_nn(d_parts, x)
        grad_gate = stage[0:16] + stage[16:32] + stage[32:48]
        gate_high, gate_mid, _ = split3(gate_w_ref[...])
        left = jnp.concatenate([d_parts[0:32], d_parts[0:16]], axis=0)
        right = jnp.concatenate([gate_high, gate_high, gate_mid], axis=0)
        d_in_ref[...] = dot_tn(left, right)
        small_ref[pl.ds(0, THID), :] = grad_w1[0:THID, 0:EOUT]
        small_ref[pl.ds(THID, THID), :] = grad_w1[THID : 2 * THID, EOUT : 2 * EOUT]
        for tile in range(4):
            small_ref[pl.ds(136 + 16 * tile, 16), :] = grad_gate[:, tile * 128 : tile * 128 + 128]
        small_ref[pl.ds(217, 1), :] = grad_b1
        lane = lax.broadcasted_iota(jnp.int32, (1, 128), 1)
        small_ref[pl.ds(218, 1), :] = jnp.where(lane < THID, grad_w2[0:1], grad_w2[1:2])
        small_ref[pl.ds(219, 1), :] = jnp.zeros((1, 128), F32)
        small_ref[pl.ds(240, 16 + 32), :] = jnp.zeros((48, 128), F32)
        small_ref[pl.ds(220, 2), :] = jnp.broadcast_to(
            jnp.sum(d_logit, axis=1, keepdims=True), (2, 128)
        )
        small_ref[pl.ds(222, 2), :] = jnp.zeros((2, 128), F32)
        small_ref[pl.ds(224, 16), :] = jnp.broadcast_to(
            jnp.sum(d_logits, axis=1, keepdims=True), (16, 128)
        )

    def backward(k, store):
        d_out = d_raw[k]
        grad_out = dot_tn(hidden[k], d_out)
        d_pre = (dot_nt(d_out, weights_out(k)) * slope[k]).astype(BF16)
        bias = jnp.sum(d_pre.astype(F32), axis=0, keepdims=True)
        for p in range(4):
            small_ref[pl.ds(8 * (TILES + p) + k, 1), pl.ds(0, PART)] = bias[
                :, PART * p : PART * p + PART
            ]
        grad_in = dot_tn(d_pre, x)
        for p in range(4):
            at = slice(PART * p, PART * p + PART)
            for block in range(4):
                store(p, block, grad_in[at, block * 128 : block * 128 + 128])
            store(p, 4, grad_out[at, :])
        d_in_ref[...] += dot_nn(d_pre, weights_in(k))

    def remote(source, target, sem, place):
        return pltpu.make_async_remote_copy(
            src_ref=source,
            dst_ref=target,
            send_sem=sems.at[sem],
            recv_sem=sems.at[sem + 1],
            device_id=place,
            device_id_type=pl.DeviceIdType.MESH,
        )

    def wait_all(ref, sem):
        pltpu.make_async_copy(ref, ref, sem).wait()

    def quarter(step):
        q = (step + at_y + at_x + part) % 4
        even = 1 - q % 2
        return q, even, even * part + (1 - even) * at_x, even * at_x + (1 - even) * part

    def experts(step, carry):
        q = quarter(step)[0]

        def for_pair(p, block, value):
            pair_send[q, p, pl.ds(PART * block, PART), :] = value.astype(BF16)

        def for_own(p, block, value):
            own_grad[step % 2, p, pl.ds(PART * block, PART), :] = value

        backward(2 * q + 1 - core, for_pair)
        pltpu.make_async_remote_copy(
            src_ref=pair_send.at[q],
            dst_ref=pair_recv.at[q],
            send_sem=sems.at[0],
            recv_sem=pair_sems.at[q],
            device_id=(line + 1 - 2 * core, part),
            device_id_type=pl.DeviceIdType.MESH,
        ).start()

        @pl.when(step > 0)
        def _():
            first_round(step - 1)

        backward(2 * q + core, for_own)
        return carry

    def first_round(step):
        q, even, first, _ = quarter(step)
        wait_all(pair_recv.at[0], pair_sems.at[q])
        for p in range(4):
            total = (own_grad[step % 2, p] + pair_recv[q, p].astype(F32)).astype(BF16)
            for r in range(4):
                piece = total[CHUNK * r : CHUNK * r + CHUNK]
                share_send[q, even * p + (1 - even) * r, even * r + (1 - even) * p] = piece
        for hop in range(1, 4):
            peer = (first + hop) % 4
            pltpu.make_async_remote_copy(
                src_ref=share_send.at[q, peer],
                dst_ref=first_recv.at[q, first],
                send_sem=sems.at[9],
                recv_sem=first_sems.at[q],
                device_id=(line + (1 - even) * 2 * (peer - at_x), even * peer + (1 - even) * part),
                device_id_type=pl.DeviceIdType.MESH,
            ).start()
        first_recv[q, first] = share_send[q, first]

    def second_round(step):
        q, even, _, second = quarter(step)
        three = first_recv.at[0, pl.ds(0, 3)]
        wait_all(three, first_sems.at[q])
        for at in range(4):
            total = first_recv[q, 0, at].astype(F32)
            for f in range(1, 4):
                total = total + first_recv[q, f, at].astype(F32)
            second_send[q, at] = total.astype(BF16)
        for at in range(4):
            target = 2 * (4 * q + even * at + (1 - even) * at_x) + core
            target_part = even * part + (1 - even) * at
            mine = (target == line) & (target_part == part)

            @pl.when(mine)
            def _():
                share_recv[4 * at_y + second] = second_send[q, at]

            @pl.when(jnp.logical_not(mine))
            def _():
                remote(
                    second_send.at[q, at],
                    share_recv.at[4 * at_y + second],
                    1,
                    (target, target_part),
                ).start()

    def tail():
        d_last = d_in_ref[:, pl.ds(DIN - DPROJ, DPROJ)]
        small_ref[pl.ds(200, 16), :] = jnp.zeros((16, 128), F32)
        small_ref[pl.ds(200, DENSE), pl.ds(0, DPROJ)] = dot_nn(feats_ref[...], d_last, EXACT)
        small_ref[pl.ds(216, 1), :] = jnp.zeros((1, 128), F32)
        small_ref[pl.ds(216, 1), pl.ds(0, DPROJ)] = jnp.sum(d_last, axis=0, keepdims=True)
        grad_dense_ref[...] = dot_nt(dw_ref[...], d_last, EXACT)

    def small_pair():
        return pltpu.make_async_remote_copy(
            src_ref=small_ref,
            dst_ref=small_two,
            send_sem=sems.at[5],
            recv_sem=sems.at[6],
            device_id=(line + 1 - 2 * core, part),
            device_id_type=pl.DeviceIdType.MESH,
        )

    adds_small = ((line < 30) & (part == line % 4)) | (line == 30)

    def share_small():
        small_pair().wait()
        small_two[...] = small_two[...] + small_ref[...]

        def share_tile(at, target, p):
            mine = (target == line) & (part == p)

            @pl.when(mine)
            def _():
                small_recv[chip] = small_two[pl.ds(eight(at), 8), :]

            @pl.when(jnp.logical_not(mine))
            def _():
                source = small_two.at[pl.ds(eight(at), 8), :]
                remote(source, small_recv.at[chip], 3, (target, p)).start()

        for a in range(15):
            target = 2 * a + core
            share_tile(8 * target, target, target % 4)

        @pl.when(core == 0)
        def _():
            for p in range(4):
                share_tile(8 * (TILES + p), 30, p)

    def add_up():
        @pl.when(line == TILES - 1)
        def _():
            small_all[...] = jnp.zeros_like(small_all)

        @pl.when(adds_small)
        def _():
            wait_all(small_recv.at[pl.ds(0, CHIPS - 1)], sems.at[4])

            def add_small(at, total):
                return total + small_recv[at]

            small_own[...] = lax.fori_loop(1, CHIPS, add_small, small_recv[0])

            @pl.when(line < 30)
            def _():
                for hop in range(1, 4):
                    remote(small_own, small_all, 10, (line, (part + hop) % 4)).start()

        wait_all(share_recv.at[pl.ds(0, 15)], sems.at[2])
        total = share_recv[0].astype(F32)
        for at in range(1, 16):
            total = total + share_recv[at].astype(F32)
        low = total.astype(BF16)
        for at in range(TILES):
            share_out_ref[at, pl.ds(0, CHUNK), :] = low

    def add_small_up():
        @pl.when((line < 30) & jnp.logical_not(adds_small))
        def _():
            wait_all(small_all, sems.at[11])

        @pl.when(adds_small)
        def _():
            small_all[...] = small_own[...]

        low = two_parts(small_all[...])
        for at in range(TILES):
            share_out_ref[at, pl.ds(CHUNK, 16), :] = low

    def drain():
        wait_all(pair_send, sems.at[0])
        wait_all(first_recv.at[pl.ds(0, 3)], sems.at[9])
        wait_all(share_recv.at[pl.ds(0, 15)], sems.at[1])
        for sends, zero_core in ((15, 1), (19, 0)):
            for mine in (0, 1):

                @pl.when((core == zero_core) & (adds_small == (mine == 1)))
                def _():
                    wait_all(small_recv.at[pl.ds(0, sends - mine)], sems.at[3])

        @pl.when(adds_small & (line < 30))
        def _():
            wait_all(small_recv.at[pl.ds(0, 3)], sems.at[10])

    def spread():
        lane_from = lax.broadcasted_iota(jnp.int32, (128, 128), 0)
        lane_to = lax.broadcasted_iota(jnp.int32, (128, 128), 1)
        for field in range(FIELDS):
            take = lane_from == EMB * (field % 8) + lane_to % EMB
            block = d_in_ref[:, pl.ds(field // 8 * 128, 128)].astype(BF16)
            copies = dot_nn(block, take.astype(F32).astype(BF16))
            rows[pl.ds(field * ROWS_LOC, ROWS_LOC), :] = copies
        rows[pl.ds(LOOKUPS, 8), :] = jnp.zeros((8, 128), F32)
        group = lane_group(1)
        wide_group = lane_group(CAP - COLD)

        def hot(at, carry):
            for n in range(COLD, CAP):
                row = rows[pl.ds(hot_src_ref[at * SLOTS + n], 1), :]
                hot_rows[at, pl.ds(n - COLD, 1), :] = row
            return carry

        lax.fori_loop(0, HOT, hot, 0)
        hot_rows[HOT] = jnp.zeros((CAP - COLD, 128), F32)

        def group_at(step):
            return (5 * (line // 2) + 4 * part + 8 * core + step) % 16

        def collect(step, slots):
            source = group_at(step) * (8 * SLOTS)
            for n in range(COLD):
                total = rows[pl.ds(src_ref[source + n], 1), :]
                for u in range(1, 8):
                    row = rows[pl.ds(src_ref[source + u * SLOTS + n], 1), :]
                    total = jnp.where(group == u, row, total)
                slots[pl.ds(n, 1), :] = total

        def finish(step, slots):
            first = group_at(step) * 8
            total = jnp.zeros((CAP - COLD, 128), F32)
            for u in range(8):
                total = jnp.where(wide_group == u, hot_rows[hot_at_ref[first + u]], total)
            slots[pl.ds(COLD, CAP - COLD), :] = total
            for half in range(2):
                turned = slots[pl.ds(half * 128, 128), :].T.astype(BF16)
                for u in range(8):
                    at = eight((first + u) * GROUPS + EMB * half, EMB)
                    ready[pl.ds(at, EMB), :] = turned[EMB * u : EMB * u + EMB]

        def send(step):
            first = group_at(step) * 8
            for u in range(8):
                dest = first + (me + u) % 8

                @pl.when(dest != me)
                def _():
                    send_block(ready, landing, me, dest, sems.at[7], sems.at[8])

        for slots in (even, odd):
            slots[pl.ds(CAP, SLOTS - CAP), :] = jnp.zeros((SLOTS - CAP, 128), F32)
        collect(0, even)

        def two_groups(pair, carry):
            step = 2 * pair
            collect(step + 1, odd)
            finish(step, even)
            send(step)
            collect(jnp.minimum(step + 2, 15), even)
            finish(step + 1, odd)
            send(step + 1)
            return carry

        lax.fori_loop(0, 1, two_groups, 0)
        second_round(0)
        second_round(1)
        second_round(2)
        second_round(3)
        tail()
        small_pair().start()
        lax.fori_loop(1, 2, two_groups, 0)
        share_small()
        lax.fori_loop(2, 8, two_groups, 0)
        add_up()
        add_small_up()
        wait_blocks(ready, landing, sems.at[7], sems.at[8])
        rows_out_ref[...] = landing[...]
        mine = pl.ds(eight(me * GROUPS, GROUPS), GROUPS)
        rows_out_ref[mine, :] = ready[mine, :]
        drain()

    @pl.when(phase == 0)
    def _():
        for k in range(EXPERTS):
            load_w_in(k).start()
        for load in loads:
            load.start()
        greet_all(me)
        loads[0].wait()
        lax.fori_loop(0, EXPERTS, forward, 0)

    @pl.when(phase == 1)
    def _():
        head()

    @pl.when(phase == 2)
    def _():
        pl.semaphore_wait(pltpu.get_barrier_semaphore(), OWNERS - 1)
        lax.fori_loop(0, 4, experts, 0)
        for load in loads[1:]:
            load.wait()
        first_round(3)
        spread()


def model(*operands):
    return pl.pallas_call(
        model_kernel,
        grid=(3,),
        in_specs=[VM] * 4 + [ANY] * 2 + [VM] * 7 + [SM] * 2 + [ANY] * 2,
        out_specs=[VM] * 3,
        out_shape=[
            shape((OWNERS * GROUPS, 128), BF16),
            shape((TILES, SHARE, 128), BF16),
            shape((DENSE, ROWS_LOC), F32),
        ],
        scratch_shapes=[
            pltpu.VMEM((8 * (TILES + 4), 128), F32),
            pltpu.VMEM((8 * (TILES + 4), 128), F32),
            pltpu.VMEM((ROWS_LOC, DIN), F32),
            pltpu.VMEM((EXPERTS, ROWS_LOC, HID), BF16),
            pltpu.VMEM((EXPERTS, ROWS_LOC, HID), F32),
            pltpu.VMEM((EXPERTS, ROWS_LOC, EOUT), F32),
            pltpu.VMEM((TASKS * EXPERTS, ROWS_LOC, EOUT), F32),
            pltpu.VMEM((EXPERTS, ROWS_LOC, EOUT), BF16),
            pltpu.VMEM((ROWS_LOC, TASKS * EXPERTS * EOUT), BF16),
            pltpu.VMEM((ROWS_LOC, TASKS * EOUT), F32),
            pltpu.VMEM((48, DIN), F32),
            pltpu.VMEM((2, 4, 4 * CHUNK, 128), F32),
            pltpu.VMEM((4, 4, 4 * CHUNK, 128), BF16),
            pltpu.VMEM((4, 4, 4 * CHUNK, 128), BF16),
            pltpu.VMEM((4, 4, 4, CHUNK, 128), BF16),
            pltpu.VMEM((4, 4, 4, CHUNK, 128), BF16),
            pltpu.VMEM((4, 4, CHUNK, 128), BF16),
            pltpu.VMEM((16, CHUNK, 128), BF16),
            pltpu.VMEM((CHIPS, 8, 128), F32),
            pltpu.VMEM((8, 128), F32),
            pltpu.VMEM((8, 128), F32),
            pltpu.VMEM((LOOKUPS + 8, 128), F32),
            pltpu.VMEM((HOT + 1, CAP - COLD, 128), F32),
            pltpu.VMEM((SLOTS, 128), F32),
            pltpu.VMEM((SLOTS, 128), F32),
            pltpu.VMEM((OWNERS * GROUPS, 128), BF16),
            pltpu.VMEM((OWNERS * GROUPS, 128), BF16),
            pltpu.VMEM((4, EXPERTS, PART, DIN), BF16),
            pltpu.VMEM((4, EXPERTS, PART, EOUT), BF16),
            pltpu.SMEM((OWNERS * SLOTS,), jnp.int32),
            pltpu.SMEM((2 * HOT * SLOTS,), jnp.int32),
            pltpu.SemaphoreType.DMA((EXPERTS + 3,)),
            pltpu.SemaphoreType.DMA((4,)),
            pltpu.SemaphoreType.DMA((4,)),
            pltpu.SemaphoreType.DMA((12,)),
        ],
        compiler_params=remote_params(MODEL_MIB, 1),
        name="model",
    )(*operands)


def scatter_kernel(
    asked_hbm,
    grads_hbm,
    out_hbm,
    rows_v,
    groups,
    rows,
    sem,
    even,
    odd,
    asked_ref,
    grads_ref,
    out_ref,
    out_sem,
    *sums,
):
    asked_copy = pltpu.make_async_copy(asked_hbm, asked_ref, sem.at[1])
    asked_copy.start()
    grads_copy = pltpu.make_async_copy(grads_hbm, grads_ref, sem.at[2])
    grads_copy.start()
    asked_copy.wait()
    split_wanted(asked_ref, rows_v, groups)
    rows_copy = pltpu.make_async_copy(rows_v, rows, sem.at[0])
    rows_copy.start()
    at_group = sublane_group()

    def clear(step, carry):
        for total in sums:
            total[pl.ds(eight(step * 512), 512), :] = jnp.zeros((512, 128), F32)
        return carry

    lax.fori_loop(0, PACKED // 512, clear, 0)
    grads_copy.wait()
    rows_copy.wait()

    def place(source, found):
        for half in range(2):
            block = grads_ref[pl.ds(eight(source * GROUPS + EMB * half, EMB), EMB), :].astype(F32)
            block = jnp.broadcast_to(block[None], (8, EMB, 128)).reshape(128, 128)
            block = jnp.where(at_group == groups[source, pl.ds(half, 1), :], block, 0.0)
            found[pl.ds(half * 128, 128), :] = block.T

    def add(source, found):
        for n in range(CAP):
            at = pl.ds(rows[source, n // 128, n % 128], 1)
            total = sums[n % SUMS]
            total[at, :] = total[at, :] + found[pl.ds(n, 1), :]

    place(0, even)

    def two_sources(step, carry):
        source = 2 * step
        place(source + 1, odd)
        add(source, even)
        place(jnp.minimum(source + 2, OWNERS - 1), even)
        add(source + 1, odd)
        return carry

    lax.fori_loop(0, OWNERS // 2, two_sources, 0)

    def write(field, carry):
        for part in range(4):
            at = pl.ds(eight(field * 512 + part * 128, 128), 128)
            block = sums[0][at, :]
            for total in sums[1:]:
                block = block + total[at, :]
            block = block.T
            for k in range(8):
                out_ref[field, :, pl.ds(part * 1024 + k * 128, 128)] = block[16 * k : 16 * k + 16]
        pltpu.make_async_copy(out_ref.at[field], out_hbm.at[field], out_sem).start()
        return carry

    lax.fori_loop(0, FIELDS, write, 0)
    pltpu.make_async_copy(out_ref, out_hbm, out_sem).wait()


def scatter_add(asked, grads):
    return pl.pallas_call(
        scatter_kernel,
        in_specs=[ANY, ANY],
        out_specs=ANY,
        out_shape=shape((FIELDS, EMB, ROWS_DEV), F32),
        scratch_shapes=split_scratch()
        + [pltpu.VMEM((SLOTS, 128), F32)] * 2
        + [
            pltpu.VMEM((OWNERS, 2, 128), jnp.int32),
            pltpu.VMEM((OWNERS * GROUPS, 128), BF16),
            pltpu.VMEM((FIELDS, EMB, ROWS_DEV), F32),
            pltpu.SemaphoreType.DMA,
        ]
        + [pltpu.VMEM((PACKED + 8, 128), F32)] * SUMS,
        compiler_params=params(58),
        name="scatter_add",
    )(asked, grads)


def unpack_kernel(
    shares_ref,
    w_in_ref,
    w_out_ref,
    w1_ref,
    b_out_ref,
    gate_ref,
    dense_w_ref,
    dense_b_ref,
    b1_ref,
    w2_ref,
    b2_ref,
    gate_b_ref,
    b_in_ref,
):
    def expert(k, carry):
        lines = [2 * (4 * (k // 2) + at) + k % 2 for at in range(4)]
        rows = [shares_ref[at, pl.ds(0, CHUNK), :] for at in lines]
        rows = jnp.concatenate(rows, axis=0).astype(F32)
        for block in range(4):
            w_in_ref[k, :, pl.ds(block * 128, 128)] = rows[PART * block : PART * block + PART]
        w_out_ref[k] = rows[4 * PART : 5 * PART]
        return carry

    lax.fori_loop(0, EXPERTS, expert, 0)

    def tile(at):
        return one_of(shares_ref[at, pl.ds(CHUNK, 16), :])

    for at in range(16):
        w1_ref[at // 8, pl.ds(at % 8 * 8, 8), :] = tile(at)
    b_out_ref[...] = tile(16)
    for at in range(8):
        gate_ref[pl.ds(at % 2 * 8, 8), pl.ds(at // 2 * 128, 128)] = tile(17 + at)
    dense_w_ref[pl.ds(0, 8), :] = tile(25)[:, 0:DPROJ]
    dense_w_ref[pl.ds(8, DENSE - 8), :] = tile(26)[0 : DENSE - 8, 0:DPROJ]
    rest = tile(27)
    dense_b_ref[...] = rest[0:1, 0:DPROJ]
    for t in range(TASKS):
        b1_ref[pl.ds(t, 1), :] = rest[1:2, t * THID : t * THID + THID]
        w2_ref[pl.ds(t, 1), :] = rest[2:3, t * THID : t * THID + THID]
    lane = lax.broadcasted_iota(jnp.int32, (1, 128), 1)
    b2_ref[...] = jnp.where(lane == 0, rest[4:5], rest[5:6])[:, 0:TASKS]
    own = lax.broadcasted_iota(jnp.int32, (8, 128), 0) == lax.broadcasted_iota(
        jnp.int32, (8, 128), 1
    )
    for t in range(TASKS):
        value = jnp.sum(jnp.where(own, tile(28 + t), 0.0), axis=0, keepdims=True)
        gate_b_ref[pl.ds(t, 1), :] = value[:, 0:EXPERTS]
    b_in_ref[...] = tile(30)[:, 0:PART]


def unpack(shares):
    return pl.pallas_call(
        unpack_kernel,
        in_specs=[VM],
        out_specs=[VM] * 12,
        out_shape=[
            shape((EXPERTS, PART, DIN), F32),
            shape((EXPERTS, PART, EOUT), F32),
            shape((TASKS, THID, EOUT), F32),
            shape((EXPERTS, EOUT), F32),
            shape((TASKS * EXPERTS, DIN), F32),
            shape((DENSE, DPROJ), F32),
            shape((1, DPROJ), F32),
            shape((TASKS, THID), F32),
            shape((TASKS, THID), F32),
            shape((1, TASKS), F32),
            shape((TASKS, EXPERTS), F32),
            shape((EXPERTS, PART), F32),
        ],
        compiler_params=params(32),
        name="unpack",
    )(shares)


def body(
    sparse_ids,
    dense_feats,
    labels,
    tables,
    dense_w,
    dense_b,
    w_in,
    b_in,
    w_out,
    b_out,
    gate_w,
    gate_b,
    tower_w1,
    tower_b1,
    tower_w2,
    tower_b2,
):
    w_in_all = lax.all_gather(w_in.transpose(0, 2, 1), "mp", axis=0)
    ids = sparse_ids.T
    field = lax.broadcasted_iota(jnp.int32, (FIELDS, ROWS_LOC), 0)
    example = lax.broadcasted_iota(jnp.int32, (FIELDS, ROWS_LOC), 1)
    row = ids & (ROWS_DEV - 1)
    packed = field * 512 + (row >> 10) * 128 + (row & 127)
    key = ((ids >> 12) << 14) | (field * ROWS_LOC + example)
    load = (packed << 3) | ((row >> 7) & 7)
    keys, loads = lax.sort((key.reshape(-1), load.reshape(-1)), num_keys=1, is_stable=False)
    requests, sources, hot_sources, hot, hot_at = route(keys.reshape(-1, 128), loads.reshape(-1, 128))
    sources = sources.reshape(-1)
    answer, asked, w_out_all, b_in_all = look_up(
        requests, tables.transpose(0, 2, 1), w_out, b_in
    )
    feats_t = dense_feats.T
    inputs = embed(sources, hot, ids, answer, feats_t, dense_w, dense_b.reshape(1, DPROJ))
    incoming, share, grad_dense = model(
        inputs,
        labels.T,
        feats_t,
        dense_w,
        w_in_all,
        w_out_all,
        b_in_all,
        b_out,
        gate_w.transpose(0, 2, 1).reshape(TASKS * EXPERTS, DIN),
        gate_b,
        tower_w1.transpose(0, 2, 1),
        tower_b1,
        tower_w2,
        tower_b2,
        hot_at,
        sources,
        hot_sources.reshape(-1),
    )
    shares = lax.all_to_all(share, "dp", split_axis=0, concat_axis=0, tiled=True)
    grad_tables = scatter_add(asked, incoming).transpose(0, 2, 1)
    (
        grad_w_in,
        grad_w_out,
        grad_w1,
        grad_b_out,
        grad_gate_w,
        grad_dense_w,
        grad_dense_b,
        grad_b1,
        grad_w2,
        grad_b2,
        grad_gate_b,
        grad_b_in,
    ) = unpack(shares)
    return (
        grad_tables,
        grad_dense_w,
        grad_dense_b.reshape(DPROJ),
        grad_w_in.transpose(0, 2, 1),
        grad_b_in,
        grad_w_out,
        grad_b_out,
        grad_gate_w.reshape(TASKS, EXPERTS, DIN).transpose(0, 2, 1),
        grad_gate_b,
        grad_w1.transpose(0, 2, 1),
        grad_b1,
        grad_w2,
        grad_b2.reshape(TASKS),
        grad_dense.T,
    )


def solution(mesh):
    return jax.shard_map(
        body,
        mesh=mesh,
        in_specs=(
            P(ALL, None),
            P(ALL, None),
            P(ALL, None),
            P(None, ALL, None),
            P(),
            P(),
            P(None, None, "mp"),
            P(None, "mp"),
            P(None, "mp", None),
            P(),
            P(),
            P(),
            P(),
            P(),
            P(),
            P(),
        ),
        out_specs=(
            P(None, ALL, None),
            P(),
            P(),
            P(None, None, "mp"),
            P(None, "mp"),
            P(None, "mp", None),
            P(),
            P(),
            P(),
            P(),
            P(),
            P(),
            P(),
            P(ALL, None),
        ),
        check_vma=False,
    )
```
